32 devices in a mesh: occi: 4 (over y, x), occj: 2 (over core), virt: 4 (over z).
Axes of the slice: x: 2, y: 2, z: 4, core: 2. Of those that a mesh axis runs over, the one named last changes fastest.
Arguments:
- amplitudes: bfloat16 [8, 8, 128, 128], P('occi', 'occj'), may hold values from -6 to 6
- vectors: bfloat16 [32, 128, 128], P('virt'), may hold values from -0.15625 to 0.15625
- tile_mask: int32 [8, 8, 2, 2], P('occi', 'occj'), may hold values 0 or 1
- pair_mask: int32 [8, 8], P('occi', 'occj'), may hold values 0 or 1
Outputs:
- ladder: bfloat16 [8, 8, 128, 128], P('occi', 'occj', 'virt')
The draws below stay inside these ranges and needn't reach their ends.
All inputs are finite; a program needn't handle non-finite values. No bound on the sum of `tile_mask` or of `pair_mask` on one device may be relied on, other than what follows from the above.
Results may differ from the reference program's by a relative error of at most 0.0059.
Values may be sent and summed in bfloat16 or wider, within the bound.
No kernel may reach another device: no remote copies, remote signals or barrier semaphores. Data moves between devices by JAX's collectives and lax.ppermute only.
A program may use at most 64 MiB of HBM per device.

```python
import jax
import jax.numpy as jnp
from jax import lax

TILE = 64
SLAB_TILES = 2
S = 128
NOCC = 8
NQ = 32
N_OCCI = 4
N_OCCJ = 2


def place_ends(entries, rng, smallest, high):
    longest = entries.shape.index(max(entries.shape))
    spots = []
    for shift in (0, 1):
        where = [jax.random.randint(jax.random.fold_in(rng, axis), (), 0, length) for axis, length in enumerate(entries.shape)]
        where[longest] = (where[longest] + shift) % entries.shape[longest]
        spots.append(tuple(where))
    return entries.at[spots[0]].set(smallest).at[spots[1]].set(high)


def levels(stream_key, shape, split, smallest, largest):
    gain, own = 1.0, jax.random.fold_in(stream_key, 6)
    for position, shards_of in split:
        heights = jnp.exp(jax.random.uniform(jax.random.fold_in(own, position), (shards_of,), jnp.float32, smallest / len(split), largest / len(split)))
        gain = gain * jnp.repeat(heights, shape[position] // shards_of).reshape([-1 if axis == position else 1 for axis in range(len(shape))])
    return gain


def normal_values(key, extent, spread, limit, cuts=(), kind=jnp.bfloat16):
    loudness = levels(key, extent, cuts, -0.22, 0.18) if cuts else 1.0
    drawn = jax.random.normal(key, extent, jnp.float32) * spread * loudness
    return jnp.minimum(jnp.maximum(drawn, -limit), limit).astype(kind)


def setup_inputs(seed: int = 0) -> dict:
    streams_of = jax.random.split(jax.random.key(seed), 5)
    return {
        "amplitudes": normal_values(streams_of[0], (NOCC, NOCC, S, S), 1.0, 6.0, ((0, 4), (1, 2))),
        "vectors": normal_values(streams_of[1], (NQ, S, S), (S * 12) ** -0.5, 0.15625, ((0, 4),)),
        "tile_mask": place_ends((jax.random.randint(streams_of[2], (NOCC, NOCC, SLAB_TILES, SLAB_TILES), 0, 4) < 3).astype(jnp.int32), jax.random.fold_in(streams_of[2], 1), 0, 1),
        "pair_mask": place_ends((jax.random.randint(streams_of[3], (NOCC, NOCC), 0, 4) < 3).astype(jnp.int32), jax.random.fold_in(streams_of[3], 1), 0, 1),
    }


def masked_tiles(amplitudes, tile_mask):
    first, second = amplitudes.shape[0], amplitudes.shape[1]
    tiled = amplitudes.reshape(first, second, SLAB_TILES, TILE, SLAB_TILES, TILE)
    keep_tiles = tile_mask.astype(jnp.bfloat16)[:, :, :, None, :, None]
    return (tiled * keep_tiles).reshape(amplitudes.shape)


def reference(amplitudes, vectors, tile_mask, pair_mask):
    kept = masked_tiles(amplitudes, tile_mask)
    kept_wide = kept.astype(jnp.float32)

    def advance(running, vector):
        vector_wide = vector.astype(jnp.float32)
        contracted = jnp.einsum("ac,ipcd->ipad", vector_wide, kept_wide).astype(jnp.bfloat16)
        return running + jnp.einsum("ipad,bd->ipab", contracted.astype(jnp.float32), vector_wide), None

    initial = jnp.zeros(kept.shape, jnp.float32)
    total, _ = lax.scan(advance, initial, vectors)
    half = total.astype(jnp.bfloat16)
    slots = jnp.arange(N_OCCI * N_OCCJ, dtype=jnp.int32)
    occ_of_slot = ((slots % N_OCCI) * N_OCCJ + slots // N_OCCI).astype(jnp.int32)
    slot_of_occ = ((slots % N_OCCJ) * N_OCCI + slots // N_OCCJ).astype(jnp.int32)
    partner = half[occ_of_slot[None, :], slot_of_occ[:, None]]
    summed = half.astype(jnp.float32) + jnp.swapaxes(partner, 2, 3).astype(jnp.float32)
    return (pair_mask.astype(jnp.float32)[:, :, None, None] * summed).astype(jnp.bfloat16)
```

```python
import functools

import jax
import jax.numpy as jnp
from jax import lax
from jax.experimental import pallas as pl
from jax.experimental.pallas import tpu as pltpu
from jax.sharding import PartitionSpec as P

TILE = 64
SLAB_TILES = 2
PAIR_GROUP = 8


def mask_kernel(mask_ref, amp_ref, kept_ref):
    firsts, seconds, slab, _ = amp_ref.shape
    row = lax.broadcasted_iota(jnp.int32, (slab, slab), 0) // TILE
    col = lax.broadcasted_iota(jnp.int32, (slab, slab), 1) // TILE
    tile = row * SLAB_TILES + col

    def one(block, _):
        first, second = block // seconds, block % seconds
        keep = jnp.zeros((slab, slab), jnp.float32)
        for t in range(SLAB_TILES * SLAB_TILES):
            keep = jnp.where(tile == t, mask_ref[block, t].astype(jnp.float32), keep)
        wide = amp_ref[first, second].astype(jnp.float32) * keep
        kept_ref[block] = wide.astype(kept_ref.dtype)
        return 0

    lax.fori_loop(0, firsts * seconds, one, 0, unroll=firsts * seconds <= 8)


def ladder_kernel(kept_ref, partner_ref, vec_ref, half_ref):
    pairs, slab, _ = kept_ref.shape
    vectors = vec_ref.shape[0]
    chunks, _, rows, _ = half_ref.shape
    flat = vec_ref[...].reshape(vectors * slab, slab)
    turned = jnp.concatenate(
        [vec_ref[q].astype(jnp.float32).T.astype(jnp.bfloat16) for q in range(vectors)], axis=0
    )

    def step(base):
        for j in range(0, min(PAIR_GROUP, pairs), 2):
            both = []
            for k in (j, j + 1):
                wide = kept_ref[base + k].astype(jnp.float32) + partner_ref[base + k].astype(jnp.float32).T
                both.append(wide.astype(jnp.bfloat16))
            inner = jnp.dot(flat, jnp.concatenate(both, axis=1), preferred_element_type=jnp.float32)
            inner = inner.astype(jnp.bfloat16).reshape(vectors, slab, 2 * slab)
            stacked = jnp.concatenate(
                [
                    jnp.concatenate([inner[q, :, n * slab : (n + 1) * slab] for q in range(vectors)], axis=1)
                    for n in range(2)
                ],
                axis=0,
            )
            half = jnp.dot(stacked, turned, preferred_element_type=jnp.float32)
            for n, k in enumerate((j, j + 1)):
                for chunk in range(chunks):
                    start = n * slab + chunk * rows
                    half_ref[chunk, base + k] = half[start : start + rows].astype(half_ref.dtype)

    if pairs <= PAIR_GROUP:
        step(0)
    else:
        lax.fori_loop(0, pairs // PAIR_GROUP, lambda g, c: (step(g * PAIR_GROUP), c)[1], 0)


def vmem_specs(count):
    return [pl.BlockSpec(memory_space=pltpu.VMEM)] * count


def shards(amplitudes, vectors, tile_mask, pair_mask):
    firsts, seconds, slab, _ = amplitudes.shape
    pairs = firsts * seconds
    virt = lax.axis_size("virt")
    rows = slab // virt
    params = pltpu.CompilerParams(vmem_limit_bytes=24 * 1024 * 1024)
    kept = pl.pallas_call(
        mask_kernel,
        out_shape=jax.ShapeDtypeStruct((pairs, slab, slab), jnp.bfloat16),
        in_specs=[pl.BlockSpec(memory_space=pltpu.SMEM)] + vmem_specs(1),
        out_specs=vmem_specs(1)[0],
        compiler_params=params,
    )(tile_mask.reshape(pairs, SLAB_TILES * SLAB_TILES), amplitudes)
    partner = lax.all_to_all(kept, ("occj", "occi"), split_axis=0, concat_axis=0, tiled=True)
    half = pl.pallas_call(
        ladder_kernel,
        out_shape=jax.ShapeDtypeStruct((virt, pairs, rows, slab), jnp.bfloat16),
        in_specs=vmem_specs(3),
        out_specs=vmem_specs(1)[0],
        compiler_params=params,
    )(kept, partner, vectors)
    terms = lax.all_to_all(half, "virt", split_axis=0, concat_axis=0, tiled=True)
    summed = jnp.sum(terms.astype(jnp.float32), axis=0).reshape(firsts, seconds, rows, slab)
    return (pair_mask.astype(jnp.float32)[:, :, None, None] * summed).astype(jnp.bfloat16)


def solution(mesh):
    placed = (
        P("occi", "occj", None, None),
        P("virt", None, None),
        P("occi", "occj", None, None),
        P("occi", "occj"),
    )
    return jax.shard_map(
        shards,
        mesh=mesh,
        in_specs=placed,
        out_specs=P("occi", "occj", "virt", None),
        check_vma=False,
    )
```

```python
import functools

import jax
import jax.numpy as jnp
from jax import lax
from jax.experimental import pallas as pl
from jax.experimental.pallas import tpu as pltpu
from jax.sharding import PartitionSpec as P

TILE = 64
SLAB_TILES = 2
PAIR_GROUP = 8
PLANE = ("occj", "occi")


def plane_index():
    return lax.axis_index("occj") * lax.axis_size("occi") + lax.axis_index("occi")


def mask_kernel(mask_ref, amp_ref, *kept_refs):
    _, seconds, slab, _ = amp_ref.shape
    row = lax.broadcasted_iota(jnp.int32, (slab, slab), 0) // TILE
    col = lax.broadcasted_iota(jnp.int32, (slab, slab), 1) // TILE

    def masked(block):
        first, second = block // seconds, block % seconds
        keep = jnp.zeros((slab, slab), jnp.float32)
        for r in range(SLAB_TILES):
            for c in range(SLAB_TILES):
                here = mask_ref[first, r, c, second].astype(jnp.float32)
                keep = jnp.where((row == r) & (col == c), here, keep)
        return (amp_ref[first, second].astype(jnp.float32) * keep).astype(jnp.bfloat16)

    if len(kept_refs) == 1:

        def one(block, carry):
            kept_refs[0][block] = masked(block)
            return carry

        lax.fori_loop(0, kept_refs[0].shape[0], one, 0)
    else:
        mine = plane_index()
        for step, kept_ref in enumerate(kept_refs):
            kept_ref[...] = masked(mine ^ step)


def ladder_kernel(steps, chunks, *refs):
    vec_ref, half_refs, refs = refs[0], refs[-chunks:], refs[1:-chunks]
    kept_refs, partner_refs = refs[:steps], refs[steps:]
    vectors, slab, _ = vec_ref.shape
    pairs, rows, _ = half_refs[0].shape
    me = lax.axis_index("virt")
    flat = jnp.concatenate(
        [
            vec_ref[q, pl.ds(pl.multiple_of((me ^ chunk) * rows, rows), rows), :]
            for q in range(vectors)
            for chunk in range(chunks)
        ],
        axis=0,
    )
    turned = jnp.concatenate(
        [vec_ref[q].astype(jnp.float32).T.astype(jnp.bfloat16) for q in range(vectors)], axis=0
    )

    def work(blocks):
        both = [
            (kept.astype(jnp.float32) + partner.astype(jnp.float32).T).astype(jnp.bfloat16)
            for _, kept, partner in blocks
        ]
        inner = jnp.dot(flat, jnp.concatenate(both, axis=1), preferred_element_type=jnp.float32)
        inner = inner.astype(jnp.bfloat16).reshape(vectors, slab, len(blocks) * slab)
        stacked = jnp.concatenate(
            [
                jnp.concatenate([inner[q, :, n * slab : (n + 1) * slab] for q in range(vectors)], axis=1)
                for n in range(len(blocks))
            ],
            axis=0,
        )
        half = jnp.dot(stacked, turned, preferred_element_type=jnp.float32)
        for n, (pair, _, _) in enumerate(blocks):
            for chunk in range(chunks):
                start = n * slab + chunk * rows
                half_refs[chunk][pair] = half[start : start + rows].astype(jnp.bfloat16)

    if steps == 1:

        def two(g, carry):
            work([(2 * g + n, kept_refs[0][2 * g + n], partner_refs[0][2 * g + n]) for n in range(2)])
            return carry

        lax.fori_loop(0, pairs // 2, two, 0)
    else:
        mine = plane_index()
        for step in range(0, steps, 2):
            blocks = []
            for s in (step, step + 1):
                partner_ref = partner_refs[s - 1] if s else kept_refs[0]
                blocks.append((mine ^ s, kept_refs[s][...], partner_ref[...]))
            work(blocks)


def vmem_specs(count):
    return [pl.BlockSpec(memory_space=pltpu.VMEM)] * count


def swap_virt(array, step):
    return lax.ppermute(array, "virt", [(d, d ^ step) for d in range(lax.axis_size("virt"))])


def swap_plane(array, step):
    size, across = lax.axis_size("occi"), lax.axis_size("occj")
    turn_j, turn_i = step // size, step % size
    moves = [(i * across + j, (i ^ turn_i) * across + (j ^ turn_j)) for i in range(size) for j in range(across)]
    return lax.ppermute(array, ("occi", "occj"), moves)


def shards(amplitudes, vectors, tile_mask, pair_mask):
    firsts, seconds, slab, _ = amplitudes.shape
    pairs = firsts * seconds
    virt = lax.axis_size("virt")
    rows = slab // virt
    plane = lax.axis_size("occi") * lax.axis_size("occj")
    params = pltpu.CompilerParams(vmem_limit_bytes=24 * 1024 * 1024)
    steps = plane if plane == pairs and plane <= PAIR_GROUP else 1
    block_shape = (slab, slab) if steps > 1 else (pairs, slab, slab)
    kept = pl.pallas_call(
        mask_kernel,
        out_shape=[jax.ShapeDtypeStruct(block_shape, jnp.bfloat16)] * steps,
        in_specs=[pl.BlockSpec(memory_space=pltpu.SMEM)] + vmem_specs(1),
        out_specs=vmem_specs(steps),
        compiler_params=params,
    )(jnp.transpose(tile_mask, (0, 2, 3, 1)), amplitudes)
    if steps > 1:
        partner = [swap_plane(kept[step], step) for step in range(1, steps)]
    else:
        partner = [lax.all_to_all(kept[0], PLANE, split_axis=0, concat_axis=0, tiled=True)]
    half = pl.pallas_call(
        functools.partial(ladder_kernel, steps, virt),
        out_shape=[jax.ShapeDtypeStruct((pairs, rows, slab), jnp.bfloat16)] * virt,
        in_specs=vmem_specs(1 + len(kept) + len(partner)),
        out_specs=vmem_specs(virt),
        compiler_params=params,
    )(vectors, *kept, *partner)
    summed = half[0].astype(jnp.float32)
    for step in range(1, virt):
        summed = summed + swap_virt(half[step], step).astype(jnp.float32)
    summed = summed.reshape(firsts, seconds, rows, slab)
    return (pair_mask.astype(jnp.float32)[:, :, None, None] * summed).astype(jnp.bfloat16)


def solution(mesh):
    placed = (
        P("occi", "occj", None, None),
        P("virt", None, None),
        P("occi", "occj", None, None),
        P("occi", "occj"),
    )
    return jax.shard_map(
        shards,
        mesh=mesh,
        in_specs=placed,
        out_specs=P("occi", "occj", "virt", None),
        check_vma=False,
    )
```

```python
import functools

import jax
import jax.numpy as jnp
from jax import lax
from jax.experimental import pallas as pl
from jax.experimental.pallas import tpu as pltpu
from jax.sharding import PartitionSpec as P

TILE = 64
SLAB_TILES = 2
CHIPS = 4
BF16 = jnp.bfloat16
F32 = jnp.float32


def swap_virt(array, step):
    return lax.ppermute(array, "virt", [(d, d ^ step) for d in range(lax.axis_size("virt"))])


def swap_core(array):
    return lax.ppermute(array, "occj", [(0, 1), (1, 0)])


def swap_chip(array, step):
    return lax.ppermute(array, "occi", [(d, d ^ step) for d in range(lax.axis_size("occi"))])


def slot(kind, step):
    first = lax.axis_index("occj") if kind == 0 else 1 - lax.axis_index("occj")
    return first, lax.axis_index("occi") ^ step


def masked(mask_ref, amp_ref, first, second):
    slab = amp_ref.shape[-1]
    row = lax.broadcasted_iota(jnp.int32, (slab, slab), 0) // TILE
    col = lax.broadcasted_iota(jnp.int32, (slab, slab), 1) // TILE
    keep = jnp.zeros((slab, slab), F32)
    for r in range(SLAB_TILES):
        for c in range(SLAB_TILES):
            keep = jnp.where((row == r) & (col == c), mask_ref[first, r, c, second].astype(F32), keep)
    return (amp_ref[first, second].astype(F32) * keep).astype(BF16)


def mask_split_kernel(mask_ref, pair_ref, amp_ref, same_ref, cross_ref, gate_ref):
    for kind, kept_ref in ((1, cross_ref), (0, same_ref)):
        for step in range(CHIPS):
            first, second = slot(kind, step)
            kept_ref[step] = masked(mask_ref, amp_ref, first, second)
            gate_ref[kind * CHIPS + step] = jnp.full(gate_ref.shape[1:], pair_ref[first, second].astype(F32))


def mask_whole_kernel(mask_ref, pair_ref, amp_ref, kept_ref, gate_ref):
    seconds = amp_ref.shape[1]

    def one(block, carry):
        first, second = block // seconds, block % seconds
        kept_ref[block] = masked(mask_ref, amp_ref, first, second)
        gate_ref[block] = jnp.full(gate_ref.shape[1:], pair_ref[first, second].astype(F32))
        return carry

    lax.fori_loop(0, kept_ref.shape[0], one, 0)


def pack_kernel(same_ref, other_ref, *send_refs):
    for step, send_ref in enumerate(send_refs, 1):
        send_ref[0] = same_ref[step]
        send_ref[1] = other_ref[step]


def turn(vec_refs, turned_ref):
    slab = vec_refs[0].shape[-1]
    at = 0
    for vec_ref in vec_refs:
        for q in range(vec_ref.shape[0]):
            turned_ref[at : at + slab] = vec_ref[q].astype(F32).T.astype(BF16)
            at += slab


def left_rows(vec_refs, rows, chunks):
    me = lax.axis_index("virt")
    return jnp.concatenate(
        [
            vec_ref[q, pl.ds(pl.multiple_of((me ^ (2 * chunk)) * rows, rows), rows), :]
            for vec_ref in vec_refs
            for q in range(vec_ref.shape[0])
            for chunk in range(chunks)
        ],
        axis=0,
    )


def products(flat, turned_ref, inner_ref, sources, outs):
    slab = turned_ref.shape[1]
    vectors = turned_ref.shape[0] // slab
    height = flat.shape[0] // vectors
    rows = height // len(outs[0])
    for base in range(0, len(sources), 2):
        both = [
            ((kept.astype(F32) + partner.astype(F32).T) * gate[:1]).astype(BF16)
            for kept, partner, gate in sources[base : base + 2]
        ]
        inner = jnp.dot(flat, jnp.concatenate(both, axis=1), preferred_element_type=F32).astype(BF16)
        for n in range(len(both)):
            for q in range(vectors):
                inner_ref[(base + n) * height : (base + n + 1) * height, q * slab : (q + 1) * slab] = inner[
                    q * height : (q + 1) * height, n * slab : (n + 1) * slab
                ]
    half = jnp.dot(inner_ref[...], turned_ref[...], preferred_element_type=F32)
    for n, targets in enumerate(outs):
        for chunk, (ref, index) in enumerate(targets):
            start = n * height + chunk * rows
            ref[index] = half[start : start + rows].astype(ref.dtype)


def early_kernel(chunks, own_ref, near_ref, gate_ref, same_ref, cross_ref, other_ref, *refs):
    got_refs, refs = refs[: CHIPS - 2], refs[CHIPS - 2 :]
    part_refs, turned_ref, inner_ref = refs[:chunks], refs[chunks], refs[chunks + 1]
    turn((own_ref, near_ref), turned_ref)
    flat = left_rows((own_ref, near_ref), part_refs[0].shape[1], chunks)
    sources = [
        (same_ref[0], same_ref[0], gate_ref[0]),
        (cross_ref[0], other_ref[0], gate_ref[CHIPS]),
    ]
    for step, got_ref in enumerate(got_refs, 1):
        sources.append((same_ref[step], got_ref[0], gate_ref[step]))
        sources.append((cross_ref[step], got_ref[1], gate_ref[CHIPS + step]))
    outs = [[(ref, n) for ref in part_refs] for n in range(len(sources))]
    products(flat, turned_ref, inner_ref, sources, outs)


def late_kernel(chunks, own_ref, near_ref, gate_ref, same_ref, cross_ref, turned_ref, got_ref, *refs):
    part_refs, inner_ref = refs[:chunks], refs[chunks]
    flat = left_rows((own_ref, near_ref), part_refs[0].shape[1], chunks)
    step = CHIPS - 1
    sources = [
        (same_ref[step], got_ref[0], gate_ref[step]),
        (cross_ref[step], got_ref[1], gate_ref[CHIPS + step]),
    ]
    outs = [[(ref, n) for ref in part_refs] for n in range(len(sources))]
    products(flat, turned_ref, inner_ref, sources, outs)


def whole_kernel(chunks, own_ref, near_ref, gate_ref, kept_ref, partner_ref, *refs):
    part_refs, turned_ref, inner_ref = refs[:chunks], refs[chunks], refs[chunks + 1]
    turn((own_ref, near_ref), turned_ref)

    def two(g, carry):
        flat = left_rows((own_ref, near_ref), part_refs[0].shape[1], chunks)
        pairs = [2 * g, 2 * g + 1]
        sources = [(kept_ref[k], partner_ref[k], gate_ref[k]) for k in pairs]
        products(flat, turned_ref, inner_ref, sources, [[(ref, k) for ref in part_refs] for k in pairs])
        return carry

    lax.fori_loop(0, kept_ref.shape[0] // 2, two, 0)


def finish_kernel(counts, chunks, *refs):
    out_ref = refs[-1]
    at = 0
    for group, count in enumerate(counts):
        terms = refs[group * chunks : (group + 1) * chunks]
        for n in range(count):
            total = terms[0][n]
            for term in terms[1:]:
                total = total + term[n].astype(F32)
            first, second = slot((at + n) % 2, (at + n) // 2)
            out_ref[first, second] = total.astype(BF16)
        at += count


def vmem_specs(count):
    return [pl.BlockSpec(memory_space=pltpu.VMEM)] * count


def shaped(dtype, *shape):
    return jax.ShapeDtypeStruct(shape, dtype)


def kernel(body, outs, operands, scalars=0, scratch=()):
    return pl.pallas_call(
        body,
        out_shape=outs,
        in_specs=[pl.BlockSpec(memory_space=pltpu.SMEM)] * scalars + vmem_specs(len(operands) - scalars),
        out_specs=vmem_specs(len(outs)),
        scratch_shapes=list(scratch),
        compiler_params=pltpu.CompilerParams(vmem_limit_bytes=24 * 1024 * 1024),
    )(*operands)


def shards(amplitudes, vectors, tile_mask, pair_mask):
    firsts, seconds, slab, _ = amplitudes.shape
    pairs = firsts * seconds
    virt, chips, cores = lax.axis_size("virt"), lax.axis_size("occi"), lax.axis_size("occj")
    rows = slab // virt
    chunks = virt // 2
    depth = 2 * vectors.shape[0] * slab
    masks = (jnp.transpose(tile_mask, (0, 2, 3, 1)), pair_mask, amplitudes)
    gate = shaped(F32, pairs, 8, slab)

    def parts(count):
        return [shaped(F32 if chunk == 0 else BF16, count, rows, slab) for chunk in range(chunks)]

    def inner(count):
        return pltpu.VMEM((count * chunks * rows, depth), BF16)

    def sent(part):
        return [part[0]] + [swap_virt(part[chunk], 2 * chunk) for chunk in range(1, chunks)]

    near = swap_virt(vectors, 1)
    turned = shaped(BF16, depth, slab)
    if (firsts, seconds, chips, cores) == (2, CHIPS, CHIPS, 2):
        half_blocks = shaped(BF16, CHIPS, slab, slab)
        same, cross, gates = kernel(mask_split_kernel, [half_blocks, half_blocks, gate], masks, 2)
        other = swap_core(cross)
        packed = kernel(pack_kernel, [shaped(BF16, 2, slab, slab)] * (CHIPS - 1), (same, other))
        got = [swap_chip(block, step) for step, block in enumerate(packed, 1)]
        count = 2 * (CHIPS - 1)
        *early, turned = kernel(
            functools.partial(early_kernel, chunks),
            parts(count) + [turned],
            (vectors, near, gates, same, cross, other, *got[:-1]),
            scratch=[inner(count)],
        )
        early = sent(early)
        late = kernel(
            functools.partial(late_kernel, chunks),
            parts(2),
            (vectors, near, gates, same, cross, turned, got[-1]),
            scratch=[inner(2)],
        )
        late = sent(late)
        (out,) = kernel(
            functools.partial(finish_kernel, (count, 2), chunks),
            [shaped(BF16, firsts, seconds, rows, slab)],
            (*early, *late),
        )
        return out
    kept, gates = kernel(mask_whole_kernel, [shaped(BF16, pairs, slab, slab), gate], masks, 2)
    partner = lax.all_to_all(kept, ("occj", "occi"), split_axis=0, concat_axis=0, tiled=True)
    *part, _ = kernel(
        functools.partial(whole_kernel, chunks),
        parts(pairs) + [turned],
        (vectors, near, gates, kept, partner),
        scratch=[inner(2)],
    )
    part = sent(part)
    summed = part[0]
    for term in part[1:]:
        summed = summed + term.astype(F32)
    return summed.reshape(firsts, seconds, rows, slab).astype(BF16)


def solution(mesh):
    placed = (
        P("occi", "occj", None, None),
        P("virt", None, None),
        P("occi", "occj", None, None),
        P("occi", "occj"),
    )
    return jax.shard_map(
        shards,
        mesh=mesh,
        in_specs=placed,
        out_specs=P("occi", "occj", "virt", None),
        check_vma=False,
    )
```

```python
import functools

import jax
import jax.numpy as jnp
from jax import lax
from jax.experimental import pallas as pl
from jax.experimental.pallas import tpu as pltpu
from jax.sharding import PartitionSpec as P

TILE = 64
SLAB_TILES = 2
CHIPS = 4
STEPS = (3, 1, 2)
GROUPS = ((0, 3), (1, 2))
BF16 = jnp.bfloat16
F32 = jnp.float32


def swap_virt(array, step):
    return lax.ppermute(array, "virt", [(d, d ^ step) for d in range(lax.axis_size("virt"))])


def swap_core(array):
    return lax.ppermute(array, "occj", [(0, 1), (1, 0)])


def swap_chip(array, step):
    return lax.ppermute(array, "occi", [(d, d ^ step) for d in range(lax.axis_size("occi"))])


def slot(kind, step):
    first = lax.axis_index("occj") if kind == 0 else 1 - lax.axis_index("occj")
    return first, lax.axis_index("occi") ^ step


def keep_rows(mask_ref, first, second, half):
    lane = lax.broadcasted_iota(jnp.int32, (1, SLAB_TILES * TILE), 1) // TILE
    keep = jnp.zeros(lane.shape, F32)
    for tile in range(SLAB_TILES):
        keep = jnp.where(lane == tile, mask_ref[first, half, tile, second].astype(F32), keep)
    return jnp.broadcast_to(keep, (TILE, SLAB_TILES * TILE)).astype(BF16)


def mask_split_kernel(mask_hbm, pair_hbm, amp_hbm, same_ref, cross_ref, gate_ref, mask_ref, pair_ref, sems):
    copies = [
        pltpu.make_async_copy(mask_hbm, mask_ref, sems.at[0]),
        pltpu.make_async_copy(pair_hbm, pair_ref, sems.at[1]),
    ]
    blocks = []
    for kind, kept_ref in ((1, cross_ref), (0, same_ref)):
        for step in range(CHIPS):
            first, second = slot(kind, step)
            copies.append(
                pltpu.make_async_copy(amp_hbm.at[first, second], kept_ref.at[step], sems.at[len(copies)])
            )
            blocks.append((first, second, kept_ref, step, kind * CHIPS + step, copies[-1]))
    for copy in copies:
        copy.start()
    copies[0].wait()
    copies[1].wait()
    for first, second, kept_ref, step, gate, copy in blocks:
        gate_ref[gate] = jnp.full(gate_ref.shape[1:], pair_ref[first, second].astype(F32))
        keeps = [keep_rows(mask_ref, first, second, half) for half in range(SLAB_TILES)]
        copy.wait()
        for half, keep in enumerate(keeps):
            part = slice(half * TILE, (half + 1) * TILE)
            kept_ref[step, part] = kept_ref[step, part] * keep


def mask_whole_kernel(mask_ref, pair_ref, amp_ref, kept_ref, gate_ref):
    seconds = amp_ref.shape[1]

    def one(block, carry):
        first, second = block // seconds, block % seconds
        for half in range(SLAB_TILES):
            part = slice(half * TILE, (half + 1) * TILE)
            kept_ref[block, part] = amp_ref[first, second, part] * keep_rows(mask_ref, first, second, half)
        gate_ref[block] = jnp.full(gate_ref.shape[1:], pair_ref[first, second].astype(F32))
        return carry

    lax.fori_loop(0, kept_ref.shape[0], one, 0)


def pack_kernel(same_ref, other_ref, *send_refs):
    for step, send_ref in zip(STEPS, send_refs):
        send_ref[0] = same_ref[step]
        send_ref[1] = other_ref[step]


def turn_kernel(chunks, vec_ref, turned_ref, left_ref):
    vectors, slab, _ = vec_ref.shape
    rows = left_ref.shape[0] // (vectors * chunks)
    me = lax.axis_index("virt")
    for q in range(vectors):
        turned_ref[q * slab : (q + 1) * slab] = vec_ref[q].astype(F32).T.astype(BF16)
        for chunk in range(chunks):
            start = pl.multiple_of((me ^ (2 * chunk)) * rows, rows)
            low = (q * chunks + chunk) * rows
            left_ref[low : low + rows] = vec_ref[q, pl.ds(start, rows), :]


def products(ready, inner_ref, sources, outs):
    turned_refs, left_refs = ready[::2], ready[1::2]
    slab = turned_refs[0].shape[1]
    depth = turned_refs[0].shape[0]
    vectors = depth // slab
    height = left_refs[0].shape[0] // vectors
    rows = height // len(outs[0])
    for base in range(0, len(sources), 2):
        both = [
            ((kept.astype(F32) + partner.astype(F32).T) * gate[:1]).astype(BF16)
            for kept, partner, gate in sources[base : base + 2]
        ]
        right = jnp.concatenate(both, axis=1)
        for side, left_ref in enumerate(left_refs):
            inner = jnp.dot(left_ref[...], right, preferred_element_type=F32).astype(BF16)
            for n in range(len(both)):
                for q in range(vectors):
                    at = side * depth + q * slab
                    inner_ref[(base + n) * height : (base + n + 1) * height, at : at + slab] = inner[
                        q * height : (q + 1) * height, n * slab : (n + 1) * slab
                    ]
    half = sum(
        jnp.dot(inner_ref[:, side * depth : (side + 1) * depth], turned_ref[...], preferred_element_type=F32)
        for side, turned_ref in enumerate(turned_refs)
    )
    for n, targets in enumerate(outs):
        for chunk, (ref, index) in enumerate(targets):
            start = n * height + chunk * rows
            ref[index] = half[start : start + rows].astype(ref.dtype)


def group_kernel(chunks, steps, *refs):
    ready, (gate_ref, same_ref, cross_ref), refs = refs[:4], refs[4:7], refs[7:]
    got_refs, part_refs, inner_ref = refs[: len(steps)], refs[len(steps) : -1], refs[-1]
    sources = []
    for step, got_ref in zip(steps, got_refs):
        if step:
            partners = got_ref[0], got_ref[1]
        else:
            partners = same_ref[0], got_ref[0]
        sources.append((same_ref[step], partners[0], gate_ref[step]))
        sources.append((cross_ref[step], partners[1], gate_ref[CHIPS + step]))
    outs = [[(ref, n) for ref in part_refs] for n in range(len(sources))]
    products(ready, inner_ref, sources, outs)


def whole_kernel(*refs):
    ready, (gate_ref, kept_ref, partner_ref), part_refs, inner_ref = refs[:4], refs[4:7], refs[7:-1], refs[-1]

    def two(g, carry):
        pairs = [2 * g, 2 * g + 1]
        sources = [(kept_ref[k], partner_ref[k], gate_ref[k]) for k in pairs]
        products(ready, inner_ref, sources, [[(ref, k) for ref in part_refs] for k in pairs])
        return carry

    lax.fori_loop(0, kept_ref.shape[0] // 2, two, 0)


def finish_kernel(groups, chunks, *refs):
    out_ref = refs[-1]
    for group, steps in enumerate(groups):
        terms = refs[group * chunks : (group + 1) * chunks]
        for n in range(2 * len(steps)):
            total = terms[0][n]
            for term in terms[1:]:
                total = total + term[n].astype(F32)
            first, second = slot(n % 2, steps[n // 2])
            out_ref[first, second] = total.astype(BF16)


def vmem_specs(count):
    return [pl.BlockSpec(memory_space=pltpu.VMEM)] * count


def shaped(dtype, *shape):
    return jax.ShapeDtypeStruct(shape, dtype)


def kernel(body, outs, operands, spaces=(), scratch=(), flops=0):
    spaces = list(spaces) + [pltpu.VMEM] * (len(operands) - len(spaces))
    return pl.pallas_call(
        body,
        out_shape=outs,
        in_specs=[pl.BlockSpec(memory_space=space) for space in spaces],
        out_specs=vmem_specs(len(outs)),
        scratch_shapes=list(scratch),
        compiler_params=pltpu.CompilerParams(vmem_limit_bytes=24 * 1024 * 1024),
        cost_estimate=pl.CostEstimate(flops=flops, bytes_accessed=1 << 20, transcendentals=0),
    )(*operands)


def shards(amplitudes, vectors, tile_mask, pair_mask):
    firsts, seconds, slab, _ = amplitudes.shape
    pairs = firsts * seconds
    virt, chips, cores = lax.axis_size("virt"), lax.axis_size("occi"), lax.axis_size("occj")
    rows = slab // virt
    chunks = virt // 2
    depth = 2 * vectors.shape[0] * slab
    turned_mask = jnp.transpose(tile_mask, (0, 2, 3, 1))
    gate = shaped(F32, pairs, 8, slab)
    arranged = [shaped(BF16, depth // 2, slab), shaped(BF16, depth // 4, slab)]
    turn = functools.partial(turn_kernel, chunks)

    def parts(count):
        return [shaped(F32 if chunk == 0 else BF16, count, rows, slab) for chunk in range(chunks)]

    def inner(count):
        return pltpu.VMEM((count * chunks * rows, depth), BF16)

    def sent(part):
        return [part[0]] + [swap_virt(part[chunk], 2 * chunk) for chunk in range(1, chunks)]

    def work(count):
        return 2 * count * depth * slab * slab

    near = swap_virt(vectors, 1)
    if (firsts, seconds, chips, cores) == (2, CHIPS, CHIPS, 2):
        half_blocks = shaped(BF16, CHIPS, slab, slab)
        same, cross, gates = kernel(
            mask_split_kernel,
            [half_blocks, half_blocks, gate],
            [
                pltpu.with_memory_space_constraint(array, pltpu.HBM)
                for array in (turned_mask, pair_mask, amplitudes)
            ],
            spaces=[pltpu.HBM] * 3,
            scratch=[
                pltpu.SMEM(turned_mask.shape, jnp.int32),
                pltpu.SMEM(pair_mask.shape, jnp.int32),
                pltpu.SemaphoreType.DMA((pairs + 2,)),
            ],
        )
        other = swap_core(cross)
        packed = kernel(pack_kernel, [shaped(BF16, 2, slab, slab)] * (CHIPS - 1), (same, other))
        got = {step: swap_chip(block, step) for step, block in zip(STEPS, packed)}
        got[0] = other
        ready = kernel(turn, arranged, (vectors,)) + kernel(turn, arranged, (near,))
        finished = []
        for steps in GROUPS:
            part = kernel(
                functools.partial(group_kernel, chunks, steps),
                parts(2 * len(steps)),
                (*ready, gates, same, cross, *[got[step] for step in steps]),
                scratch=[inner(2 * len(steps))],
                flops=work(2 * len(steps)),
            )
            finished += sent(part)
        (out,) = kernel(
            functools.partial(finish_kernel, GROUPS, chunks),
            [shaped(BF16, firsts, seconds, rows, slab)],
            finished,
        )
        return out
    kept, gates = kernel(
        mask_whole_kernel,
        [shaped(BF16, pairs, slab, slab), gate],
        (turned_mask, pair_mask, amplitudes),
        spaces=[pltpu.SMEM] * 2,
    )
    partner = lax.all_to_all(kept, ("occj", "occi"), split_axis=0, concat_axis=0, tiled=True)
    ready = kernel(turn, arranged, (vectors,)) + kernel(turn, arranged, (near,))
    part = sent(
        kernel(whole_kernel, parts(pairs), (*ready, gates, kept, partner), scratch=[inner(2)], flops=work(pairs))
    )
    summed = part[0]
    for term in part[1:]:
        summed = summed + term.astype(F32)
    return summed.reshape(firsts, seconds, rows, slab).astype(BF16)


def solution(mesh):
    placed = (
        P("occi", "occj", None, None),
        P("virt", None, None),
        P("occi", "occj", None, None),
        P("occi", "occj"),
    )
    return jax.shard_map(
        shards,
        mesh=mesh,
        in_specs=placed,
        out_specs=P("occi", "occj", "virt", None),
        check_vma=False,
    )
```

```python
import functools

import jax
import jax.numpy as jnp
from jax import lax
from jax.experimental import pallas as pl
from jax.experimental.pallas import tpu as pltpu
from jax.sharding import PartitionSpec as P

TILE = 64
SLAB_TILES = 2
CHIPS = 4
STEPS = (3, 1, 2)
BF16 = jnp.bfloat16
F32 = jnp.float32


def swap_virt(array, step):
    return lax.ppermute(array, "virt", [(d, d ^ step) for d in range(lax.axis_size("virt"))])


def swap_core(array):
    return lax.ppermute(array, "occj", [(0, 1), (1, 0)])


def swap_chip(array, step):
    return lax.ppermute(array, "occi", [(d, d ^ step) for d in range(lax.axis_size("occi"))])


def slot(kind, step):
    first = lax.axis_index("occj") if kind == 0 else 1 - lax.axis_index("occj")
    return first, lax.axis_index("occi") ^ step


def keep_rows(mask_ref, first, second, half):
    lane = lax.broadcasted_iota(jnp.int32, (1, SLAB_TILES * TILE), 1) // TILE
    keep = jnp.zeros(lane.shape, F32)
    for tile in range(SLAB_TILES):
        keep = jnp.where(lane == tile, mask_ref[first, half, tile, second].astype(F32), keep)
    return jnp.broadcast_to(keep, (TILE, SLAB_TILES * TILE)).astype(BF16)


def mask_split_kernel(mask_hbm, pair_hbm, amp_hbm, vec_hbm, *refs):
    kept_refs, (gate_ref, part_ref, mask_ref, pair_ref, sems) = refs[:CHIPS], refs[CHIPS:]
    count = part_ref.shape[0]
    mine = vec_hbm.at[pl.ds(lax.axis_index("occj") * count, count)]
    copies = [
        pltpu.make_async_copy(mask_hbm, mask_ref, sems.at[0]),
        pltpu.make_async_copy(pair_hbm, pair_ref, sems.at[1]),
        pltpu.make_async_copy(mine, part_ref, sems.at[2]),
    ]
    blocks = []
    for step in STEPS + (0,):
        for kind in range(2):
            first, second = slot(kind, step)
            target = kept_refs[step].at[kind]
            copies.append(pltpu.make_async_copy(amp_hbm.at[first, second], target, sems.at[len(copies)]))
            blocks.append((first, second, target, kind * CHIPS + step, copies[-1]))
    for copy in copies:
        copy.start()
    copies[0].wait()
    copies[1].wait()
    for first, second, target, gate, copy in blocks:
        gate_ref[gate] = jnp.full(gate_ref.shape[1:], pair_ref[first, second].astype(F32))
        keeps = [keep_rows(mask_ref, first, second, half) for half in range(SLAB_TILES)]
        copy.wait()
        for half, keep in enumerate(keeps):
            part = slice(half * TILE, (half + 1) * TILE)
            target[part] = target[part] * keep
    copies[2].wait()


def mask_whole_kernel(mask_ref, pair_ref, amp_ref, kept_ref, gate_ref):
    seconds = amp_ref.shape[1]

    def one(block, carry):
        first, second = block // seconds, block % seconds
        for half in range(SLAB_TILES):
            part = slice(half * TILE, (half + 1) * TILE)
            kept_ref[block, part] = amp_ref[first, second, part] * keep_rows(mask_ref, first, second, half)
        gate_ref[block] = jnp.full(gate_ref.shape[1:], pair_ref[first, second].astype(F32))
        return carry

    lax.fori_loop(0, kept_ref.shape[0], one, 0)


def pack_kernel(*refs):
    for step in range(CHIPS):
        refs[-1][step] = refs[step][1]


def turn_kernel(chunks, *refs):
    vec_refs, turned_ref, left_ref = refs[:-2], refs[-2], refs[-1]
    slab = turned_ref.shape[1]
    rows = slab * left_ref.shape[0] // (turned_ref.shape[0] * chunks)
    me = lax.axis_index("virt")
    at, low = 0, 0
    for vec_ref in vec_refs:
        for q in range(vec_ref.shape[0]):
            turned_ref[at : at + slab] = vec_ref[q].astype(F32).T.astype(BF16)
            at += slab
            for chunk in range(chunks):
                start = pl.multiple_of((me ^ (2 * chunk)) * rows, rows)
                left_ref[low : low + rows] = vec_ref[q, pl.ds(start, rows), :]
                low += rows


def products(ready, inner_ref, sources, outs):
    turned_refs, left_refs = ready[::2], ready[1::2]
    slab = turned_refs[0].shape[1]
    depth = turned_refs[0].shape[0]
    vectors = depth // slab
    height = left_refs[0].shape[0] // vectors
    rows = height // len(outs[0])
    for base in range(0, len(sources), 2):
        both = [
            ((kept.astype(F32) + partner.astype(F32).T) * gate[:1]).astype(BF16)
            for kept, partner, gate in sources[base : base + 2]
        ]
        right = jnp.concatenate(both, axis=1)
        for side, left_ref in enumerate(left_refs):
            inner = jnp.dot(left_ref[...], right, preferred_element_type=F32).astype(BF16)
            for n in range(len(both)):
                for q in range(vectors):
                    at = side * depth + q * slab
                    inner_ref[(base + n) * height : (base + n + 1) * height, at : at + slab] = inner[
                        q * height : (q + 1) * height, n * slab : (n + 1) * slab
                    ]
    half = sum(
        jnp.dot(inner_ref[:, side * depth : (side + 1) * depth], turned_ref[...], preferred_element_type=F32)
        for side, turned_ref in enumerate(turned_refs)
    )
    for n, targets in enumerate(outs):
        for chunk, (ref, index) in enumerate(targets):
            start = n * height + chunk * rows
            ref[index] = half[start : start + rows].astype(ref.dtype)


def same_kernel(chunks, *refs):
    ready, gate_ref, kept_refs, refs = refs[:4], refs[4], refs[5 : 5 + CHIPS], refs[5 + CHIPS :]
    got_refs, part_refs, inner_ref = (kept_refs[0],) + refs[: CHIPS - 1], refs[CHIPS - 1 : -1], refs[-1]
    sources = [(kept_refs[step][0], got_refs[step][0], gate_ref[step]) for step in range(CHIPS)]
    products(ready, inner_ref, sources, [[(ref, n) for ref in part_refs] for n in range(CHIPS)])


def cross_kernel(chunks, *refs):
    ready, gate_ref, kept_refs, other_ref, refs = refs[:4], refs[4], refs[5 : 5 + CHIPS], refs[5 + CHIPS], refs[6 + CHIPS :]
    part_refs, inner_ref = refs[:-1], refs[-1]
    sources = [(kept_refs[step][1], other_ref[step], gate_ref[CHIPS + step]) for step in range(CHIPS)]
    products(ready, inner_ref, sources, [[(ref, n) for ref in part_refs] for n in range(CHIPS)])


def whole_kernel(*refs):
    ready, (gate_ref, kept_ref, partner_ref), part_refs, inner_ref = refs[:4], refs[4:7], refs[7:-1], refs[-1]

    def two(g, carry):
        pairs = [2 * g, 2 * g + 1]
        sources = [(kept_ref[k], partner_ref[k], gate_ref[k]) for k in pairs]
        products(ready, inner_ref, sources, [[(ref, k) for ref in part_refs] for k in pairs])
        return carry

    lax.fori_loop(0, kept_ref.shape[0] // 2, two, 0)


def finish_kernel(chunks, *refs):
    out_ref = refs[-1]
    for kind in range(2):
        terms = refs[kind * chunks : (kind + 1) * chunks]
        for step in range(CHIPS):
            total = terms[0][step]
            for term in terms[1:]:
                total = total + term[step].astype(F32)
            first, second = slot(kind, step)
            out_ref[first, second] = total.astype(BF16)


def vmem_specs(count):
    return [pl.BlockSpec(memory_space=pltpu.VMEM)] * count


def shaped(dtype, *shape):
    return jax.ShapeDtypeStruct(shape, dtype)


def kernel(body, outs, operands, spaces=(), scratch=(), flops=0):
    spaces = list(spaces) + [pltpu.VMEM] * (len(operands) - len(spaces))
    return pl.pallas_call(
        body,
        out_shape=outs,
        in_specs=[pl.BlockSpec(memory_space=space) for space in spaces],
        out_specs=vmem_specs(len(outs)),
        scratch_shapes=list(scratch),
        compiler_params=pltpu.CompilerParams(vmem_limit_bytes=24 * 1024 * 1024),
        cost_estimate=pl.CostEstimate(flops=flops, bytes_accessed=1 << 20, transcendentals=0),
    )(*operands)


def shards(amplitudes, vectors, tile_mask, pair_mask):
    firsts, seconds, slab, _ = amplitudes.shape
    pairs = firsts * seconds
    virt, chips, cores = lax.axis_size("virt"), lax.axis_size("occi"), lax.axis_size("occj")
    rows = slab // virt
    chunks = virt // 2
    depth = 2 * vectors.shape[0] * slab
    turned_mask = jnp.transpose(tile_mask, (0, 2, 3, 1))
    gate = shaped(F32, pairs, 8, slab)
    arranged = [shaped(BF16, depth // 2, slab), shaped(BF16, depth // 4, slab)]
    turn = functools.partial(turn_kernel, chunks)

    def parts(count):
        return [shaped(F32 if chunk == 0 else BF16, count, rows, slab) for chunk in range(chunks)]

    def inner(count):
        return pltpu.VMEM((count * chunks * rows, depth), BF16)

    def sent(part):
        return [part[0]] + [swap_virt(part[chunk], 2 * chunk) for chunk in range(1, chunks)]

    def work(count):
        return 2 * count * depth * slab * slab

    if (firsts, seconds, chips, cores) == (2, CHIPS, CHIPS, 2):
        half_vectors = shaped(vectors.dtype, vectors.shape[0] // 2, slab, slab)
        *kept, gates, mine = kernel(
            mask_split_kernel,
            [shaped(BF16, 2, slab, slab)] * CHIPS + [gate, half_vectors],
            [
                pltpu.with_memory_space_constraint(array, pltpu.HBM)
                for array in (turned_mask, pair_mask, amplitudes, vectors)
            ],
            spaces=[pltpu.HBM] * 4,
            scratch=[
                pltpu.SMEM(turned_mask.shape, jnp.int32),
                pltpu.SMEM(pair_mask.shape, jnp.int32),
                pltpu.SemaphoreType.DMA((pairs + 3,)),
            ],
        )
        near = swap_virt(mine, 1)
        swapped = {step: swap_chip(kept[step], step) for step in STEPS}
        got = [swapped[step] for step in range(1, CHIPS)]
        beside = swap_core(near)
        (packed,) = kernel(pack_kernel, [shaped(BF16, CHIPS, slab, slab)], (kept[0], *got))
        other = swap_core(packed)
        ready = kernel(turn, arranged, (vectors,)) + kernel(turn, arranged, (near, beside))
        finished = []
        for body, partners in ((same_kernel, got), (cross_kernel, [other])):
            part = kernel(
                functools.partial(body, chunks),
                parts(CHIPS),
                (*ready, gates, *kept, *partners),
                scratch=[inner(CHIPS)],
                flops=work(CHIPS),
            )
            finished += sent(part)
        (out,) = kernel(
            functools.partial(finish_kernel, chunks), [shaped(BF16, firsts, seconds, rows, slab)], finished
        )
        return out
    kept, gates = kernel(
        mask_whole_kernel,
        [shaped(BF16, pairs, slab, slab), gate],
        (turned_mask, pair_mask, amplitudes),
        spaces=[pltpu.SMEM] * 2,
    )
    partner = lax.all_to_all(kept, ("occj", "occi"), split_axis=0, concat_axis=0, tiled=True)
    ready = kernel(turn, arranged, (vectors,)) + kernel(turn, arranged, (swap_virt(vectors, 1),))
    part = sent(
        kernel(whole_kernel, parts(pairs), (*ready, gates, kept, partner), scratch=[inner(2)], flops=work(pairs))
    )
    summed = part[0]
    for term in part[1:]:
        summed = summed + term.astype(F32)
    return summed.reshape(firsts, seconds, rows, slab).astype(BF16)


def solution(mesh):
    placed = (
        P("occi", "occj", None, None),
        P("virt", None, None),
        P("occi", "occj", None, None),
        P("occi", "occj"),
    )
    return jax.shard_map(
        shards,
        mesh=mesh,
        in_specs=placed,
        out_specs=P("occi", "occj", "virt", None),
        check_vma=False,
    )
```

```python
import functools

import jax
import jax.numpy as jnp
from jax import lax
from jax.experimental import pallas as pl
from jax.experimental.pallas import tpu as pltpu
from jax.sharding import PartitionSpec as P

TILE = 64
SLAB_TILES = 2
CHIPS = 4
STEPS = (3, 1, 2)
GROUPS = ((0, 3), (1, 2))
BF16 = jnp.bfloat16
F32 = jnp.float32


def swap_virt(array, step):
    return lax.ppermute(array, "virt", [(d, d ^ step) for d in range(lax.axis_size("virt"))])


def move_virt(array, step, up):
    size = lax.axis_size("virt")
    low = [d for d in range(size) if not d & step]
    return lax.ppermute(array, "virt", [(d, d + step) if up else (d + step, d) for d in low])


def swap_core(array):
    return lax.ppermute(array, "occj", [(0, 1), (1, 0)])


def swap_chip(array, step):
    return lax.ppermute(array, "occi", [(d, d ^ step) for d in range(lax.axis_size("occi"))])


def slot(kind, step):
    first = lax.axis_index("occj") if kind == 0 else 1 - lax.axis_index("occj")
    return first, lax.axis_index("occi") ^ step


def keep_rows(mask_ref, first, second, half):
    lane = lax.broadcasted_iota(jnp.int32, (1, SLAB_TILES * TILE), 1) // TILE
    keep = jnp.zeros(lane.shape, F32)
    for tile in range(SLAB_TILES):
        keep = jnp.where(lane == tile, mask_ref[first, half, tile, second].astype(F32), keep)
    return jnp.broadcast_to(keep, (TILE, SLAB_TILES * TILE)).astype(BF16)


def mask_split_kernel(mask_hbm, pair_hbm, amp_hbm, same_ref, cross_ref, gate_ref, mask_ref, pair_ref, sems):
    copies = [
        pltpu.make_async_copy(mask_hbm, mask_ref, sems.at[0]),
        pltpu.make_async_copy(pair_hbm, pair_ref, sems.at[1]),
    ]
    blocks = []
    for kind, kept_ref in ((1, cross_ref), (0, same_ref)):
        for step in range(CHIPS):
            first, second = slot(kind, step)
            copies.append(
                pltpu.make_async_copy(amp_hbm.at[first, second], kept_ref.at[step], sems.at[len(copies)])
            )
            blocks.append((first, second, kept_ref, step, kind * CHIPS + step, copies[-1]))
    for copy in copies:
        copy.start()
    copies[0].wait()
    copies[1].wait()
    for first, second, kept_ref, step, gate, copy in blocks:
        gate_ref[gate] = jnp.full(gate_ref.shape[1:], pair_ref[first, second].astype(F32))
        keeps = [keep_rows(mask_ref, first, second, half) for half in range(SLAB_TILES)]
        copy.wait()
        for half, keep in enumerate(keeps):
            part = slice(half * TILE, (half + 1) * TILE)
            kept_ref[step, part] = kept_ref[step, part] * keep


def mask_whole_kernel(mask_ref, pair_ref, amp_ref, kept_ref, gate_ref):
    seconds = amp_ref.shape[1]

    def one(block, carry):
        first, second = block // seconds, block % seconds
        for half in range(SLAB_TILES):
            part = slice(half * TILE, (half + 1) * TILE)
            kept_ref[block, part] = amp_ref[first, second, part] * keep_rows(mask_ref, first, second, half)
        gate_ref[block] = jnp.full(gate_ref.shape[1:], pair_ref[first, second].astype(F32))
        return carry

    lax.fori_loop(0, kept_ref.shape[0], one, 0)


def pack_kernel(same_ref, other_ref, *send_refs):
    for step, send_ref in zip(STEPS, send_refs):
        send_ref[0] = same_ref[step]
        send_ref[1] = other_ref[step]


def turn_kernel(chunks, vec_ref, turned_ref, left_ref):
    vectors, slab, _ = vec_ref.shape
    rows = left_ref.shape[0] // (vectors * chunks)
    me = lax.axis_index("virt")
    for q in range(vectors):
        turned_ref[q * slab : (q + 1) * slab] = vec_ref[q].astype(F32).T.astype(BF16)
        for chunk in range(chunks):
            start = pl.multiple_of((me ^ (2 * chunk)) * rows, rows)
            low = (q * chunks + chunk) * rows
            left_ref[low : low + rows] = vec_ref[q, pl.ds(start, rows), :]


def products(ready, inner_ref, sources, outs):
    turned_refs, left_refs = ready[::2], ready[1::2]
    slab = turned_refs[0].shape[1]
    depth = turned_refs[0].shape[0]
    vectors = depth // slab
    height = left_refs[0].shape[0] // vectors
    rows = height // len(outs[0])
    for base in range(0, len(sources), 2):
        both = [
            ((kept.astype(F32) + partner.astype(F32).T) * gate[:1]).astype(BF16)
            for kept, partner, gate in sources[base : base + 2]
        ]
        right = jnp.concatenate(both, axis=1)
        for side, left_ref in enumerate(left_refs):
            inner = jnp.dot(left_ref[...], right, preferred_element_type=F32).astype(BF16)
            for n in range(len(both)):
                for q in range(vectors):
                    at = side * depth + q * slab
                    inner_ref[(base + n) * height : (base + n + 1) * height, at : at + slab] = inner[
                        q * height : (q + 1) * height, n * slab : (n + 1) * slab
                    ]
    half = sum(
        jnp.dot(inner_ref[:, side * depth : (side + 1) * depth], turned_ref[...], preferred_element_type=F32)
        for side, turned_ref in enumerate(turned_refs)
    )
    for n, targets in enumerate(outs):
        for chunk, (ref, index) in enumerate(targets):
            start = n * height + chunk * rows
            ref[index] = half[start : start + rows].astype(ref.dtype)


def group_kernel(chunks, steps, *refs):
    ready, (gate_ref, same_ref, cross_ref), refs = refs[:4], refs[4:7], refs[7:]
    got_refs, refs = refs[: len(steps)], refs[len(steps) :]
    joined = len(refs) > chunks + 1
    part_refs, inner_ref = refs[joined : joined + chunks], refs[-1]
    sources = []
    for step, got_ref in zip(steps, got_refs):
        if step:
            partners = got_ref[0], got_ref[1]
        else:
            partners = same_ref[0], got_ref[0]
        sources.append((same_ref[step], partners[0], gate_ref[step]))
        sources.append((cross_ref[step], partners[1], gate_ref[CHIPS + step]))
    outs = [[(ref, n) for ref in part_refs] for n in range(len(sources))]
    products(ready, inner_ref, sources, outs)
    if joined:
        refs[-3][...] = refs[0][...]
        refs[-2][...] = part_refs[1][...]


def whole_kernel(*refs):
    ready, (gate_ref, kept_ref, partner_ref), part_refs, inner_ref = refs[:4], refs[4:7], refs[7:-1], refs[-1]

    def two(g, carry):
        pairs = [2 * g, 2 * g + 1]
        sources = [(kept_ref[k], partner_ref[k], gate_ref[k]) for k in pairs]
        products(ready, inner_ref, sources, [[(ref, k) for ref in part_refs] for k in pairs])
        return carry

    lax.fori_loop(0, kept_ref.shape[0] // 2, two, 0)


def add_kernel(own_ref, down_ref, *refs):
    refs[-1][...] = own_ref[...] + down_ref[...].astype(F32)


def finish_kernel(*refs):
    total_refs, up_refs, out_ref = refs[: len(GROUPS)], refs[len(GROUPS) : -1], refs[-1]
    for steps, total_ref, up_ref in zip(GROUPS, total_refs, up_refs):
        for n in range(2 * len(steps)):
            first, second = slot(n % 2, steps[n // 2])
            out_ref[first, second] = (total_ref[n] + up_ref[n].astype(F32)).astype(BF16)


def vmem_specs(count):
    return [pl.BlockSpec(memory_space=pltpu.VMEM)] * count


def shaped(dtype, *shape):
    return jax.ShapeDtypeStruct(shape, dtype)


def kernel(body, outs, operands, spaces=(), scratch=(), flops=0):
    spaces = list(spaces) + [pltpu.VMEM] * (len(operands) - len(spaces))
    return pl.pallas_call(
        body,
        out_shape=outs,
        in_specs=[pl.BlockSpec(memory_space=space) for space in spaces],
        out_specs=vmem_specs(len(outs)),
        scratch_shapes=list(scratch),
        compiler_params=pltpu.CompilerParams(vmem_limit_bytes=24 * 1024 * 1024),
        cost_estimate=pl.CostEstimate(flops=flops, bytes_accessed=1 << 20, transcendentals=0),
    )(*operands)


def shards(amplitudes, vectors, tile_mask, pair_mask):
    firsts, seconds, slab, _ = amplitudes.shape
    pairs = firsts * seconds
    virt, chips, cores = lax.axis_size("virt"), lax.axis_size("occi"), lax.axis_size("occj")
    rows = slab // virt
    chunks = virt // 2
    depth = 2 * vectors.shape[0] * slab
    turned_mask = jnp.transpose(tile_mask, (0, 2, 3, 1))
    gate = shaped(F32, pairs, 8, slab)
    arranged = [shaped(BF16, depth // 2, slab), shaped(BF16, depth // 4, slab)]
    turn = functools.partial(turn_kernel, chunks)

    def parts(count):
        return [shaped(F32 if chunk == 0 else BF16, count, rows, slab) for chunk in range(chunks)]

    def inner(count):
        return pltpu.VMEM((count * chunks * rows, depth), BF16)

    def sent(part):
        return [part[0]] + [swap_virt(part[chunk], 2 * chunk) for chunk in range(1, chunks)]

    def work(count):
        return 2 * count * depth * slab * slab

    near = swap_virt(vectors, 1)
    if (firsts, seconds, chips, cores, virt) == (2, CHIPS, CHIPS, 2, 4):
        half_blocks = shaped(BF16, CHIPS, slab, slab)
        same, cross, gates = kernel(
            mask_split_kernel,
            [half_blocks, half_blocks, gate],
            [
                pltpu.with_memory_space_constraint(array, pltpu.HBM)
                for array in (turned_mask, pair_mask, amplitudes)
            ],
            spaces=[pltpu.HBM] * 3,
            scratch=[
                pltpu.SMEM(turned_mask.shape, jnp.int32),
                pltpu.SMEM(pair_mask.shape, jnp.int32),
                pltpu.SemaphoreType.DMA((pairs + 2,)),
            ],
        )
        other = swap_core(cross)
        packed = kernel(pack_kernel, [shaped(BF16, 2, slab, slab)] * (CHIPS - 1), (same, other))
        got = {step: swap_chip(block, step) for step, block in zip(STEPS, packed)}
        got[0] = other
        ready = kernel(turn, arranged, (vectors,)) + kernel(turn, arranged, (near,))
        owned, down, leaving = [], [], []
        for steps in GROUPS:
            count = 2 * len(steps)
            own, sending, *leaving = kernel(
                functools.partial(group_kernel, chunks, steps),
                parts(count) + [shaped(BF16, count, rows, slab)] * (2 * len(leaving)),
                (*ready, gates, same, cross, *[got[step] for step in steps], *leaving),
                scratch=[inner(count)],
                flops=work(count),
            )
            owned.append(own)
            down.append(move_virt(sending, 2, False))
            leaving = leaving or [sending]
        up = [move_virt(sending, 2, True) for sending in leaving]
        totals = []
        for own, arrived in zip(owned, down):
            totals += kernel(
                add_kernel,
                [shaped(F32, *own.shape)],
                (own, arrived, *totals),
                spaces=[pltpu.VMEM] * 2 + [pl.ANY] * len(totals),
                flops=work(pairs),
            )
        (out,) = kernel(finish_kernel, [shaped(BF16, firsts, seconds, rows, slab)], (*totals, *up))
        return out
    kept, gates = kernel(
        mask_whole_kernel,
        [shaped(BF16, pairs, slab, slab), gate],
        (turned_mask, pair_mask, amplitudes),
        spaces=[pltpu.SMEM] * 2,
    )
    partner = lax.all_to_all(kept, ("occj", "occi"), split_axis=0, concat_axis=0, tiled=True)
    ready = kernel(turn, arranged, (vectors,)) + kernel(turn, arranged, (near,))
    part = sent(
        kernel(whole_kernel, parts(pairs), (*ready, gates, kept, partner), scratch=[inner(2)], flops=work(pairs))
    )
    summed = part[0]
    for term in part[1:]:
        summed = summed + term.astype(F32)
    return summed.reshape(firsts, seconds, rows, slab).astype(BF16)


def solution(mesh):
    placed = (
        P("occi", "occj", None, None),
        P("virt", None, None),
        P("occi", "occj", None, None),
        P("occi", "occj"),
    )
    return jax.shard_map(
        shards,
        mesh=mesh,
        in_specs=placed,
        out_specs=P("occi", "occj", "virt", None),
        check_vma=False,
    )
```

```python
import functools

import jax
import jax.numpy as jnp
from jax import lax
from jax.experimental import pallas as pl
from jax.experimental.pallas import tpu as pltpu
from jax.sharding import PartitionSpec as P

TILE = 64
SLAB_TILES = 2
CHIPS = 4
STEPS = (3, 1, 2)
GROUPS = ((0, 3, 1), (2,))
BF16 = jnp.bfloat16
F32 = jnp.float32


def swap_virt(array, step):
    return lax.ppermute(array, "virt", [(d, d ^ step) for d in range(lax.axis_size("virt"))])


def swap_core(array):
    return lax.ppermute(array, "occj", [(0, 1), (1, 0)])


def swap_chip(array, step):
    return lax.ppermute(array, "occi", [(d, d ^ step) for d in range(lax.axis_size("occi"))])


def slot(kind, step):
    first = lax.axis_index("occj") if kind == 0 else 1 - lax.axis_index("occj")
    return first, lax.axis_index("occi") ^ step


def keep_rows(mask_ref, first, second, half):
    lane = lax.broadcasted_iota(jnp.int32, (1, SLAB_TILES * TILE), 1) // TILE
    keep = jnp.zeros(lane.shape, F32)
    for tile in range(SLAB_TILES):
        keep = jnp.where(lane == tile, mask_ref[first, half, tile, second].astype(F32), keep)
    return jnp.broadcast_to(keep, (TILE, SLAB_TILES * TILE)).astype(BF16)


def mask_split_kernel(mask_hbm, pair_hbm, amp_hbm, same_ref, cross_ref, gate_ref, mask_ref, pair_ref, sems):
    copies = [
        pltpu.make_async_copy(mask_hbm, mask_ref, sems.at[0]),
        pltpu.make_async_copy(pair_hbm, pair_ref, sems.at[1]),
    ]
    blocks = []
    for kind, kept_ref in ((1, cross_ref), (0, same_ref)):
        for step in range(CHIPS):
            first, second = slot(kind, step)
            copies.append(
                pltpu.make_async_copy(amp_hbm.at[first, second], kept_ref.at[step], sems.at[len(copies)])
            )
            blocks.append((first, second, kept_ref, step, kind * CHIPS + step, copies[-1]))
    for copy in copies:
        copy.start()
    copies[0].wait()
    copies[1].wait()
    for first, second, kept_ref, step, gate, copy in blocks:
        gate_ref[gate] = jnp.full(gate_ref.shape[1:], pair_ref[first, second].astype(F32))
        keeps = [keep_rows(mask_ref, first, second, half) for half in range(SLAB_TILES)]
        copy.wait()
        for half, keep in enumerate(keeps):
            part = slice(half * TILE, (half + 1) * TILE)
            kept_ref[step, part] = kept_ref[step, part] * keep


def mask_whole_kernel(mask_ref, pair_ref, amp_ref, kept_ref, gate_ref):
    seconds = amp_ref.shape[1]

    def one(block, carry):
        first, second = block // seconds, block % seconds
        for half in range(SLAB_TILES):
            part = slice(half * TILE, (half + 1) * TILE)
            kept_ref[block, part] = amp_ref[first, second, part] * keep_rows(mask_ref, first, second, half)
        gate_ref[block] = jnp.full(gate_ref.shape[1:], pair_ref[first, second].astype(F32))
        return carry

    lax.fori_loop(0, kept_ref.shape[0], one, 0)


def pack_kernel(same_ref, other_ref, *send_refs):
    for step, send_ref in zip(STEPS, send_refs):
        send_ref[0] = same_ref[step]
        send_ref[1] = other_ref[step]


def turn_kernel(chunks, vec_ref, turned_ref, left_ref):
    vectors, slab, _ = vec_ref.shape
    rows = left_ref.shape[0] // (vectors * chunks)
    me = lax.axis_index("virt")
    for q in range(vectors):
        turned_ref[q * slab : (q + 1) * slab] = vec_ref[q].astype(F32).T.astype(BF16)
        for chunk in range(chunks):
            start = pl.multiple_of((me ^ (2 * chunk)) * rows, rows)
            low = (q * chunks + chunk) * rows
            left_ref[low : low + rows] = vec_ref[q, pl.ds(start, rows), :]


def products(ready, inner_ref, sources, outs):
    turned_refs, left_refs = ready[::2], ready[1::2]
    slab = turned_refs[0].shape[1]
    depth = turned_refs[0].shape[0]
    vectors = depth // slab
    height = left_refs[0].shape[0] // vectors
    rows = height // len(outs[0])
    for base in range(0, len(sources), 2):
        both = [
            ((kept.astype(F32) + partner.astype(F32).T) * gate[:1]).astype(BF16)
            for kept, partner, gate in sources[base : base + 2]
        ]
        right = jnp.concatenate(both, axis=1)
        for side, left_ref in enumerate(left_refs):
            inner = jnp.dot(left_ref[...], right, preferred_element_type=F32).astype(BF16)
            for n in range(len(both)):
                for q in range(vectors):
                    at = side * depth + q * slab
                    inner_ref[(base + n) * height : (base + n + 1) * height, at : at + slab] = inner[
                        q * height : (q + 1) * height, n * slab : (n + 1) * slab
                    ]
    half = sum(
        jnp.dot(inner_ref[:, side * depth : (side + 1) * depth], turned_ref[...], preferred_element_type=F32)
        for side, turned_ref in enumerate(turned_refs)
    )
    for n, targets in enumerate(outs):
        for chunk, (ref, index) in enumerate(targets):
            start = n * height + chunk * rows
            ref[index] = half[start : start + rows].astype(ref.dtype)


def group_kernel(chunks, steps, *refs):
    ready, (gate_ref, same_ref, cross_ref), refs = refs[:4], refs[4:7], refs[7:]
    got_refs, refs = refs[: len(steps)], refs[len(steps) :]
    joined = len(refs) > chunks + 1
    part_refs, inner_ref = refs[joined : joined + chunks], refs[-1]
    sources = []
    for step, got_ref in zip(steps, got_refs):
        if step:
            partners = got_ref[0], got_ref[1]
        else:
            partners = same_ref[0], got_ref[0]
        sources.append((same_ref[step], partners[0], gate_ref[step]))
        sources.append((cross_ref[step], partners[1], gate_ref[CHIPS + step]))
    outs = [[(ref, n) for ref in part_refs] for n in range(len(sources))]
    products(ready, inner_ref, sources, outs)
    if joined:
        count = refs[0].shape[0]
        refs[-2][:count] = refs[0][...]
        refs[-2][count:] = part_refs[1][...]


def whole_kernel(*refs):
    ready, (gate_ref, kept_ref, partner_ref), part_refs, inner_ref = refs[:4], refs[4:7], refs[7:-1], refs[-1]

    def two(g, carry):
        pairs = [2 * g, 2 * g + 1]
        sources = [(kept_ref[k], partner_ref[k], gate_ref[k]) for k in pairs]
        products(ready, inner_ref, sources, [[(ref, k) for ref in part_refs] for k in pairs])
        return carry

    lax.fori_loop(0, kept_ref.shape[0] // 2, two, 0)


def finish_kernel(*refs):
    own_refs, got_ref, out_ref = refs[: len(GROUPS)], refs[-2], refs[-1]
    at = 0
    for steps, own_ref in zip(GROUPS, own_refs):
        for n in range(2 * len(steps)):
            first, second = slot(n % 2, steps[n // 2])
            out_ref[first, second] = (own_ref[n] + got_ref[at].astype(F32)).astype(BF16)
            at += 1


def vmem_specs(count):
    return [pl.BlockSpec(memory_space=pltpu.VMEM)] * count


def shaped(dtype, *shape):
    return jax.ShapeDtypeStruct(shape, dtype)


def kernel(body, outs, operands, spaces=(), scratch=(), flops=0):
    spaces = list(spaces) + [pltpu.VMEM] * (len(operands) - len(spaces))
    return pl.pallas_call(
        body,
        out_shape=outs,
        in_specs=[pl.BlockSpec(memory_space=space) for space in spaces],
        out_specs=vmem_specs(len(outs)),
        scratch_shapes=list(scratch),
        compiler_params=pltpu.CompilerParams(vmem_limit_bytes=24 * 1024 * 1024),
        cost_estimate=pl.CostEstimate(flops=flops, bytes_accessed=1 << 20, transcendentals=0),
    )(*operands)


def shards(amplitudes, vectors, tile_mask, pair_mask):
    firsts, seconds, slab, _ = amplitudes.shape
    pairs = firsts * seconds
    virt, chips, cores = lax.axis_size("virt"), lax.axis_size("occi"), lax.axis_size("occj")
    rows = slab // virt
    chunks = virt // 2
    depth = 2 * vectors.shape[0] * slab
    turned_mask = jnp.transpose(tile_mask, (0, 2, 3, 1))
    gate = shaped(F32, pairs, 8, slab)
    arranged = [shaped(BF16, depth // 2, slab), shaped(BF16, depth // 4, slab)]
    turn = functools.partial(turn_kernel, chunks)

    def parts(count):
        return [shaped(F32 if chunk == 0 else BF16, count, rows, slab) for chunk in range(chunks)]

    def inner(count):
        return pltpu.VMEM((count * chunks * rows, depth), BF16)

    def sent(part):
        return [part[0]] + [swap_virt(part[chunk], 2 * chunk) for chunk in range(1, chunks)]

    def work(count):
        return 2 * count * depth * slab * slab

    near = swap_virt(vectors, 1)
    if (firsts, seconds, chips, cores, virt) == (2, CHIPS, CHIPS, 2, 4):
        half_blocks = shaped(BF16, CHIPS, slab, slab)
        same, cross, gates = kernel(
            mask_split_kernel,
            [half_blocks, half_blocks, gate],
            [
                pltpu.with_memory_space_constraint(array, pltpu.HBM)
                for array in (turned_mask, pair_mask, amplitudes)
            ],
            spaces=[pltpu.HBM] * 3,
            scratch=[
                pltpu.SMEM(turned_mask.shape, jnp.int32),
                pltpu.SMEM(pair_mask.shape, jnp.int32),
                pltpu.SemaphoreType.DMA((pairs + 2,)),
            ],
        )
        other = swap_core(cross)
        packed = kernel(pack_kernel, [shaped(BF16, 2, slab, slab)] * (CHIPS - 1), (same, other))
        got = {step: swap_chip(block, step) for step, block in zip(STEPS, packed)}
        got[0] = other
        ready = kernel(turn, arranged, (vectors,)) + kernel(turn, arranged, (near,))
        owned, leaving = [], []
        for steps in GROUPS:
            count = 2 * len(steps)
            own, *leaving = kernel(
                functools.partial(group_kernel, chunks, steps),
                parts(count) + [shaped(BF16, pairs, rows, slab)] * len(leaving),
                (*ready, gates, same, cross, *[got[step] for step in steps], *leaving),
                scratch=[inner(count)],
                flops=work(count),
            )
            owned.append(own)
        operands = (*owned, swap_virt(leaving[-1], 2))
        (out,) = kernel(finish_kernel, [shaped(BF16, firsts, seconds, rows, slab)], operands)
        return out
    kept, gates = kernel(
        mask_whole_kernel,
        [shaped(BF16, pairs, slab, slab), gate],
        (turned_mask, pair_mask, amplitudes),
        spaces=[pltpu.SMEM] * 2,
    )
    partner = lax.all_to_all(kept, ("occj", "occi"), split_axis=0, concat_axis=0, tiled=True)
    ready = kernel(turn, arranged, (vectors,)) + kernel(turn, arranged, (near,))
    part = sent(
        kernel(whole_kernel, parts(pairs), (*ready, gates, kept, partner), scratch=[inner(2)], flops=work(pairs))
    )
    summed = part[0]
    for term in part[1:]:
        summed = summed + term.astype(F32)
    return summed.reshape(firsts, seconds, rows, slab).astype(BF16)


def solution(mesh):
    placed = (
        P("occi", "occj", None, None),
        P("virt", None, None),
        P("occi", "occj", None, None),
        P("occi", "occj"),
    )
    return jax.shard_map(
        shards,
        mesh=mesh,
        in_specs=placed,
        out_specs=P("occi", "occj", "virt", None),
        check_vma=False,
    )
```

```python
import functools

import jax
import jax.numpy as jnp
from jax import lax
from jax.experimental import pallas as pl
from jax.experimental.pallas import tpu as pltpu
from jax.sharding import PartitionSpec as P

TILE = 64
SLAB_TILES = 2
CHIPS = 4
STEPS = (3, 1, 2)
GROUPS = ((0, 3), (1, 2))
BF16 = jnp.bfloat16
F32 = jnp.float32


def swap_virt(array, step):
    return lax.ppermute(array, "virt", [(d, d ^ step) for d in range(lax.axis_size("virt"))])


def swap_core(array):
    return lax.ppermute(array, "occj", [(0, 1), (1, 0)])


def swap_chip(array, step):
    return lax.ppermute(array, "occi", [(d, d ^ step) for d in range(lax.axis_size("occi"))])


def slot(kind, step):
    first = lax.axis_index("occj") if kind == 0 else 1 - lax.axis_index("occj")
    return first, lax.axis_index("occi") ^ step


def keep_rows(mask_ref, first, second, half):
    lane = lax.broadcasted_iota(jnp.int32, (1, SLAB_TILES * TILE), 1) // TILE
    keep = jnp.zeros(lane.shape, F32)
    for tile in range(SLAB_TILES):
        keep = jnp.where(lane == tile, mask_ref[first, half, tile, second].astype(F32), keep)
    return jnp.broadcast_to(keep, (TILE, SLAB_TILES * TILE)).astype(BF16)


def mask_split_kernel(mask_hbm, pair_hbm, amp_hbm, same_ref, cross_ref, gate_ref, mask_ref, pair_ref, sems):
    copies = [
        pltpu.make_async_copy(mask_hbm, mask_ref, sems.at[0]),
        pltpu.make_async_copy(pair_hbm, pair_ref, sems.at[1]),
    ]
    blocks = []
    for kind, kept_ref in ((1, cross_ref), (0, same_ref)):
        for step in range(CHIPS):
            first, second = slot(kind, step)
            copies.append(
                pltpu.make_async_copy(amp_hbm.at[first, second], kept_ref.at[step], sems.at[len(copies)])
            )
            blocks.append((first, second, kept_ref, step, kind * CHIPS + step, copies[-1]))
    for copy in copies:
        copy.start()
    copies[0].wait()
    copies[1].wait()
    for first, second, kept_ref, step, gate, copy in blocks:
        gate_ref[gate] = jnp.full(gate_ref.shape[1:], pair_ref[first, second].astype(F32))
        keeps = [keep_rows(mask_ref, first, second, half) for half in range(SLAB_TILES)]
        copy.wait()
        for half, keep in enumerate(keeps):
            part = slice(half * TILE, (half + 1) * TILE)
            kept_ref[step, part] = kept_ref[step, part] * keep


def mask_whole_kernel(mask_ref, pair_ref, amp_ref, kept_ref, gate_ref):
    seconds = amp_ref.shape[1]

    def one(block, carry):
        first, second = block // seconds, block % seconds
        for half in range(SLAB_TILES):
            part = slice(half * TILE, (half + 1) * TILE)
            kept_ref[block, part] = amp_ref[first, second, part] * keep_rows(mask_ref, first, second, half)
        gate_ref[block] = jnp.full(gate_ref.shape[1:], pair_ref[first, second].astype(F32))
        return carry

    lax.fori_loop(0, kept_ref.shape[0], one, 0)


def pack_kernel(same_ref, other_ref, *send_refs):
    for step, send_ref in zip(STEPS, send_refs):
        send_ref[0] = same_ref[step]
        send_ref[1] = other_ref[step]


def turn_kernel(chunks, vec_ref, turned_ref, left_ref):
    vectors, slab, _ = vec_ref.shape
    rows = left_ref.shape[0] // (vectors * chunks)
    me = lax.axis_index("virt")
    for q in range(vectors):
        turned_ref[q * slab : (q + 1) * slab] = vec_ref[q].astype(F32).T.astype(BF16)
        for chunk in range(chunks):
            start = pl.multiple_of((me ^ chunk) * rows, rows)
            low = (q * chunks + chunk) * rows
            left_ref[low : low + rows] = vec_ref[q, pl.ds(start, rows), :]


def products(ready, inner_ref, sources, outs):
    turned_refs, left_refs = ready[::2], ready[1::2]
    slab = turned_refs[0].shape[1]
    depth = turned_refs[0].shape[0]
    vectors = depth // slab
    height = left_refs[0].shape[0] // vectors
    rows = height // len(outs[0])
    for base in range(0, len(sources), 2):
        both = [
            ((kept.astype(F32) + partner.astype(F32).T) * gate[:1]).astype(BF16)
            for kept, partner, gate in sources[base : base + 2]
        ]
        right = jnp.concatenate(both, axis=1)
        for side, left_ref in enumerate(left_refs):
            inner = jnp.dot(left_ref[...], right, preferred_element_type=F32).astype(BF16)
            for n in range(len(both)):
                for q in range(vectors):
                    at = side * depth + q * slab
                    inner_ref[(base + n) * height : (base + n + 1) * height, at : at + slab] = inner[
                        q * height : (q + 1) * height, n * slab : (n + 1) * slab
                    ]
    half = sum(
        jnp.dot(inner_ref[:, side * depth : (side + 1) * depth], turned_ref[...], preferred_element_type=F32)
        for side, turned_ref in enumerate(turned_refs)
    )
    for n, targets in enumerate(outs):
        for chunk, (ref, index) in enumerate(targets):
            start = n * height + chunk * rows
            ref[index] = half[start : start + rows].astype(ref.dtype)


def group_kernel(chunks, steps, *refs):
    ready, (gate_ref, same_ref, cross_ref), refs = refs[:4], refs[4:7], refs[7:]
    got_refs, part_refs, inner_ref = refs[: len(steps)], refs[len(steps) : -1], refs[-1]
    sources = []
    for step, got_ref in zip(steps, got_refs):
        if step:
            partners = got_ref[0], got_ref[1]
        else:
            partners = same_ref[0], got_ref[0]
        sources.append((same_ref[step], partners[0], gate_ref[step]))
        sources.append((cross_ref[step], partners[1], gate_ref[CHIPS + step]))
    outs = [[(ref, n) for ref in part_refs] for n in range(len(sources))]
    products(ready, inner_ref, sources, outs)


def whole_kernel(*refs):
    ready, (gate_ref, kept_ref, partner_ref), part_refs, inner_ref = refs[:4], refs[4:7], refs[7:-1], refs[-1]

    def two(g, carry):
        pairs = [2 * g, 2 * g + 1]
        sources = [(kept_ref[k], partner_ref[k], gate_ref[k]) for k in pairs]
        products(ready, inner_ref, sources, [[(ref, k) for ref in part_refs] for k in pairs])
        return carry

    lax.fori_loop(0, kept_ref.shape[0] // 2, two, 0)


def finish_kernel(groups, chunks, *refs):
    out_ref = refs[-1]
    for group, steps in enumerate(groups):
        terms = refs[group * chunks : (group + 1) * chunks]
        for n in range(2 * len(steps)):
            total = terms[0][n]
            for term in terms[1:]:
                total = total + term[n].astype(F32)
            first, second = slot(n % 2, steps[n // 2])
            out_ref[first, second] = total.astype(BF16)


def vmem_specs(count):
    return [pl.BlockSpec(memory_space=pltpu.VMEM)] * count


def shaped(dtype, *shape):
    return jax.ShapeDtypeStruct(shape, dtype)


def kernel(body, outs, operands, spaces=(), scratch=(), flops=0):
    spaces = list(spaces) + [pltpu.VMEM] * (len(operands) - len(spaces))
    return pl.pallas_call(
        body,
        out_shape=outs,
        in_specs=[pl.BlockSpec(memory_space=space) for space in spaces],
        out_specs=vmem_specs(len(outs)),
        scratch_shapes=list(scratch),
        compiler_params=pltpu.CompilerParams(vmem_limit_bytes=24 * 1024 * 1024),
        cost_estimate=pl.CostEstimate(flops=flops, bytes_accessed=1 << 20, transcendentals=0),
    )(*operands)


def shards(amplitudes, vectors, tile_mask, pair_mask):
    firsts, seconds, slab, _ = amplitudes.shape
    pairs = firsts * seconds
    virt, chips, cores = lax.axis_size("virt"), lax.axis_size("occi"), lax.axis_size("occj")
    rows = slab // virt
    chunks = virt // 2
    depth = 2 * vectors.shape[0] * slab
    turned_mask = jnp.transpose(tile_mask, (0, 2, 3, 1))
    gate = shaped(F32, pairs, 8, slab)
    arranged = [shaped(BF16, depth // 2, slab), shaped(BF16, depth // 4, slab)]
    turn = functools.partial(turn_kernel, chunks)

    def parts(count):
        return [shaped(F32 if chunk == 0 else BF16, count, rows, slab) for chunk in range(chunks)]

    def inner(count):
        return pltpu.VMEM((count * chunks * rows, depth), BF16)

    def sent(part):
        return [part[0]] + [swap_virt(part[chunk], chunk) for chunk in range(1, chunks)]

    def work(count):
        return 2 * count * depth * slab * slab

    near = swap_virt(vectors, chunks)
    if (firsts, seconds, chips, cores) == (2, CHIPS, CHIPS, 2):
        half_blocks = shaped(BF16, CHIPS, slab, slab)
        same, cross, gates = kernel(
            mask_split_kernel,
            [half_blocks, half_blocks, gate],
            [
                pltpu.with_memory_space_constraint(array, pltpu.HBM)
                for array in (turned_mask, pair_mask, amplitudes)
            ],
            spaces=[pltpu.HBM] * 3,
            scratch=[
                pltpu.SMEM(turned_mask.shape, jnp.int32),
                pltpu.SMEM(pair_mask.shape, jnp.int32),
                pltpu.SemaphoreType.DMA((pairs + 2,)),
            ],
        )
        other = swap_core(cross)
        packed = kernel(pack_kernel, [shaped(BF16, 2, slab, slab)] * (CHIPS - 1), (same, other))
        got = {step: swap_chip(block, step) for step, block in zip(STEPS, packed)}
        got[0] = other
        ready = kernel(turn, arranged, (vectors,)) + kernel(turn, arranged, (near,))
        finished = []
        for steps in GROUPS:
            part = kernel(
                functools.partial(group_kernel, chunks, steps),
                parts(2 * len(steps)),
                (*ready, gates, same, cross, *[got[step] for step in steps]),
                scratch=[inner(2 * len(steps))],
                flops=work(2 * len(steps)),
            )
            finished += sent(part)
        (out,) = kernel(
            functools.partial(finish_kernel, GROUPS, chunks),
            [shaped(BF16, firsts, seconds, rows, slab)],
            finished,
        )
        return out
    kept, gates = kernel(
        mask_whole_kernel,
        [shaped(BF16, pairs, slab, slab), gate],
        (turned_mask, pair_mask, amplitudes),
        spaces=[pltpu.SMEM] * 2,
    )
    partner = lax.all_to_all(kept, ("occj", "occi"), split_axis=0, concat_axis=0, tiled=True)
    ready = kernel(turn, arranged, (vectors,)) + kernel(turn, arranged, (near,))
    part = sent(
        kernel(whole_kernel, parts(pairs), (*ready, gates, kept, partner), scratch=[inner(2)], flops=work(pairs))
    )
    summed = part[0]
    for term in part[1:]:
        summed = summed + term.astype(F32)
    return summed.reshape(firsts, seconds, rows, slab).astype(BF16)


def solution(mesh):
    placed = (
        P("occi", "occj", None, None),
        P("virt", None, None),
        P("occi", "occj", None, None),
        P("occi", "occj"),
    )
    return jax.shard_map(
        shards,
        mesh=mesh,
        in_specs=placed,
        out_specs=P("occi", "occj", "virt", None),
        check_vma=False,
    )
```

```python
import functools

import jax
import jax.numpy as jnp
from jax import lax
from jax.experimental import pallas as pl
from jax.experimental.pallas import tpu as pltpu
from jax.sharding import PartitionSpec as P

TILE = 64
SLAB_TILES = 2
CHIPS = 4
STEPS = (3, 1, 2)
ORDER = (0, 3, 1, 2)
BF16 = jnp.bfloat16
F32 = jnp.float32


def swap_virt(array, step):
    return lax.ppermute(array, "virt", [(d, d ^ step) for d in range(lax.axis_size("virt"))])


def swap_both(array, step):
    size = lax.axis_size("virt")
    moves = [(c * size + d, (1 - c) * size + (d ^ step)) for c in range(2) for d in range(size)]
    return lax.ppermute(array, ("occj", "virt"), moves)


def swap_core(array):
    return lax.ppermute(array, "occj", [(0, 1), (1, 0)])


def swap_chip(array, step):
    return lax.ppermute(array, "occi", [(d, d ^ step) for d in range(lax.axis_size("occi"))])


def slot(kind, step):
    first = lax.axis_index("occj") if kind == 0 else 1 - lax.axis_index("occj")
    return first, lax.axis_index("occi") ^ step


def keep_rows(mask_ref, first, second, half):
    lane = lax.broadcasted_iota(jnp.int32, (1, SLAB_TILES * TILE), 1) // TILE
    keep = jnp.zeros(lane.shape, F32)
    for tile in range(SLAB_TILES):
        keep = jnp.where(lane == tile, mask_ref[first, half, tile, second].astype(F32), keep)
    return jnp.broadcast_to(keep, (TILE, SLAB_TILES * TILE)).astype(BF16)


def mask_split_kernel(mask_hbm, pair_hbm, amp_hbm, *refs):
    kept_refs, (cross_ref, gate_ref, mask_ref, pair_ref, sems) = refs[:CHIPS], refs[CHIPS:]
    copies = [
        pltpu.make_async_copy(mask_hbm, mask_ref, sems.at[0]),
        pltpu.make_async_copy(pair_hbm, pair_ref, sems.at[1]),
    ]
    blocks = []
    for step in STEPS + (0,):
        for kind in range(2):
            first, second = slot(kind, step)
            target = kept_refs[step].at[kind]
            copies.append(pltpu.make_async_copy(amp_hbm.at[first, second], target, sems.at[len(copies)]))
            blocks.append((first, second, target, kind, step, copies[-1]))
    for copy in copies:
        copy.start()
    copies[0].wait()
    copies[1].wait()
    for first, second, target, kind, step, copy in blocks:
        gate_ref[kind * CHIPS + step] = jnp.full(gate_ref.shape[1:], pair_ref[first, second].astype(F32))
        keeps = [keep_rows(mask_ref, first, second, half) for half in range(SLAB_TILES)]
        copy.wait()
        for half, keep in enumerate(keeps):
            part = slice(half * TILE, (half + 1) * TILE)
            kept = target[part] * keep
            target[part] = kept
            if kind:
                cross_ref[step, part] = kept


def mask_whole_kernel(mask_ref, pair_ref, amp_ref, kept_ref, gate_ref):
    seconds = amp_ref.shape[1]

    def one(block, carry):
        first, second = block // seconds, block % seconds
        for half in range(SLAB_TILES):
            part = slice(half * TILE, (half + 1) * TILE)
            kept_ref[block, part] = amp_ref[first, second, part] * keep_rows(mask_ref, first, second, half)
        gate_ref[block] = jnp.full(gate_ref.shape[1:], pair_ref[first, second].astype(F32))
        return carry

    lax.fori_loop(0, kept_ref.shape[0], one, 0)


def turn_kernel(chunks, vec_ref, turned_ref, left_ref):
    vectors, slab, _ = vec_ref.shape
    rows = left_ref.shape[0] // (vectors * chunks)
    me = lax.axis_index("virt")
    for q in range(vectors):
        turned_ref[q * slab : (q + 1) * slab] = vec_ref[q].astype(F32).T.astype(BF16)
        for chunk in range(chunks):
            start = pl.multiple_of((me ^ (2 * chunk)) * rows, rows)
            low = (q * chunks + chunk) * rows
            left_ref[low : low + rows] = vec_ref[q, pl.ds(start, rows), :]


def products(ready, inner_ref, sources, outs):
    turned_refs, left_refs = ready[::2], ready[1::2]
    slab = turned_refs[0].shape[1]
    depth = turned_refs[0].shape[0]
    vectors = depth // slab
    height = left_refs[0].shape[0] // vectors
    rows = height // len(outs[0])
    for base in range(0, len(sources), 2):
        both = [
            (kept.astype(F32) + partner.astype(F32).T).astype(BF16)
            for kept, partner in sources[base : base + 2]
        ]
        right = jnp.concatenate(both, axis=1)
        for side, left_ref in enumerate(left_refs):
            inner = jnp.dot(left_ref[...], right, preferred_element_type=F32).astype(BF16)
            for n in range(len(both)):
                for q in range(vectors):
                    at = side * depth + q * slab
                    inner_ref[(base + n) * height : (base + n + 1) * height, at : at + slab] = inner[
                        q * height : (q + 1) * height, n * slab : (n + 1) * slab
                    ]
    half = sum(
        jnp.dot(inner_ref[:, side * depth : (side + 1) * depth], turned_ref[...], preferred_element_type=F32)
        for side, turned_ref in enumerate(turned_refs)
    )
    for n, targets in enumerate(outs):
        for chunk, (ref, index) in enumerate(targets):
            start = n * height + chunk * rows
            ref[index] = half[start : start + rows].astype(ref.dtype)


def first_kernel(*refs):
    ready, (kept_ref, far_ref, got_ref, beside_ref), outs = refs[:4], refs[4:8], refs[8:]
    own_ref, lent_ref, send_ref, inner_ref = outs
    sources = [
        (kept_ref[0], kept_ref[0]),
        (far_ref[0], got_ref[0]),
        (beside_ref[0], kept_ref[1]),
        (beside_ref[ORDER[1]], got_ref[1]),
    ]
    targets = [[(ref, n), (send_ref, at + n)] for at, ref in ((0, own_ref), (2, lent_ref)) for n in range(2)]
    products(ready, inner_ref, sources, targets)


def second_kernel(*refs):
    ready, kept_refs, got_refs, (beside_ref, lent_in, send_in) = refs[:4], refs[4:6], refs[6:8], refs[8:11]
    own_ref, lent_ref, same_ref, cross_ref, inner_ref = refs[11:]
    sources = [(kept[0], got[0]) for kept, got in zip(kept_refs, got_refs)]
    sources += [(beside_ref[step], got[1]) for step, got in zip(ORDER[2:], got_refs)]
    targets = [[(own_ref, n), (same_ref, 2 + n)] for n in range(2)]
    targets += [[(lent_ref, 2 + n), (cross_ref, 2 + n)] for n in range(2)]
    lent_ref[:2] = lent_in[...]
    same_ref[:2] = send_in[:2]
    cross_ref[:2] = send_in[2:]
    products(ready, inner_ref, sources, targets)


def whole_kernel(*refs):
    ready, (kept_ref, partner_ref), part_refs, inner_ref = refs[:4], refs[4:6], refs[6:-1], refs[-1]

    def two(g, carry):
        pairs = [2 * g, 2 * g + 1]
        sources = [(kept_ref[k], partner_ref[k]) for k in pairs]
        products(ready, inner_ref, sources, [[(ref, k) for ref in part_refs] for k in pairs])
        return carry

    lax.fori_loop(0, kept_ref.shape[0] // 2, two, 0)


def finish_kernel(first_ref, second_ref, same_ref, cross_ref, lent_ref, gate_ref, out_ref):
    for n, step in enumerate(ORDER):
        own = first_ref[n] if n < 2 else second_ref[n - 2]
        totals = own + same_ref[n].astype(F32), lent_ref[n].astype(F32) + cross_ref[n].astype(F32)
        for kind, total in enumerate(totals):
            first, second = slot(kind, step)
            gate = gate_ref[kind * CHIPS + step, :1]
            out_ref[first, second] = (total * gate).astype(BF16)


def vmem_specs(count):
    return [pl.BlockSpec(memory_space=pltpu.VMEM)] * count


def shaped(dtype, *shape):
    return jax.ShapeDtypeStruct(shape, dtype)


def kernel(body, outs, operands, spaces=(), scratch=(), flops=0):
    spaces = list(spaces) + [pltpu.VMEM] * (len(operands) - len(spaces))
    return pl.pallas_call(
        body,
        out_shape=outs,
        in_specs=[pl.BlockSpec(memory_space=space) for space in spaces],
        out_specs=vmem_specs(len(outs)),
        scratch_shapes=list(scratch),
        compiler_params=pltpu.CompilerParams(vmem_limit_bytes=24 * 1024 * 1024),
        cost_estimate=pl.CostEstimate(flops=flops, bytes_accessed=1 << 20, transcendentals=0),
    )(*operands)


def shards(amplitudes, vectors, tile_mask, pair_mask):
    firsts, seconds, slab, _ = amplitudes.shape
    pairs = firsts * seconds
    virt, chips, cores = lax.axis_size("virt"), lax.axis_size("occi"), lax.axis_size("occj")
    rows = slab // virt
    chunks = virt // 2
    depth = 2 * vectors.shape[0] * slab
    turned_mask = jnp.transpose(tile_mask, (0, 2, 3, 1))
    gate = shaped(F32, pairs, 8, slab)
    arranged = [shaped(BF16, depth // 2, slab), shaped(BF16, depth // 4, slab)]
    turn = functools.partial(turn_kernel, chunks)

    def parts(count):
        return [shaped(F32 if chunk == 0 else BF16, count, rows, slab) for chunk in range(chunks)]

    def inner(count):
        return pltpu.VMEM((count * chunks * rows, depth), BF16)

    def sent(part):
        return [part[0]] + [swap_virt(part[chunk], 2 * chunk) for chunk in range(1, chunks)]

    def work(count):
        return 2 * count * depth * slab * slab

    near = swap_virt(vectors, 1)
    if (firsts, seconds, chips, cores, virt) == (2, CHIPS, CHIPS, 2, 4):
        *kept, cross, gates = kernel(
            mask_split_kernel,
            [shaped(BF16, 2, slab, slab)] * CHIPS + [shaped(BF16, CHIPS, slab, slab), gate],
            [
                pltpu.with_memory_space_constraint(array, pltpu.HBM)
                for array in (turned_mask, pair_mask, amplitudes)
            ],
            spaces=[pltpu.HBM] * 3,
            scratch=[
                pltpu.SMEM(turned_mask.shape, jnp.int32),
                pltpu.SMEM(pair_mask.shape, jnp.int32),
                pltpu.SemaphoreType.DMA((pairs + 2,)),
            ],
        )
        got = {step: swap_chip(kept[step], step) for step in STEPS}
        beside = swap_core(cross)
        ready = kernel(turn, arranged, (vectors,)) + kernel(turn, arranged, (near,))
        _, far, *rest = ORDER
        own_first, lent, sending = kernel(
            first_kernel,
            [shaped(F32, 2, rows, slab), shaped(BF16, 2, rows, slab), shaped(BF16, 4, rows, slab)],
            (*ready, kept[0], kept[far], got[far], beside),
            scratch=[inner(4)],
            flops=work(4),
        )
        own_second, lent, same, crossing = kernel(
            second_kernel,
            [shaped(F32, 2, rows, slab)] + [shaped(BF16, 4, rows, slab)] * 3,
            (*ready, *[kept[step] for step in rest], *[got[step] for step in rest], beside, lent, sending),
            scratch=[inner(4)],
            flops=work(4),
        )
        operands = (own_first, own_second, swap_virt(same, 2), swap_both(crossing, 2), swap_core(lent), gates)
        (out,) = kernel(finish_kernel, [shaped(BF16, firsts, seconds, rows, slab)], operands)
        return out
    kept, gates = kernel(
        mask_whole_kernel,
        [shaped(BF16, pairs, slab, slab), gate],
        (turned_mask, pair_mask, amplitudes),
        spaces=[pltpu.SMEM] * 2,
    )
    partner = lax.all_to_all(kept, ("occj", "occi"), split_axis=0, concat_axis=0, tiled=True)
    ready = kernel(turn, arranged, (vectors,)) + kernel(turn, arranged, (near,))
    part = sent(
        kernel(whole_kernel, parts(pairs), (*ready, kept, partner), scratch=[inner(2)], flops=work(pairs))
    )
    summed = part[0]
    for term in part[1:]:
        summed = summed + term.astype(F32)
    return (summed * gates[:, :1]).reshape(firsts, seconds, rows, slab).astype(BF16)


def solution(mesh):
    placed = (
        P("occi", "occj", None, None),
        P("virt", None, None),
        P("occi", "occj", None, None),
        P("occi", "occj"),
    )
    return jax.shard_map(
        shards,
        mesh=mesh,
        in_specs=placed,
        out_specs=P("occi", "occj", "virt", None),
        check_vma=False,
    )
```

```python
import functools

import jax
import jax.numpy as jnp
from jax import lax
from jax.experimental import pallas as pl
from jax.experimental.pallas import tpu as pltpu
from jax.sharding import PartitionSpec as P

TILE = 64
SLAB_TILES = 2
CHIPS = 4
STEPS = (3, 1, 2)
ORDER = (0, 3, 1, 2)
BF16 = jnp.bfloat16
F32 = jnp.float32


def swap_virt(array, step):
    return lax.ppermute(array, "virt", [(d, d ^ step) for d in range(lax.axis_size("virt"))])


def swap_core(array):
    return lax.ppermute(array, "occj", [(0, 1), (1, 0)])


def swap_chip(array, step):
    return lax.ppermute(array, "occi", [(d, d ^ step) for d in range(lax.axis_size("occi"))])


def slot(kind, step):
    first = lax.axis_index("occj") if kind == 0 else 1 - lax.axis_index("occj")
    return first, lax.axis_index("occi") ^ step


def keep_rows(mask_ref, first, second, half):
    lane = lax.broadcasted_iota(jnp.int32, (1, SLAB_TILES * TILE), 1) // TILE
    keep = jnp.zeros(lane.shape, F32)
    for tile in range(SLAB_TILES):
        keep = jnp.where(lane == tile, mask_ref[first, half, tile, second].astype(F32), keep)
    return jnp.broadcast_to(keep, (TILE, SLAB_TILES * TILE)).astype(BF16)


def mask_split_kernel(mask_hbm, pair_hbm, amp_hbm, *refs):
    kept_refs, (cross_ref, gate_ref, mask_ref, pair_ref, sems) = refs[:CHIPS], refs[CHIPS:]
    copies = [
        pltpu.make_async_copy(mask_hbm, mask_ref, sems.at[0]),
        pltpu.make_async_copy(pair_hbm, pair_ref, sems.at[1]),
    ]
    blocks = []
    for step in STEPS + (0,):
        for kind in range(2):
            first, second = slot(kind, step)
            target = kept_refs[step].at[kind]
            copies.append(pltpu.make_async_copy(amp_hbm.at[first, second], target, sems.at[len(copies)]))
            blocks.append((first, second, target, kind, step, copies[-1]))
    for copy in copies:
        copy.start()
    copies[0].wait()
    copies[1].wait()
    for first, second, target, kind, step, copy in blocks:
        gate_ref[kind * CHIPS + step] = jnp.full(gate_ref.shape[1:], pair_ref[first, second].astype(F32))
        keeps = [keep_rows(mask_ref, first, second, half) for half in range(SLAB_TILES)]
        copy.wait()
        for half, keep in enumerate(keeps):
            part = slice(half * TILE, (half + 1) * TILE)
            kept = target[part] * keep
            target[part] = kept
            if kind:
                cross_ref[step, part] = kept


def mask_whole_kernel(mask_ref, pair_ref, amp_ref, kept_ref, gate_ref):
    seconds = amp_ref.shape[1]

    def one(block, carry):
        first, second = block // seconds, block % seconds
        for half in range(SLAB_TILES):
            part = slice(half * TILE, (half + 1) * TILE)
            kept_ref[block, part] = amp_ref[first, second, part] * keep_rows(mask_ref, first, second, half)
        gate_ref[block] = jnp.full(gate_ref.shape[1:], pair_ref[first, second].astype(F32))
        return carry

    lax.fori_loop(0, kept_ref.shape[0], one, 0)


def turn_kernel(chunks, *refs):
    vec_refs, turned_ref, left_ref = refs[:-2], refs[-2], refs[-1]
    slab = turned_ref.shape[1]
    rows = slab * left_ref.shape[0] // (turned_ref.shape[0] * chunks)
    me = lax.axis_index("virt")
    at, low = 0, 0
    for vec_ref in vec_refs:
        for q in range(vec_ref.shape[0]):
            turned_ref[at : at + slab] = vec_ref[q].astype(F32).T.astype(BF16)
            at += slab
            for chunk in range(chunks):
                start = pl.multiple_of((me ^ (2 * chunk)) * rows, rows)
                left_ref[low : low + rows] = vec_ref[q, pl.ds(start, rows), :]
                low += rows


def products(ready, inner_ref, sources, outs):
    turned_refs, left_refs = ready[::2], ready[1::2]
    slab = turned_refs[0].shape[1]
    depth = turned_refs[0].shape[0]
    vectors = depth // slab
    height = left_refs[0].shape[0] // vectors
    rows = height // len(outs[0])
    for base in range(0, len(sources), 2):
        both = [
            (kept.astype(F32) + partner.astype(F32).T).astype(BF16)
            for kept, partner in sources[base : base + 2]
        ]
        right = jnp.concatenate(both, axis=1)
        for side, left_ref in enumerate(left_refs):
            inner = jnp.dot(left_ref[...], right, preferred_element_type=F32).astype(BF16)
            for n in range(len(both)):
                for q in range(vectors):
                    at = side * depth + q * slab
                    inner_ref[(base + n) * height : (base + n + 1) * height, at : at + slab] = inner[
                        q * height : (q + 1) * height, n * slab : (n + 1) * slab
                    ]
    half = sum(
        jnp.dot(inner_ref[:, side * depth : (side + 1) * depth], turned_ref[...], preferred_element_type=F32)
        for side, turned_ref in enumerate(turned_refs)
    )
    for n, targets in enumerate(outs):
        for chunk, (ref, index) in enumerate(targets):
            start = n * height + chunk * rows
            ref[index] = half[start : start + rows].astype(ref.dtype)


def first_kernel(*refs):
    ready, (kept_ref, far_ref, got_ref, beside_ref), outs = refs[:4], refs[4:8], refs[8:]
    own_ref, send_ref, lent_ref, inner_ref = outs
    sources = [
        (kept_ref[0], kept_ref[0]),
        (kept_ref[1], beside_ref[0]),
        (far_ref[0], got_ref[0]),
        (beside_ref[ORDER[1]], got_ref[1]),
    ]
    targets = [[(own_ref, n), (send_ref, n)] for n in range(3)] + [[(lent_ref.at[0], 0), (lent_ref.at[1], 0)]]
    products(ready, inner_ref, sources, targets)


def cross_kernel(*refs):
    ready, got_refs, (beside_ref, lent_in, lent_ref, inner_ref) = refs[:4], refs[4:6], refs[6:]
    lent_ref[:, :1] = lent_in[...]
    sources = [(beside_ref[step], got[1]) for step, got in zip(ORDER[2:], got_refs)]
    targets = [[(lent_ref.at[0], 1 + n), (lent_ref.at[1], 1 + n)] for n in range(2)]
    products(ready, inner_ref, sources, targets)


def same_kernel(*refs):
    ready, kept_refs, got_refs, (own_ref, send_ref, inner_ref) = refs[:4], refs[4:6], refs[6:8], refs[8:]
    sources = [(kept[0], got[0]) for kept, got in zip(kept_refs, got_refs)]
    products(ready, inner_ref, sources, [[(own_ref, n), (send_ref, n)] for n in range(2)])


def join_kernel(first_ref, second_ref, back_ref, out_ref):
    out_ref[:3] = first_ref[...]
    out_ref[3:5] = second_ref[...]
    out_ref[5:] = back_ref[1]


def whole_kernel(*refs):
    ready, (kept_ref, partner_ref), part_refs, inner_ref = refs[:4], refs[4:6], refs[6:-1], refs[-1]

    def two(g, carry):
        pairs = [2 * g, 2 * g + 1]
        sources = [(kept_ref[k], partner_ref[k]) for k in pairs]
        products(ready, inner_ref, sources, [[(ref, k) for ref in part_refs] for k in pairs])
        return carry

    lax.fori_loop(0, kept_ref.shape[0] // 2, two, 0)


def finish_kernel(first_ref, second_ref, back_ref, got_ref, gate_ref, out_ref):
    places = [(0, 0), (1, 0)] + [(0, step) for step in ORDER[1:]] + [(1, step) for step in ORDER[1:]]
    for n, (kind, step) in enumerate(places):
        own = first_ref[n] if n < 3 else second_ref[n - 3] if n < 5 else back_ref[0, n - 5].astype(F32)
        first, second = slot(kind, step)
        gate = gate_ref[kind * CHIPS + step, :1]
        out_ref[first, second] = ((own + got_ref[n].astype(F32)) * gate).astype(BF16)


def vmem_specs(count):
    return [pl.BlockSpec(memory_space=pltpu.VMEM)] * count


def shaped(dtype, *shape):
    return jax.ShapeDtypeStruct(shape, dtype)


def kernel(body, outs, operands, spaces=(), scratch=(), flops=0):
    spaces = list(spaces) + [pltpu.VMEM] * (len(operands) - len(spaces))
    return pl.pallas_call(
        body,
        out_shape=outs,
        in_specs=[pl.BlockSpec(memory_space=space) for space in spaces],
        out_specs=vmem_specs(len(outs)),
        scratch_shapes=list(scratch),
        compiler_params=pltpu.CompilerParams(vmem_limit_bytes=24 * 1024 * 1024),
        cost_estimate=pl.CostEstimate(flops=flops, bytes_accessed=1 << 20, transcendentals=0),
    )(*operands)


def shards(amplitudes, vectors, tile_mask, pair_mask):
    firsts, seconds, slab, _ = amplitudes.shape
    pairs = firsts * seconds
    virt, chips, cores = lax.axis_size("virt"), lax.axis_size("occi"), lax.axis_size("occj")
    rows = slab // virt
    chunks = virt // 2
    depth = 2 * vectors.shape[0] * slab
    turned_mask = jnp.transpose(tile_mask, (0, 2, 3, 1))
    gate = shaped(F32, pairs, 8, slab)
    arranged = [shaped(BF16, depth // 2, slab), shaped(BF16, depth // 4, slab)]
    turn = functools.partial(turn_kernel, chunks)

    def parts(count):
        return [shaped(F32 if chunk == 0 else BF16, count, rows, slab) for chunk in range(chunks)]

    def inner(count):
        return pltpu.VMEM((count * chunks * rows, depth), BF16)

    def sent(part):
        return [part[0]] + [swap_virt(part[chunk], 2 * chunk) for chunk in range(1, chunks)]

    def work(count):
        return 2 * count * depth * slab * slab

    if (firsts, seconds, chips, cores, virt) == (2, CHIPS, CHIPS, 2, 4):
        *kept, cross, gates = kernel(
            mask_split_kernel,
            [shaped(BF16, 2, slab, slab)] * CHIPS + [shaped(BF16, CHIPS, slab, slab), gate],
            [
                pltpu.with_memory_space_constraint(array, pltpu.HBM)
                for array in (turned_mask, pair_mask, amplitudes)
            ],
            spaces=[pltpu.HBM] * 3,
            scratch=[
                pltpu.SMEM(turned_mask.shape, jnp.int32),
                pltpu.SMEM(pair_mask.shape, jnp.int32),
                pltpu.SemaphoreType.DMA((pairs + 2,)),
            ],
        )
        near = swap_virt(vectors, 1)
        got = {step: swap_chip(kept[step], step) for step in STEPS}
        beside = swap_core(cross)
        ready = kernel(turn, arranged, (vectors,)) + kernel(turn, arranged, (near,))
        _, far, *rest = ORDER
        arrived = [got[step] for step in rest]
        own_first, send_first, lent = kernel(
            first_kernel,
            [shaped(F32, 3, rows, slab), shaped(BF16, 3, rows, slab), shaped(BF16, 2, 1, rows, slab)],
            (*ready, kept[0], kept[far], got[far], beside),
            scratch=[inner(4)],
            flops=work(4),
        )
        (lent,) = kernel(
            cross_kernel,
            [shaped(BF16, 2, 3, rows, slab)],
            (*ready, *arrived, beside, lent),
            scratch=[inner(2)],
            flops=work(2),
        )
        back = swap_core(lent)
        own_second, send_second = kernel(
            same_kernel,
            [shaped(F32, 2, rows, slab), shaped(BF16, 2, rows, slab)],
            (*ready, *[kept[step] for step in rest], *arrived),
            scratch=[inner(2)],
            flops=work(2),
        )
        (sending,) = kernel(join_kernel, [shaped(BF16, pairs, rows, slab)], (send_first, send_second, back))
        operands = (own_first, own_second, back, swap_virt(sending, 2), gates)
        (out,) = kernel(finish_kernel, [shaped(BF16, firsts, seconds, rows, slab)], operands)
        return out
    kept, gates = kernel(
        mask_whole_kernel,
        [shaped(BF16, pairs, slab, slab), gate],
        (turned_mask, pair_mask, amplitudes),
        spaces=[pltpu.SMEM] * 2,
    )
    partner = lax.all_to_all(kept, ("occj", "occi"), split_axis=0, concat_axis=0, tiled=True)
    ready = kernel(turn, arranged, (vectors,)) + kernel(turn, arranged, (swap_virt(vectors, 1),))
    part = sent(
        kernel(whole_kernel, parts(pairs), (*ready, kept, partner), scratch=[inner(2)], flops=work(pairs))
    )
    summed = part[0]
    for term in part[1:]:
        summed = summed + term.astype(F32)
    return (summed * gates[:, :1]).reshape(firsts, seconds, rows, slab).astype(BF16)


def solution(mesh):
    placed = (
        P("occi", "occj", None, None),
        P("virt", None, None),
        P("occi", "occj", None, None),
        P("occi", "occj"),
    )
    return jax.shard_map(
        shards,
        mesh=mesh,
        in_specs=placed,
        out_specs=P("occi", "occj", "virt", None),
        check_vma=False,
    )
```

```python
import functools

import jax
import jax.numpy as jnp
from jax import lax
from jax.experimental import pallas as pl
from jax.experimental.pallas import tpu as pltpu
from jax.sharding import PartitionSpec as P

TILE = 64
SLAB_TILES = 2
CHIPS = 4
STEPS = (3, 1, 2)
ORDER = (0, 3, 1, 2)
BF16 = jnp.bfloat16
F32 = jnp.float32


def swap_virt(array, step):
    return lax.ppermute(array, "virt", [(d, d ^ step) for d in range(lax.axis_size("virt"))])


def swap_both(array, step):
    size = lax.axis_size("virt")
    moves = [(c * size + d, (1 - c) * size + (d ^ step)) for c in range(2) for d in range(size)]
    return lax.ppermute(array, ("occj", "virt"), moves)


def swap_core(array):
    return lax.ppermute(array, "occj", [(0, 1), (1, 0)])


def swap_chip(array, step):
    return lax.ppermute(array, "occi", [(d, d ^ step) for d in range(lax.axis_size("occi"))])


def slot(kind, step):
    first = lax.axis_index("occj") if kind == 0 else 1 - lax.axis_index("occj")
    return first, lax.axis_index("occi") ^ step


def keep_rows(mask_ref, first, second, half):
    lane = lax.broadcasted_iota(jnp.int32, (1, SLAB_TILES * TILE), 1) // TILE
    keep = jnp.zeros(lane.shape, F32)
    for tile in range(SLAB_TILES):
        keep = jnp.where(lane == tile, mask_ref[first, half, tile, second].astype(F32), keep)
    return jnp.broadcast_to(keep, (TILE, SLAB_TILES * TILE)).astype(BF16)


def mask_split_kernel(mask_hbm, pair_hbm, amp_hbm, *refs):
    kept_refs, (cross_ref, gate_ref, mask_ref, pair_ref, sems) = refs[:CHIPS], refs[CHIPS:]
    copies = [
        pltpu.make_async_copy(mask_hbm, mask_ref, sems.at[0]),
        pltpu.make_async_copy(pair_hbm, pair_ref, sems.at[1]),
    ]
    blocks = []
    for step in STEPS + (0,):
        for kind in range(2):
            first, second = slot(kind, step)
            target = kept_refs[step].at[kind]
            copies.append(pltpu.make_async_copy(amp_hbm.at[first, second], target, sems.at[len(copies)]))
            blocks.append((first, second, target, kind, step, copies[-1]))
    for copy in copies:
        copy.start()
    copies[0].wait()
    copies[1].wait()
    for first, second, target, kind, step, copy in blocks:
        gate_ref[kind * CHIPS + step] = jnp.full(gate_ref.shape[1:], pair_ref[first, second].astype(F32))
        keeps = [keep_rows(mask_ref, first, second, half) for half in range(SLAB_TILES)]
        copy.wait()
        for half, keep in enumerate(keeps):
            part = slice(half * TILE, (half + 1) * TILE)
            kept = target[part] * keep
            target[part] = kept
            if kind:
                cross_ref[step, part] = kept


def mask_whole_kernel(mask_ref, pair_ref, amp_ref, kept_ref, gate_ref):
    seconds = amp_ref.shape[1]

    def one(block, carry):
        first, second = block // seconds, block % seconds
        for half in range(SLAB_TILES):
            part = slice(half * TILE, (half + 1) * TILE)
            kept_ref[block, part] = amp_ref[first, second, part] * keep_rows(mask_ref, first, second, half)
        gate_ref[block] = jnp.full(gate_ref.shape[1:], pair_ref[first, second].astype(F32))
        return carry

    lax.fori_loop(0, kept_ref.shape[0], one, 0)


def turn_kernel(chunks, vec_ref, turned_ref, left_ref):
    vectors, slab, _ = vec_ref.shape
    rows = left_ref.shape[0] // (vectors * chunks)
    me = lax.axis_index("virt")
    for q in range(vectors):
        turned_ref[q * slab : (q + 1) * slab] = vec_ref[q].astype(F32).T.astype(BF16)
        for chunk in range(chunks):
            start = pl.multiple_of((me ^ (2 * chunk)) * rows, rows)
            low = (q * chunks + chunk) * rows
            left_ref[low : low + rows] = vec_ref[q, pl.ds(start, rows), :]


def products(ready, inner_ref, sources, outs):
    turned_refs, left_refs = ready[::2], ready[1::2]
    slab = turned_refs[0].shape[1]
    depth = turned_refs[0].shape[0]
    vectors = depth // slab
    height = left_refs[0].shape[0] // vectors
    rows = height // len(outs[0])
    for base in range(0, len(sources), 2):
        both = [
            (kept.astype(F32) + partner.astype(F32).T).astype(BF16)
            for kept, partner in sources[base : base + 2]
        ]
        right = jnp.concatenate(both, axis=1)
        for side, left_ref in enumerate(left_refs):
            inner = jnp.dot(left_ref[...], right, preferred_element_type=F32).astype(BF16)
            for n in range(len(both)):
                for q in range(vectors):
                    at = side * depth + q * slab
                    inner_ref[(base + n) * height : (base + n + 1) * height, at : at + slab] = inner[
                        q * height : (q + 1) * height, n * slab : (n + 1) * slab
                    ]
    half = sum(
        jnp.dot(inner_ref[:, side * depth : (side + 1) * depth], turned_ref[...], preferred_element_type=F32)
        for side, turned_ref in enumerate(turned_refs)
    )
    for n, targets in enumerate(outs):
        for chunk, (ref, index) in enumerate(targets):
            start = n * height + chunk * rows
            ref[index] = half[start : start + rows].astype(ref.dtype)


def first_kernel(*refs):
    ready, (kept_ref, far_ref, got_ref, beside_ref), outs = refs[:4], refs[4:8], refs[8:]
    own_ref, lent_ref, send_ref, inner_ref = outs
    sources = [
        (kept_ref[0], kept_ref[0]),
        (far_ref[0], got_ref[0]),
        (beside_ref[0], kept_ref[1]),
        (beside_ref[ORDER[1]], got_ref[1]),
    ]
    targets = [[(ref, n), (send_ref, at + n)] for at, ref in ((0, own_ref), (2, lent_ref)) for n in range(2)]
    products(ready, inner_ref, sources, targets)


def second_kernel(*refs):
    ready, kept_refs, got_refs, (beside_ref, lent_in, send_in) = refs[:4], refs[4:6], refs[6:8], refs[8:11]
    own_ref, lent_ref, same_ref, cross_ref, inner_ref = refs[11:]
    sources = [(kept[0], got[0]) for kept, got in zip(kept_refs, got_refs)]
    sources += [(beside_ref[step], got[1]) for step, got in zip(ORDER[2:], got_refs)]
    targets = [[(own_ref, n), (same_ref, 2 + n)] for n in range(2)]
    targets += [[(lent_ref, 2 + n), (cross_ref, 2 + n)] for n in range(2)]
    lent_ref[:2] = lent_in[...]
    same_ref[:2] = send_in[:2]
    cross_ref[:2] = send_in[2:]
    products(ready, inner_ref, sources, targets)


def whole_kernel(*refs):
    ready, (kept_ref, partner_ref), part_refs, inner_ref = refs[:4], refs[4:6], refs[6:-1], refs[-1]

    def two(g, carry):
        pairs = [2 * g, 2 * g + 1]
        sources = [(kept_ref[k], partner_ref[k]) for k in pairs]
        products(ready, inner_ref, sources, [[(ref, k) for ref in part_refs] for k in pairs])
        return carry

    lax.fori_loop(0, kept_ref.shape[0] // 2, two, 0)


def finish_kernel(first_ref, second_ref, cross_ref, same_ref, lent_ref, gate_ref, out_ref):
    for n, step in enumerate(ORDER):
        own = first_ref[n] if n < 2 else second_ref[n - 2]
        totals = own + same_ref[n].astype(F32), lent_ref[n].astype(F32) + cross_ref[n].astype(F32)
        for kind, total in enumerate(totals):
            first, second = slot(kind, step)
            gate = gate_ref[kind * CHIPS + step, :1]
            out_ref[first, second] = (total * gate).astype(BF16)


def vmem_specs(count):
    return [pl.BlockSpec(memory_space=pltpu.VMEM)] * count


def shaped(dtype, *shape):
    return jax.ShapeDtypeStruct(shape, dtype)


def kernel(body, outs, operands, spaces=(), scratch=(), flops=0):
    spaces = list(spaces) + [pltpu.VMEM] * (len(operands) - len(spaces))
    return pl.pallas_call(
        body,
        out_shape=outs,
        in_specs=[pl.BlockSpec(memory_space=space) for space in spaces],
        out_specs=vmem_specs(len(outs)),
        scratch_shapes=list(scratch),
        compiler_params=pltpu.CompilerParams(vmem_limit_bytes=24 * 1024 * 1024),
        cost_estimate=pl.CostEstimate(flops=flops, bytes_accessed=1 << 20, transcendentals=0),
    )(*operands)


def shards(amplitudes, vectors, tile_mask, pair_mask):
    firsts, seconds, slab, _ = amplitudes.shape
    pairs = firsts * seconds
    virt, chips, cores = lax.axis_size("virt"), lax.axis_size("occi"), lax.axis_size("occj")
    rows = slab // virt
    chunks = virt // 2
    depth = 2 * vectors.shape[0] * slab
    turned_mask = jnp.transpose(tile_mask, (0, 2, 3, 1))
    gate = shaped(F32, pairs, 8, slab)
    arranged = [shaped(BF16, depth // 2, slab), shaped(BF16, depth // 4, slab)]
    turn = functools.partial(turn_kernel, chunks)

    def parts(count):
        return [shaped(F32 if chunk == 0 else BF16, count, rows, slab) for chunk in range(chunks)]

    def inner(count):
        return pltpu.VMEM((count * chunks * rows, depth), BF16)

    def sent(part):
        return [part[0]] + [swap_virt(part[chunk], 2 * chunk) for chunk in range(1, chunks)]

    def work(count):
        return 2 * count * depth * slab * slab

    near = swap_virt(vectors, 1)
    if (firsts, seconds, chips, cores, virt) == (2, CHIPS, CHIPS, 2, 4):
        *kept, cross, gates = kernel(
            mask_split_kernel,
            [shaped(BF16, 2, slab, slab)] * CHIPS + [shaped(BF16, CHIPS, slab, slab), gate],
            [
                pltpu.with_memory_space_constraint(array, pltpu.HBM)
                for array in (turned_mask, pair_mask, amplitudes)
            ],
            spaces=[pltpu.HBM] * 3,
            scratch=[
                pltpu.SMEM(turned_mask.shape, jnp.int32),
                pltpu.SMEM(pair_mask.shape, jnp.int32),
                pltpu.SemaphoreType.DMA((pairs + 2,)),
            ],
        )
        got = {step: swap_chip(kept[step], step) for step in STEPS}
        beside = swap_core(cross)
        ready = kernel(turn, arranged, (vectors,)) + kernel(turn, arranged, (near,))
        _, far, *rest = ORDER
        own_first, lent, sending = kernel(
            first_kernel,
            [shaped(F32, 2, rows, slab), shaped(BF16, 2, rows, slab), shaped(BF16, 4, rows, slab)],
            (*ready, kept[0], kept[far], got[far], beside),
            scratch=[inner(4)],
            flops=work(4),
        )
        own_second, lent, same, crossing = kernel(
            second_kernel,
            [shaped(F32, 2, rows, slab)] + [shaped(BF16, 4, rows, slab)] * 3,
            (*ready, *[kept[step] for step in rest], *[got[step] for step in rest], beside, lent, sending),
            scratch=[inner(4)],
            flops=work(4),
        )
        operands = (own_first, own_second, swap_both(crossing, 2), swap_virt(same, 2), swap_core(lent), gates)
        (out,) = kernel(finish_kernel, [shaped(BF16, firsts, seconds, rows, slab)], operands)
        return out
    kept, gates = kernel(
        mask_whole_kernel,
        [shaped(BF16, pairs, slab, slab), gate],
        (turned_mask, pair_mask, amplitudes),
        spaces=[pltpu.SMEM] * 2,
    )
    partner = lax.all_to_all(kept, ("occj", "occi"), split_axis=0, concat_axis=0, tiled=True)
    ready = kernel(turn, arranged, (vectors,)) + kernel(turn, arranged, (near,))
    part = sent(
        kernel(whole_kernel, parts(pairs), (*ready, kept, partner), scratch=[inner(2)], flops=work(pairs))
    )
    summed = part[0]
    for term in part[1:]:
        summed = summed + term.astype(F32)
    return (summed * gates[:, :1]).reshape(firsts, seconds, rows, slab).astype(BF16)


def solution(mesh):
    placed = (
        P("occi", "occj", None, None),
        P("virt", None, None),
        P("occi", "occj", None, None),
        P("occi", "occj"),
    )
    return jax.shard_map(
        shards,
        mesh=mesh,
        in_specs=placed,
        out_specs=P("occi", "occj", "virt", None),
        check_vma=False,
    )
```

```python
import functools

import jax
import jax.numpy as jnp
from jax import lax
from jax.experimental import pallas as pl
from jax.experimental.pallas import tpu as pltpu
from jax.sharding import PartitionSpec as P

TILE = 64
SLAB_TILES = 2
CHIPS = 4
STEPS = (3, 1, 2)
ORDER = (0, 3, 1, 2)
BF16 = jnp.bfloat16
F32 = jnp.float32


def swap_virt(array, step):
    return lax.ppermute(array, "virt", [(d, d ^ step) for d in range(lax.axis_size("virt"))])


def swap_both(array, step):
    size = lax.axis_size("virt")
    moves = [(c * size + d, (1 - c) * size + (d ^ step)) for c in range(2) for d in range(size)]
    return lax.ppermute(array, ("occj", "virt"), moves)


def swap_core(array):
    return lax.ppermute(array, "occj", [(0, 1), (1, 0)])


def swap_chip(array, step):
    return lax.ppermute(array, "occi", [(d, d ^ step) for d in range(lax.axis_size("occi"))])


def slot(kind, step):
    first = lax.axis_index("occj") if kind == 0 else 1 - lax.axis_index("occj")
    return first, lax.axis_index("occi") ^ step


def keep_rows(mask_ref, first, second, half):
    lane = lax.broadcasted_iota(jnp.int32, (1, SLAB_TILES * TILE), 1) // TILE
    keep = jnp.zeros(lane.shape, F32)
    for tile in range(SLAB_TILES):
        keep = jnp.where(lane == tile, mask_ref[first, half, tile, second].astype(F32), keep)
    return jnp.broadcast_to(keep, (TILE, SLAB_TILES * TILE)).astype(BF16)


def mask_split_kernel(mask_hbm, pair_hbm, amp_hbm, *refs):
    kept_refs, (cross_ref, gate_ref, mask_ref, pair_ref, sems) = refs[:CHIPS], refs[CHIPS:]
    copies = [
        pltpu.make_async_copy(mask_hbm, mask_ref, sems.at[0]),
        pltpu.make_async_copy(pair_hbm, pair_ref, sems.at[1]),
    ]
    blocks = []
    for step in STEPS + (0,):
        for kind in range(2):
            first, second = slot(kind, step)
            target = kept_refs[step].at[kind]
            copies.append(pltpu.make_async_copy(amp_hbm.at[first, second], target, sems.at[len(copies)]))
            blocks.append((first, second, target, kind, step, copies[-1]))
    for copy in copies:
        copy.start()
    copies[0].wait()
    copies[1].wait()
    for first, second, target, kind, step, copy in blocks:
        gate_ref[kind * CHIPS + step] = jnp.full(gate_ref.shape[1:], pair_ref[first, second].astype(F32))
        keeps = [keep_rows(mask_ref, first, second, half) for half in range(SLAB_TILES)]
        copy.wait()
        for half, keep in enumerate(keeps):
            part = slice(half * TILE, (half + 1) * TILE)
            kept = target[part] * keep
            target[part] = kept
            if kind:
                cross_ref[step, part] = kept


def mask_whole_kernel(mask_ref, pair_ref, amp_ref, kept_ref, gate_ref):
    seconds = amp_ref.shape[1]

    def one(block, carry):
        first, second = block // seconds, block % seconds
        for half in range(SLAB_TILES):
            part = slice(half * TILE, (half + 1) * TILE)
            kept_ref[block, part] = amp_ref[first, second, part] * keep_rows(mask_ref, first, second, half)
        gate_ref[block] = jnp.full(gate_ref.shape[1:], pair_ref[first, second].astype(F32))
        return carry

    lax.fori_loop(0, kept_ref.shape[0], one, 0)


def turn_kernel(chunks, vec_ref, turned_ref, left_ref):
    vectors, slab, _ = vec_ref.shape
    rows = left_ref.shape[0] // (vectors * chunks)
    me = lax.axis_index("virt")
    for q in range(vectors):
        turned_ref[q * slab : (q + 1) * slab] = vec_ref[q].astype(F32).T.astype(BF16)
        for chunk in range(chunks):
            start = pl.multiple_of((me ^ (2 * chunk)) * rows, rows)
            low = (q * chunks + chunk) * rows
            left_ref[low : low + rows] = vec_ref[q, pl.ds(start, rows), :]


def near_kernel(chunks, both_hbm, turned_ref, left_ref, vec_ref, sems):
    count = vec_ref.shape[0]
    base = (1 - lax.axis_index("virt") % 2) * count
    copies = [pltpu.make_async_copy(both_hbm.at[base + q], vec_ref.at[q], sems.at[q]) for q in range(count)]
    for copy in copies:
        copy.start()
    for copy in copies:
        copy.wait()
    turn_kernel(chunks, vec_ref, turned_ref, left_ref)


def products(ready, inner_ref, sources, outs):
    turned_refs, left_refs = ready[::2], ready[1::2]
    slab = turned_refs[0].shape[1]
    depth = turned_refs[0].shape[0]
    vectors = depth // slab
    height = left_refs[0].shape[0] // vectors
    rows = height // len(outs[0])
    for base in range(0, len(sources), 2):
        both = [
            (kept.astype(F32) + partner.astype(F32).T).astype(BF16)
            for kept, partner in sources[base : base + 2]
        ]
        right = jnp.concatenate(both, axis=1)
        for side, left_ref in enumerate(left_refs):
            inner = jnp.dot(left_ref[...], right, preferred_element_type=F32).astype(BF16)
            for n in range(len(both)):
                for q in range(vectors):
                    at = side * depth + q * slab
                    inner_ref[(base + n) * height : (base + n + 1) * height, at : at + slab] = inner[
                        q * height : (q + 1) * height, n * slab : (n + 1) * slab
                    ]
    half = sum(
        jnp.dot(inner_ref[:, side * depth : (side + 1) * depth], turned_ref[...], preferred_element_type=F32)
        for side, turned_ref in enumerate(turned_refs)
    )
    for n, targets in enumerate(outs):
        for chunk, (ref, index) in enumerate(targets):
            start = n * height + chunk * rows
            ref[index] = half[start : start + rows].astype(ref.dtype)


def first_kernel(*refs):
    ready, (kept_ref, far_ref, got_ref, beside_ref), outs = refs[:4], refs[4:8], refs[8:]
    own_ref, lent_ref, send_ref, inner_ref = outs
    sources = [
        (kept_ref[0], kept_ref[0]),
        (far_ref[0], got_ref[0]),
        (beside_ref[0], kept_ref[1]),
        (beside_ref[ORDER[1]], got_ref[1]),
    ]
    targets = [[(ref, n), (send_ref, at + n)] for at, ref in ((0, own_ref), (2, lent_ref)) for n in range(2)]
    products(ready, inner_ref, sources, targets)


def second_kernel(*refs):
    ready, kept_refs, got_refs, (beside_ref, lent_in, send_in) = refs[:4], refs[4:6], refs[6:8], refs[8:11]
    own_ref, lent_ref, same_ref, cross_ref, inner_ref = refs[11:]
    sources = [(kept[0], got[0]) for kept, got in zip(kept_refs, got_refs)]
    sources += [(beside_ref[step], got[1]) for step, got in zip(ORDER[2:], got_refs)]
    targets = [[(own_ref, n), (same_ref, 2 + n)] for n in range(2)]
    targets += [[(lent_ref, 2 + n), (cross_ref, 2 + n)] for n in range(2)]
    lent_ref[:2] = lent_in[...]
    same_ref[:2] = send_in[:2]
    cross_ref[:2] = send_in[2:]
    products(ready, inner_ref, sources, targets)


def whole_kernel(*refs):
    ready, (kept_ref, partner_ref), part_refs, inner_ref = refs[:4], refs[4:6], refs[6:-1], refs[-1]

    def two(g, carry):
        pairs = [2 * g, 2 * g + 1]
        sources = [(kept_ref[k], partner_ref[k]) for k in pairs]
        products(ready, inner_ref, sources, [[(ref, k) for ref in part_refs] for k in pairs])
        return carry

    lax.fori_loop(0, kept_ref.shape[0] // 2, two, 0)


def finish_kernel(first_ref, second_ref, cross_ref, same_ref, lent_ref, gate_ref, out_ref):
    for n, step in enumerate(ORDER):
        own = first_ref[n] if n < 2 else second_ref[n - 2]
        totals = own + same_ref[n].astype(F32), lent_ref[n].astype(F32) + cross_ref[n].astype(F32)
        for kind, total in enumerate(totals):
            first, second = slot(kind, step)
            gate = gate_ref[kind * CHIPS + step, :1]
            out_ref[first, second] = (total * gate).astype(BF16)


def vmem_specs(count):
    return [pl.BlockSpec(memory_space=pltpu.VMEM)] * count


def shaped(dtype, *shape):
    return jax.ShapeDtypeStruct(shape, dtype)


def kernel(body, outs, operands, spaces=(), scratch=(), flops=0):
    spaces = list(spaces) + [pltpu.VMEM] * (len(operands) - len(spaces))
    return pl.pallas_call(
        body,
        out_shape=outs,
        in_specs=[pl.BlockSpec(memory_space=space) for space in spaces],
        out_specs=vmem_specs(len(outs)),
        scratch_shapes=list(scratch),
        compiler_params=pltpu.CompilerParams(vmem_limit_bytes=24 * 1024 * 1024),
        cost_estimate=pl.CostEstimate(flops=flops, bytes_accessed=1 << 20, transcendentals=0),
    )(*operands)


def shards(amplitudes, vectors, tile_mask, pair_mask):
    firsts, seconds, slab, _ = amplitudes.shape
    pairs = firsts * seconds
    virt, chips, cores = lax.axis_size("virt"), lax.axis_size("occi"), lax.axis_size("occj")
    rows = slab // virt
    chunks = virt // 2
    depth = 2 * vectors.shape[0] * slab
    turned_mask = jnp.transpose(tile_mask, (0, 2, 3, 1))
    gate = shaped(F32, pairs, 8, slab)
    arranged = [shaped(BF16, depth // 2, slab), shaped(BF16, depth // 4, slab)]
    turn = functools.partial(turn_kernel, chunks)

    def parts(count):
        return [shaped(F32 if chunk == 0 else BF16, count, rows, slab) for chunk in range(chunks)]

    def inner(count):
        return pltpu.VMEM((count * chunks * rows, depth), BF16)

    def sent(part):
        return [part[0]] + [swap_virt(part[chunk], 2 * chunk) for chunk in range(1, chunks)]

    def work(count):
        return 2 * count * depth * slab * slab

    groups = [[d, d + 1] for d in range(0, virt, 2)]
    both = lax.all_gather(vectors, "virt", axis_index_groups=groups, tiled=True)
    near = kernel(
        functools.partial(near_kernel, chunks),
        arranged,
        [pltpu.with_memory_space_constraint(both, pltpu.HBM)],
        spaces=[pltpu.HBM],
        scratch=[pltpu.VMEM(vectors.shape, vectors.dtype), pltpu.SemaphoreType.DMA((vectors.shape[0],))],
    )
    if (firsts, seconds, chips, cores, virt) == (2, CHIPS, CHIPS, 2, 4):
        *kept, cross, gates = kernel(
            mask_split_kernel,
            [shaped(BF16, 2, slab, slab)] * CHIPS + [shaped(BF16, CHIPS, slab, slab), gate],
            [
                pltpu.with_memory_space_constraint(array, pltpu.HBM)
                for array in (turned_mask, pair_mask, amplitudes)
            ],
            spaces=[pltpu.HBM] * 3,
            scratch=[
                pltpu.SMEM(turned_mask.shape, jnp.int32),
                pltpu.SMEM(pair_mask.shape, jnp.int32),
                pltpu.SemaphoreType.DMA((pairs + 2,)),
            ],
        )
        got = {step: swap_chip(kept[step], step) for step in STEPS}
        beside = swap_core(cross)
        ready = kernel(turn, arranged, (vectors,)) + near
        _, far, *rest = ORDER
        own_first, lent, sending = kernel(
            first_kernel,
            [shaped(F32, 2, rows, slab), shaped(BF16, 2, rows, slab), shaped(BF16, 4, rows, slab)],
            (*ready, kept[0], kept[far], got[far], beside),
            scratch=[inner(4)],
            flops=work(4),
        )
        own_second, lent, same, crossing = kernel(
            second_kernel,
            [shaped(F32, 2, rows, slab)] + [shaped(BF16, 4, rows, slab)] * 3,
            (*ready, *[kept[step] for step in rest], *[got[step] for step in rest], beside, lent, sending),
            scratch=[inner(4)],
            flops=work(4),
        )
        operands = (own_first, own_second, swap_both(crossing, 2), swap_virt(same, 2), swap_core(lent), gates)
        (out,) = kernel(finish_kernel, [shaped(BF16, firsts, seconds, rows, slab)], operands)
        return out
    kept, gates = kernel(
        mask_whole_kernel,
        [shaped(BF16, pairs, slab, slab), gate],
        (turned_mask, pair_mask, amplitudes),
        spaces=[pltpu.SMEM] * 2,
    )
    partner = lax.all_to_all(kept, ("occj", "occi"), split_axis=0, concat_axis=0, tiled=True)
    ready = kernel(turn, arranged, (vectors,)) + near
    part = sent(
        kernel(whole_kernel, parts(pairs), (*ready, kept, partner), scratch=[inner(2)], flops=work(pairs))
    )
    summed = part[0]
    for term in part[1:]:
        summed = summed + term.astype(F32)
    return (summed * gates[:, :1]).reshape(firsts, seconds, rows, slab).astype(BF16)


def solution(mesh):
    placed = (
        P("occi", "occj", None, None),
        P("virt", None, None),
        P("occi", "occj", None, None),
        P("occi", "occj"),
    )
    return jax.shard_map(
        shards,
        mesh=mesh,
        in_specs=placed,
        out_specs=P("occi", "occj", "virt", None),
        check_vma=False,
    )
```

```python
import functools

import jax
import jax.numpy as jnp
from jax import lax
from jax.experimental import pallas as pl
from jax.experimental.pallas import tpu as pltpu
from jax.sharding import PartitionSpec as P

TILE = 64
SLAB_TILES = 2
CHIPS = 4
STEPS = (1, 3, 2)
ORDER = (0, 1, 3, 2)
BF16 = jnp.bfloat16
F32 = jnp.float32


def swap_virt(array, step):
    return lax.ppermute(array, "virt", [(d, d ^ step) for d in range(lax.axis_size("virt"))])


def swap_both(array, step):
    size = lax.axis_size("virt")
    moves = [(c * size + d, (1 - c) * size + (d ^ step)) for c in range(2) for d in range(size)]
    return lax.ppermute(array, ("occj", "virt"), moves)


def swap_core(array):
    return lax.ppermute(array, "occj", [(0, 1), (1, 0)])


def swap_chip(array, step):
    return lax.ppermute(array, "occi", [(d, d ^ step) for d in range(lax.axis_size("occi"))])


def slot(kind, step):
    first = lax.axis_index("occj") if kind == 0 else 1 - lax.axis_index("occj")
    return first, lax.axis_index("occi") ^ step


def keep_rows(mask_ref, first, second, half):
    lane = lax.broadcasted_iota(jnp.int32, (1, SLAB_TILES * TILE), 1) // TILE
    keep = jnp.zeros(lane.shape, F32)
    for tile in range(SLAB_TILES):
        keep = jnp.where(lane == tile, mask_ref[first, half, tile, second].astype(F32), keep)
    return jnp.broadcast_to(keep, (TILE, SLAB_TILES * TILE)).astype(BF16)


def mask_split_kernel(mask_hbm, pair_hbm, amp_hbm, *refs):
    kept_refs, (cross_ref, gate_ref, mask_ref, pair_ref, sems) = refs[:CHIPS], refs[CHIPS:]
    copies = [
        pltpu.make_async_copy(mask_hbm, mask_ref, sems.at[0]),
        pltpu.make_async_copy(pair_hbm, pair_ref, sems.at[1]),
    ]
    blocks = []
    for step in STEPS + (0,):
        for kind in range(2):
            first, second = slot(kind, step)
            target = kept_refs[step].at[kind]
            copies.append(pltpu.make_async_copy(amp_hbm.at[first, second], target, sems.at[len(copies)]))
            blocks.append((first, second, target, kind, step, copies[-1]))
    for copy in copies:
        copy.start()
    copies[0].wait()
    copies[1].wait()
    for first, second, target, kind, step, copy in blocks:
        gate_ref[kind * CHIPS + step] = jnp.full(gate_ref.shape[1:], pair_ref[first, second].astype(F32))
        keeps = [keep_rows(mask_ref, first, second, half) for half in range(SLAB_TILES)]
        copy.wait()
        for half, keep in enumerate(keeps):
            part = slice(half * TILE, (half + 1) * TILE)
            kept = target[part] * keep
            target[part] = kept
            if kind:
                cross_ref[step, part] = kept


def mask_whole_kernel(mask_ref, pair_ref, amp_ref, kept_ref, gate_ref):
    seconds = amp_ref.shape[1]

    def one(block, carry):
        first, second = block // seconds, block % seconds
        for half in range(SLAB_TILES):
            part = slice(half * TILE, (half + 1) * TILE)
            kept_ref[block, part] = amp_ref[first, second, part] * keep_rows(mask_ref, first, second, half)
        gate_ref[block] = jnp.full(gate_ref.shape[1:], pair_ref[first, second].astype(F32))
        return carry

    lax.fori_loop(0, kept_ref.shape[0], one, 0)


def turn_kernel(chunks, vec_ref, turned_ref, left_ref):
    vectors, slab, _ = vec_ref.shape
    rows = left_ref.shape[0] // (vectors * chunks)
    me = lax.axis_index("virt")
    for q in range(vectors):
        turned_ref[q * slab : (q + 1) * slab] = vec_ref[q].astype(F32).T.astype(BF16)
        for chunk in range(chunks):
            start = pl.multiple_of((me ^ (2 * chunk)) * rows, rows)
            low = (q * chunks + chunk) * rows
            left_ref[low : low + rows] = vec_ref[q, pl.ds(start, rows), :]


def products(ready, inner_ref, sources, outs):
    turned_refs, left_refs = ready[::2], ready[1::2]
    slab = turned_refs[0].shape[1]
    depth = turned_refs[0].shape[0]
    vectors = depth // slab
    height = left_refs[0].shape[0] // vectors
    rows = height // len(outs[0])
    for base in range(0, len(sources), 2):
        both = [
            (kept.astype(F32) + partner.astype(F32).T).astype(BF16)
            for kept, partner in sources[base : base + 2]
        ]
        right = jnp.concatenate(both, axis=1)
        for side, left_ref in enumerate(left_refs):
            inner = jnp.dot(left_ref[...], right, preferred_element_type=F32).astype(BF16)
            for n in range(len(both)):
                for q in range(vectors):
                    at = side * depth + q * slab
                    inner_ref[(base + n) * height : (base + n + 1) * height, at : at + slab] = inner[
                        q * height : (q + 1) * height, n * slab : (n + 1) * slab
                    ]
    half = sum(
        jnp.dot(inner_ref[:, side * depth : (side + 1) * depth], turned_ref[...], preferred_element_type=F32)
        for side, turned_ref in enumerate(turned_refs)
    )
    for n, targets in enumerate(outs):
        for chunk, (ref, index) in enumerate(targets):
            start = n * height + chunk * rows
            ref[index] = half[start : start + rows].astype(ref.dtype)


def first_kernel(*refs):
    ready, (kept_ref, far_ref, got_ref, beside_ref), outs = refs[:4], refs[4:8], refs[8:]
    own_ref, lent_ref, send_ref, inner_ref = outs
    sources = [
        (kept_ref[0], kept_ref[0]),
        (far_ref[0], got_ref[0]),
        (beside_ref[0], kept_ref[1]),
        (beside_ref[ORDER[1]], got_ref[1]),
    ]
    targets = [[(ref, n), (send_ref, at + n)] for at, ref in ((0, own_ref), (2, lent_ref)) for n in range(2)]
    products(ready, inner_ref, sources, targets)


def second_kernel(*refs):
    ready, kept_refs, got_refs, (beside_ref, lent_in, send_in) = refs[:4], refs[4:6], refs[6:8], refs[8:11]
    own_ref, lent_ref, same_ref, cross_ref, inner_ref = refs[11:]
    sources = [(kept[0], got[0]) for kept, got in zip(kept_refs, got_refs)]
    sources += [(beside_ref[step], got[1]) for step, got in zip(ORDER[2:], got_refs)]
    targets = [[(own_ref, n), (same_ref, 2 + n)] for n in range(2)]
    targets += [[(lent_ref, 2 + n), (cross_ref, 2 + n)] for n in range(2)]
    lent_ref[:2] = lent_in[...]
    same_ref[:2] = send_in[:2]
    cross_ref[:2] = send_in[2:]
    products(ready, inner_ref, sources, targets)


def whole_kernel(*refs):
    ready, (kept_ref, partner_ref), part_refs, inner_ref = refs[:4], refs[4:6], refs[6:-1], refs[-1]

    def two(g, carry):
        pairs = [2 * g, 2 * g + 1]
        sources = [(kept_ref[k], partner_ref[k]) for k in pairs]
        products(ready, inner_ref, sources, [[(ref, k) for ref in part_refs] for k in pairs])
        return carry

    lax.fori_loop(0, kept_ref.shape[0] // 2, two, 0)


def finish_kernel(first_ref, second_ref, cross_ref, same_ref, lent_ref, gate_ref, out_ref):
    for n, step in enumerate(ORDER):
        own = first_ref[n] if n < 2 else second_ref[n - 2]
        totals = own + same_ref[n].astype(F32), lent_ref[n].astype(F32) + cross_ref[n].astype(F32)
        for kind, total in enumerate(totals):
            first, second = slot(kind, step)
            gate = gate_ref[kind * CHIPS + step, :1]
            out_ref[first, second] = (total * gate).astype(BF16)


def vmem_specs(count):
    return [pl.BlockSpec(memory_space=pltpu.VMEM)] * count


def shaped(dtype, *shape):
    return jax.ShapeDtypeStruct(shape, dtype)


def kernel(body, outs, operands, spaces=(), scratch=(), flops=0):
    spaces = list(spaces) + [pltpu.VMEM] * (len(operands) - len(spaces))
    return pl.pallas_call(
        body,
        out_shape=outs,
        in_specs=[pl.BlockSpec(memory_space=space) for space in spaces],
        out_specs=vmem_specs(len(outs)),
        scratch_shapes=list(scratch),
        compiler_params=pltpu.CompilerParams(vmem_limit_bytes=24 * 1024 * 1024),
        cost_estimate=pl.CostEstimate(flops=flops, bytes_accessed=1 << 20, transcendentals=0),
    )(*operands)


def shards(amplitudes, vectors, tile_mask, pair_mask):
    firsts, seconds, slab, _ = amplitudes.shape
    pairs = firsts * seconds
    virt, chips, cores = lax.axis_size("virt"), lax.axis_size("occi"), lax.axis_size("occj")
    rows = slab // virt
    chunks = virt // 2
    depth = 2 * vectors.shape[0] * slab
    turned_mask = jnp.transpose(tile_mask, (0, 2, 3, 1))
    gate = shaped(F32, pairs, 8, slab)
    arranged = [shaped(BF16, depth // 2, slab), shaped(BF16, depth // 4, slab)]
    turn = functools.partial(turn_kernel, chunks)

    def parts(count):
        return [shaped(F32 if chunk == 0 else BF16, count, rows, slab) for chunk in range(chunks)]

    def inner(count):
        return pltpu.VMEM((count * chunks * rows, depth), BF16)

    def sent(part):
        return [part[0]] + [swap_virt(part[chunk], 2 * chunk) for chunk in range(1, chunks)]

    def work(count):
        return 2 * count * depth * slab * slab

    near = swap_virt(vectors, 1)
    if (firsts, seconds, chips, cores, virt) == (2, CHIPS, CHIPS, 2, 4):
        *kept, cross, gates = kernel(
            mask_split_kernel,
            [shaped(BF16, 2, slab, slab)] * CHIPS + [shaped(BF16, CHIPS, slab, slab), gate],
            [
                pltpu.with_memory_space_constraint(array, pltpu.HBM)
                for array in (turned_mask, pair_mask, amplitudes)
            ],
            spaces=[pltpu.HBM] * 3,
            scratch=[
                pltpu.SMEM(turned_mask.shape, jnp.int32),
                pltpu.SMEM(pair_mask.shape, jnp.int32),
                pltpu.SemaphoreType.DMA((pairs + 2,)),
            ],
        )
        got = {step: swap_chip(kept[step], step) for step in STEPS}
        beside = swap_core(cross)
        ready = kernel(turn, arranged, (vectors,)) + kernel(turn, arranged, (near,))
        _, far, *rest = ORDER
        own_first, lent, sending = kernel(
            first_kernel,
            [shaped(F32, 2, rows, slab), shaped(BF16, 2, rows, slab), shaped(BF16, 4, rows, slab)],
            (*ready, kept[0], kept[far], got[far], beside),
            scratch=[inner(4)],
            flops=work(4),
        )
        own_second, lent, same, crossing = kernel(
            second_kernel,
            [shaped(F32, 2, rows, slab)] + [shaped(BF16, 4, rows, slab)] * 3,
            (*ready, *[kept[step] for step in rest], *[got[step] for step in rest], beside, lent, sending),
            scratch=[inner(4)],
            flops=work(4),
        )
        operands = (own_first, own_second, swap_both(crossing, 2), swap_virt(same, 2), swap_core(lent), gates)
        (out,) = kernel(finish_kernel, [shaped(BF16, firsts, seconds, rows, slab)], operands)
        return out
    kept, gates = kernel(
        mask_whole_kernel,
        [shaped(BF16, pairs, slab, slab), gate],
        (turned_mask, pair_mask, amplitudes),
        spaces=[pltpu.SMEM] * 2,
    )
    partner = lax.all_to_all(kept, ("occj", "occi"), split_axis=0, concat_axis=0, tiled=True)
    ready = kernel(turn, arranged, (vectors,)) + kernel(turn, arranged, (near,))
    part = sent(
        kernel(whole_kernel, parts(pairs), (*ready, kept, partner), scratch=[inner(2)], flops=work(pairs))
    )
    summed = part[0]
    for term in part[1:]:
        summed = summed + term.astype(F32)
    return (summed * gates[:, :1]).reshape(firsts, seconds, rows, slab).astype(BF16)


def solution(mesh):
    placed = (
        P("occi", "occj", None, None),
        P("virt", None, None),
        P("occi", "occj", None, None),
        P("occi", "occj"),
    )
    return jax.shard_map(
        shards,
        mesh=mesh,
        in_specs=placed,
        out_specs=P("occi", "occj", "virt", None),
        check_vma=False,
    )
```

```python
import functools

import jax
import jax.numpy as jnp
from jax import lax
from jax.experimental import pallas as pl
from jax.experimental.pallas import tpu as pltpu
from jax.sharding import PartitionSpec as P

TILE = 64
SLAB_TILES = 2
CHIPS = 4
STEPS = (3, 2, 1)
ORDER = (0, 3, 2, 1)
BF16 = jnp.bfloat16
F32 = jnp.float32


def swap_virt(array, step):
    return lax.ppermute(array, "virt", [(d, d ^ step) for d in range(lax.axis_size("virt"))])


def swap_both(array, step):
    size = lax.axis_size("virt")
    moves = [(c * size + d, (1 - c) * size + (d ^ step)) for c in range(2) for d in range(size)]
    return lax.ppermute(array, ("occj", "virt"), moves)


def swap_core(array):
    return lax.ppermute(array, "occj", [(0, 1), (1, 0)])


def swap_chip(array, step):
    return lax.ppermute(array, "occi", [(d, d ^ step) for d in range(lax.axis_size("occi"))])


def slot(kind, step):
    first = lax.axis_index("occj") if kind == 0 else 1 - lax.axis_index("occj")
    return first, lax.axis_index("occi") ^ step


def keep_rows(mask_ref, first, second, half):
    lane = lax.broadcasted_iota(jnp.int32, (1, SLAB_TILES * TILE), 1) // TILE
    keep = jnp.zeros(lane.shape, F32)
    for tile in range(SLAB_TILES):
        keep = jnp.where(lane == tile, mask_ref[first, half, tile, second].astype(F32), keep)
    return jnp.broadcast_to(keep, (TILE, SLAB_TILES * TILE)).astype(BF16)


def mask_split_kernel(mask_hbm, pair_hbm, amp_hbm, *refs):
    kept_refs, (cross_ref, gate_ref, mask_ref, pair_ref, sems) = refs[:CHIPS], refs[CHIPS:]
    copies = [
        pltpu.make_async_copy(mask_hbm, mask_ref, sems.at[0]),
        pltpu.make_async_copy(pair_hbm, pair_ref, sems.at[1]),
    ]
    blocks = []
    for step in STEPS + (0,):
        for kind in range(2):
            first, second = slot(kind, step)
            target = kept_refs[step].at[kind]
            copies.append(pltpu.make_async_copy(amp_hbm.at[first, second], target, sems.at[len(copies)]))
            blocks.append((first, second, target, kind, step, copies[-1]))
    for copy in copies:
        copy.start()
    copies[0].wait()
    copies[1].wait()
    for first, second, target, kind, step, copy in blocks:
        gate_ref[kind * CHIPS + step] = jnp.full(gate_ref.shape[1:], pair_ref[first, second].astype(F32))
        keeps = [keep_rows(mask_ref, first, second, half) for half in range(SLAB_TILES)]
        copy.wait()
        for half, keep in enumerate(keeps):
            part = slice(half * TILE, (half + 1) * TILE)
            kept = target[part] * keep
            target[part] = kept
            if kind:
                cross_ref[step, part] = kept


def mask_whole_kernel(mask_ref, pair_ref, amp_ref, kept_ref, gate_ref):
    seconds = amp_ref.shape[1]

    def one(block, carry):
        first, second = block // seconds, block % seconds
        for half in range(SLAB_TILES):
            part = slice(half * TILE, (half + 1) * TILE)
            kept_ref[block, part] = amp_ref[first, second, part] * keep_rows(mask_ref, first, second, half)
        gate_ref[block] = jnp.full(gate_ref.shape[1:], pair_ref[first, second].astype(F32))
        return carry

    lax.fori_loop(0, kept_ref.shape[0], one, 0)


def turn_kernel(chunks, vec_ref, turned_ref, left_ref):
    vectors, slab, _ = vec_ref.shape
    rows = left_ref.shape[0] // (vectors * chunks)
    me = lax.axis_index("virt")
    for q in range(vectors):
        turned_ref[q * slab : (q + 1) * slab] = vec_ref[q].astype(F32).T.astype(BF16)
        for chunk in range(chunks):
            start = pl.multiple_of((me ^ (2 * chunk)) * rows, rows)
            low = (q * chunks + chunk) * rows
            left_ref[low : low + rows] = vec_ref[q, pl.ds(start, rows), :]


def products(ready, inner_ref, sources, outs):
    turned_refs, left_refs = ready[::2], ready[1::2]
    slab = turned_refs[0].shape[1]
    depth = turned_refs[0].shape[0]
    vectors = depth // slab
    height = left_refs[0].shape[0] // vectors
    rows = height // len(outs[0])
    for base in range(0, len(sources), 2):
        both = [
            (kept.astype(F32) + partner.astype(F32).T).astype(BF16)
            for kept, partner in sources[base : base + 2]
        ]
        right = jnp.concatenate(both, axis=1)
        for side, left_ref in enumerate(left_refs):
            inner = jnp.dot(left_ref[...], right, preferred_element_type=F32).astype(BF16)
            for n in range(len(both)):
                for q in range(vectors):
                    at = side * depth + q * slab
                    inner_ref[(base + n) * height : (base + n + 1) * height, at : at + slab] = inner[
                        q * height : (q + 1) * height, n * slab : (n + 1) * slab
                    ]
    half = sum(
        jnp.dot(inner_ref[:, side * depth : (side + 1) * depth], turned_ref[...], preferred_element_type=F32)
        for side, turned_ref in enumerate(turned_refs)
    )
    for n, targets in enumerate(outs):
        for chunk, (ref, index) in enumerate(targets):
            start = n * height + chunk * rows
            ref[index] = half[start : start + rows].astype(ref.dtype)


def first_kernel(*refs):
    ready, (kept_ref, far_ref, got_ref, beside_ref), outs = refs[:4], refs[4:8], refs[8:]
    own_ref, lent_ref, send_ref, inner_ref = outs
    sources = [
        (kept_ref[0], kept_ref[0]),
        (far_ref[0], got_ref[0]),
        (beside_ref[0], kept_ref[1]),
        (beside_ref[ORDER[1]], got_ref[1]),
    ]
    targets = [[(ref, n), (send_ref, at + n)] for at, ref in ((0, own_ref), (2, lent_ref)) for n in range(2)]
    products(ready, inner_ref, sources, targets)


def second_kernel(*refs):
    ready, kept_refs, got_refs, (beside_ref, lent_in, send_in) = refs[:4], refs[4:6], refs[6:8], refs[8:11]
    own_ref, lent_ref, same_ref, cross_ref, inner_ref = refs[11:]
    sources = [(kept[0], got[0]) for kept, got in zip(kept_refs, got_refs)]
    sources += [(beside_ref[step], got[1]) for step, got in zip(ORDER[2:], got_refs)]
    targets = [[(own_ref, n), (same_ref, 2 + n)] for n in range(2)]
    targets += [[(lent_ref, 2 + n), (cross_ref, 2 + n)] for n in range(2)]
    lent_ref[:2] = lent_in[...]
    same_ref[:2] = send_in[:2]
    cross_ref[:2] = send_in[2:]
    products(ready, inner_ref, sources, targets)


def whole_kernel(*refs):
    ready, (kept_ref, partner_ref), part_refs, inner_ref = refs[:4], refs[4:6], refs[6:-1], refs[-1]

    def two(g, carry):
        pairs = [2 * g, 2 * g + 1]
        sources = [(kept_ref[k], partner_ref[k]) for k in pairs]
        products(ready, inner_ref, sources, [[(ref, k) for ref in part_refs] for k in pairs])
        return carry

    lax.fori_loop(0, kept_ref.shape[0] // 2, two, 0)


def finish_kernel(first_ref, second_ref, cross_ref, same_ref, lent_ref, gate_ref, out_ref):
    for n, step in enumerate(ORDER):
        own = first_ref[n] if n < 2 else second_ref[n - 2]
        totals = own + same_ref[n].astype(F32), lent_ref[n].astype(F32) + cross_ref[n].astype(F32)
        for kind, total in enumerate(totals):
            first, second = slot(kind, step)
            gate = gate_ref[kind * CHIPS + step, :1]
            out_ref[first, second] = (total * gate).astype(BF16)


def vmem_specs(count):
    return [pl.BlockSpec(memory_space=pltpu.VMEM)] * count


def shaped(dtype, *shape):
    return jax.ShapeDtypeStruct(shape, dtype)


def kernel(body, outs, operands, spaces=(), scratch=(), flops=0):
    spaces = list(spaces) + [pltpu.VMEM] * (len(operands) - len(spaces))
    return pl.pallas_call(
        body,
        out_shape=outs,
        in_specs=[pl.BlockSpec(memory_space=space) for space in spaces],
        out_specs=vmem_specs(len(outs)),
        scratch_shapes=list(scratch),
        compiler_params=pltpu.CompilerParams(vmem_limit_bytes=24 * 1024 * 1024),
        cost_estimate=pl.CostEstimate(flops=flops, bytes_accessed=1 << 20, transcendentals=0),
    )(*operands)


def shards(amplitudes, vectors, tile_mask, pair_mask):
    firsts, seconds, slab, _ = amplitudes.shape
    pairs = firsts * seconds
    virt, chips, cores = lax.axis_size("virt"), lax.axis_size("occi"), lax.axis_size("occj")
    rows = slab // virt
    chunks = virt // 2
    depth = 2 * vectors.shape[0] * slab
    turned_mask = jnp.transpose(tile_mask, (0, 2, 3, 1))
    gate = shaped(F32, pairs, 8, slab)
    arranged = [shaped(BF16, depth // 2, slab), shaped(BF16, depth // 4, slab)]
    turn = functools.partial(turn_kernel, chunks)

    def parts(count):
        return [shaped(F32 if chunk == 0 else BF16, count, rows, slab) for chunk in range(chunks)]

    def inner(count):
        return pltpu.VMEM((count * chunks * rows, depth), BF16)

    def sent(part):
        return [part[0]] + [swap_virt(part[chunk], 2 * chunk) for chunk in range(1, chunks)]

    def work(count):
        return 2 * count * depth * slab * slab

    near = swap_virt(vectors, 1)
    if (firsts, seconds, chips, cores, virt) == (2, CHIPS, CHIPS, 2, 4):
        *kept, cross, gates = kernel(
            mask_split_kernel,
            [shaped(BF16, 2, slab, slab)] * CHIPS + [shaped(BF16, CHIPS, slab, slab), gate],
            [
                pltpu.with_memory_space_constraint(array, pltpu.HBM)
                for array in (turned_mask, pair_mask, amplitudes)
            ],
            spaces=[pltpu.HBM] * 3,
            scratch=[
                pltpu.SMEM(turned_mask.shape, jnp.int32),
                pltpu.SMEM(pair_mask.shape, jnp.int32),
                pltpu.SemaphoreType.DMA((pairs + 2,)),
            ],
        )
        got = {step: swap_chip(kept[step], step) for step in STEPS}
        beside = swap_core(cross)
        ready = kernel(turn, arranged, (vectors,)) + kernel(turn, arranged, (near,))
        _, far, *rest = ORDER
        own_first, lent, sending = kernel(
            first_kernel,
            [shaped(F32, 2, rows, slab), shaped(BF16, 2, rows, slab), shaped(BF16, 4, rows, slab)],
            (*ready, kept[0], kept[far], got[far], beside),
            scratch=[inner(4)],
            flops=work(4),
        )
        own_second, lent, same, crossing = kernel(
            second_kernel,
            [shaped(F32, 2, rows, slab)] + [shaped(BF16, 4, rows, slab)] * 3,
            (*ready, *[kept[step] for step in rest], *[got[step] for step in rest], beside, lent, sending),
            scratch=[inner(4)],
            flops=work(4),
        )
        operands = (own_first, own_second, swap_both(crossing, 2), swap_virt(same, 2), swap_core(lent), gates)
        (out,) = kernel(finish_kernel, [shaped(BF16, firsts, seconds, rows, slab)], operands)
        return out
    kept, gates = kernel(
        mask_whole_kernel,
        [shaped(BF16, pairs, slab, slab), gate],
        (turned_mask, pair_mask, amplitudes),
        spaces=[pltpu.SMEM] * 2,
    )
    partner = lax.all_to_all(kept, ("occj", "occi"), split_axis=0, concat_axis=0, tiled=True)
    ready = kernel(turn, arranged, (vectors,)) + kernel(turn, arranged, (near,))
    part = sent(
        kernel(whole_kernel, parts(pairs), (*ready, kept, partner), scratch=[inner(2)], flops=work(pairs))
    )
    summed = part[0]
    for term in part[1:]:
        summed = summed + term.astype(F32)
    return (summed * gates[:, :1]).reshape(firsts, seconds, rows, slab).astype(BF16)


def solution(mesh):
    placed = (
        P("occi", "occj", None, None),
        P("virt", None, None),
        P("occi", "occj", None, None),
        P("occi", "occj"),
    )
    return jax.shard_map(
        shards,
        mesh=mesh,
        in_specs=placed,
        out_specs=P("occi", "occj", "virt", None),
        check_vma=False,
    )
```

```python
import functools

import jax
import jax.numpy as jnp
from jax import lax
from jax.experimental import pallas as pl
from jax.experimental.pallas import tpu as pltpu
from jax.sharding import PartitionSpec as P

TILE = 64
SLAB_TILES = 2
CHIPS = 4
STEPS = (3, 2, 1)
ORDER = (0, 3, 2, 1)
BF16 = jnp.bfloat16
F32 = jnp.float32


def swap_virt(array, step):
    return lax.ppermute(array, "virt", [(d, d ^ step) for d in range(lax.axis_size("virt"))])


def swap_both(array, step):
    size = lax.axis_size("virt")
    moves = [(c * size + d, (1 - c) * size + (d ^ step)) for c in range(2) for d in range(size)]
    return lax.ppermute(array, ("occj", "virt"), moves)


def swap_core(array):
    return lax.ppermute(array, "occj", [(0, 1), (1, 0)])


def swap_chip(array, step):
    return lax.ppermute(array, "occi", [(d, d ^ step) for d in range(lax.axis_size("occi"))])


def slot(kind, step):
    first = lax.axis_index("occj") if kind == 0 else 1 - lax.axis_index("occj")
    return first, lax.axis_index("occi") ^ step


def keep_rows(mask_ref, first, second, half):
    lane = lax.broadcasted_iota(jnp.int32, (1, SLAB_TILES * TILE), 1) // TILE
    keep = jnp.zeros(lane.shape, F32)
    for tile in range(SLAB_TILES):
        keep = jnp.where(lane == tile, mask_ref[first, half, tile, second].astype(F32), keep)
    return jnp.broadcast_to(keep, (TILE, SLAB_TILES * TILE)).astype(BF16)


def mask_split_kernel(mask_hbm, pair_hbm, amp_hbm, *refs):
    kept_refs, (cross_ref, gate_ref, mask_ref, pair_ref, sems) = refs[:CHIPS], refs[CHIPS:]
    copies = [
        pltpu.make_async_copy(mask_hbm, mask_ref, sems.at[0]),
        pltpu.make_async_copy(pair_hbm, pair_ref, sems.at[1]),
    ]
    blocks = []
    for step in STEPS + (0,):
        for kind in range(2):
            first, second = slot(kind, step)
            target = kept_refs[step].at[kind]
            copies.append(pltpu.make_async_copy(amp_hbm.at[first, second], target, sems.at[len(copies)]))
            blocks.append((first, second, target, kind, step, copies[-1]))
    for copy in copies:
        copy.start()
    copies[0].wait()
    copies[1].wait()
    for first, second, target, kind, step, copy in blocks:
        gate_ref[kind * CHIPS + step] = jnp.full(gate_ref.shape[1:], pair_ref[first, second].astype(F32))
        keeps = [keep_rows(mask_ref, first, second, half) for half in range(SLAB_TILES)]
        copy.wait()
        for half, keep in enumerate(keeps):
            part = slice(half * TILE, (half + 1) * TILE)
            kept = target[part] * keep
            target[part] = kept
            if kind:
                cross_ref[step, part] = kept


def mask_whole_kernel(mask_ref, pair_ref, amp_ref, kept_ref, gate_ref):
    seconds = amp_ref.shape[1]

    def one(block, carry):
        first, second = block // seconds, block % seconds
        for half in range(SLAB_TILES):
            part = slice(half * TILE, (half + 1) * TILE)
            kept_ref[block, part] = amp_ref[first, second, part] * keep_rows(mask_ref, first, second, half)
        gate_ref[block] = jnp.full(gate_ref.shape[1:], pair_ref[first, second].astype(F32))
        return carry

    lax.fori_loop(0, kept_ref.shape[0], one, 0)


def turn_kernel(chunks, *refs):
    vec_refs, turned_ref, left_ref = refs[:-2], refs[-2], refs[-1]
    slab = turned_ref.shape[1]
    rows = slab * left_ref.shape[0] // (turned_ref.shape[0] * chunks)
    me = lax.axis_index("virt")
    at, low = 0, 0
    for vec_ref in vec_refs:
        for q in range(vec_ref.shape[0]):
            turned_ref[at : at + slab] = vec_ref[q].astype(F32).T.astype(BF16)
            at += slab
            for chunk in range(chunks):
                start = pl.multiple_of((me ^ (2 * chunk)) * rows, rows)
                left_ref[low : low + rows] = vec_ref[q, pl.ds(start, rows), :]
                low += rows


def products(ready, inner_ref, sources, outs):
    turned_ref, left_ref = ready
    slab = turned_ref.shape[1]
    vectors = turned_ref.shape[0] // slab
    height = left_ref.shape[0] // vectors
    rows = height // len(outs[0])
    for base in range(0, len(sources), 2):
        both = [
            (kept.astype(F32) + partner.astype(F32).T).astype(BF16)
            for kept, partner in sources[base : base + 2]
        ]
        inner = jnp.dot(left_ref[...], jnp.concatenate(both, axis=1), preferred_element_type=F32).astype(BF16)
        for n in range(len(both)):
            for q in range(vectors):
                inner_ref[(base + n) * height : (base + n + 1) * height, q * slab : (q + 1) * slab] = inner[
                    q * height : (q + 1) * height, n * slab : (n + 1) * slab
                ]
    half = jnp.dot(inner_ref[...], turned_ref[...], preferred_element_type=F32)
    for n, targets in enumerate(outs):
        for chunk, (ref, index) in enumerate(targets):
            start = n * height + chunk * rows
            ref[index] = half[start : start + rows].astype(ref.dtype)


def first_kernel(*refs):
    ready, (kept_ref, far_ref, got_ref, beside_ref), outs = refs[:2], refs[2:6], refs[6:]
    own_ref, lent_ref, send_ref, inner_ref = outs
    sources = [
        (kept_ref[0], kept_ref[0]),
        (far_ref[0], got_ref[0]),
        (beside_ref[0], kept_ref[1]),
        (beside_ref[ORDER[1]], got_ref[1]),
    ]
    targets = [[(ref, n), (send_ref, at + n)] for at, ref in ((0, own_ref), (2, lent_ref)) for n in range(2)]
    products(ready, inner_ref, sources, targets)


def second_kernel(*refs):
    ready, kept_refs, got_refs, (beside_ref, lent_in, send_in) = refs[:2], refs[2:4], refs[4:6], refs[6:9]
    own_ref, lent_ref, same_ref, cross_ref, inner_ref = refs[9:]
    sources = [(kept[0], got[0]) for kept, got in zip(kept_refs, got_refs)]
    sources += [(beside_ref[step], got[1]) for step, got in zip(ORDER[2:], got_refs)]
    targets = [[(own_ref, n), (same_ref, 2 + n)] for n in range(2)]
    targets += [[(lent_ref, 2 + n), (cross_ref, 2 + n)] for n in range(2)]
    lent_ref[:2] = lent_in[...]
    same_ref[:2] = send_in[:2]
    cross_ref[:2] = send_in[2:]
    products(ready, inner_ref, sources, targets)


def whole_kernel(*refs):
    ready, (kept_ref, partner_ref), part_refs, inner_ref = refs[:2], refs[2:4], refs[4:-1], refs[-1]

    def two(g, carry):
        pairs = [2 * g, 2 * g + 1]
        sources = [(kept_ref[k], partner_ref[k]) for k in pairs]
        products(ready, inner_ref, sources, [[(ref, k) for ref in part_refs] for k in pairs])
        return carry

    lax.fori_loop(0, kept_ref.shape[0] // 2, two, 0)


def finish_kernel(first_ref, second_ref, cross_ref, same_ref, lent_ref, gate_ref, out_ref):
    for n, step in enumerate(ORDER):
        own = first_ref[n] if n < 2 else second_ref[n - 2]
        totals = own + same_ref[n].astype(F32), lent_ref[n].astype(F32) + cross_ref[n].astype(F32)
        for kind, total in enumerate(totals):
            first, second = slot(kind, step)
            gate = gate_ref[kind * CHIPS + step, :1]
            out_ref[first, second] = (total * gate).astype(BF16)


def vmem_specs(count):
    return [pl.BlockSpec(memory_space=pltpu.VMEM)] * count


def shaped(dtype, *shape):
    return jax.ShapeDtypeStruct(shape, dtype)


def kernel(body, outs, operands, spaces=(), scratch=(), flops=0):
    spaces = list(spaces) + [pltpu.VMEM] * (len(operands) - len(spaces))
    return pl.pallas_call(
        body,
        out_shape=outs,
        in_specs=[pl.BlockSpec(memory_space=space) for space in spaces],
        out_specs=vmem_specs(len(outs)),
        scratch_shapes=list(scratch),
        compiler_params=pltpu.CompilerParams(vmem_limit_bytes=24 * 1024 * 1024),
        cost_estimate=pl.CostEstimate(flops=flops, bytes_accessed=1 << 20, transcendentals=0),
    )(*operands)


def shards(amplitudes, vectors, tile_mask, pair_mask):
    firsts, seconds, slab, _ = amplitudes.shape
    pairs = firsts * seconds
    virt, chips, cores = lax.axis_size("virt"), lax.axis_size("occi"), lax.axis_size("occj")
    rows = slab // virt
    chunks = virt // 2
    depth = 2 * vectors.shape[0] * slab
    turned_mask = jnp.transpose(tile_mask, (0, 2, 3, 1))
    gate = shaped(F32, pairs, 8, slab)
    arranged = [shaped(BF16, depth, slab), shaped(BF16, depth // slab * chunks * rows, slab)]
    turn = functools.partial(turn_kernel, chunks)

    def parts(count):
        return [shaped(F32 if chunk == 0 else BF16, count, rows, slab) for chunk in range(chunks)]

    def inner(count):
        return pltpu.VMEM((count * chunks * rows, depth), BF16)

    def sent(part):
        return [part[0]] + [swap_virt(part[chunk], 2 * chunk) for chunk in range(1, chunks)]

    def work(count):
        return 2 * count * depth * slab * slab

    near = swap_virt(vectors, 1)
    if (firsts, seconds, chips, cores, virt) == (2, CHIPS, CHIPS, 2, 4):
        *kept, cross, gates = kernel(
            mask_split_kernel,
            [shaped(BF16, 2, slab, slab)] * CHIPS + [shaped(BF16, CHIPS, slab, slab), gate],
            [
                pltpu.with_memory_space_constraint(array, pltpu.HBM)
                for array in (turned_mask, pair_mask, amplitudes)
            ],
            spaces=[pltpu.HBM] * 3,
            scratch=[
                pltpu.SMEM(turned_mask.shape, jnp.int32),
                pltpu.SMEM(pair_mask.shape, jnp.int32),
                pltpu.SemaphoreType.DMA((pairs + 2,)),
            ],
        )
        got = {step: swap_chip(kept[step], step) for step in STEPS}
        beside = swap_core(cross)
        ready = kernel(turn, arranged, (vectors, near))
        _, far, *rest = ORDER
        own_first, lent, sending = kernel(
            first_kernel,
            [shaped(F32, 2, rows, slab), shaped(BF16, 2, rows, slab), shaped(BF16, 4, rows, slab)],
            (*ready, kept[0], kept[far], got[far], beside),
            scratch=[inner(4)],
            flops=work(4),
        )
        own_second, lent, same, crossing = kernel(
            second_kernel,
            [shaped(F32, 2, rows, slab)] + [shaped(BF16, 4, rows, slab)] * 3,
            (*ready, *[kept[step] for step in rest], *[got[step] for step in rest], beside, lent, sending),
            scratch=[inner(4)],
            flops=work(4),
        )
        operands = (own_first, own_second, swap_both(crossing, 2), swap_virt(same, 2), swap_core(lent), gates)
        (out,) = kernel(finish_kernel, [shaped(BF16, firsts, seconds, rows, slab)], operands)
        return out
    kept, gates = kernel(
        mask_whole_kernel,
        [shaped(BF16, pairs, slab, slab), gate],
        (turned_mask, pair_mask, amplitudes),
        spaces=[pltpu.SMEM] * 2,
    )
    partner = lax.all_to_all(kept, ("occj", "occi"), split_axis=0, concat_axis=0, tiled=True)
    ready = kernel(turn, arranged, (vectors, near))
    part = sent(
        kernel(whole_kernel, parts(pairs), (*ready, kept, partner), scratch=[inner(2)], flops=work(pairs))
    )
    summed = part[0]
    for term in part[1:]:
        summed = summed + term.astype(F32)
    return (summed * gates[:, :1]).reshape(firsts, seconds, rows, slab).astype(BF16)


def solution(mesh):
    placed = (
        P("occi", "occj", None, None),
        P("virt", None, None),
        P("occi", "occj", None, None),
        P("occi", "occj"),
    )
    return jax.shard_map(
        shards,
        mesh=mesh,
        in_specs=placed,
        out_specs=P("occi", "occj", "virt", None),
        check_vma=False,
    )
```

```python
import functools

import jax
import jax.numpy as jnp
from jax import lax
from jax.experimental import pallas as pl
from jax.experimental.pallas import tpu as pltpu
from jax.sharding import PartitionSpec as P

TILE = 64
SLAB_TILES = 2
CHIPS = 4
STEPS = (3, 2, 1)
ORDER = (0, 3, 2, 1)
BF16 = jnp.bfloat16
F32 = jnp.float32


def swap_virt(array, step):
    return lax.ppermute(array, "virt", [(d, d ^ step) for d in range(lax.axis_size("virt"))])


def swap_both(array, step):
    size = lax.axis_size("virt")
    moves = [(c * size + d, (1 - c) * size + (d ^ step)) for c in range(2) for d in range(size)]
    return lax.ppermute(array, ("occj", "virt"), moves)


def swap_core(array):
    return lax.ppermute(array, "occj", [(0, 1), (1, 0)])


def swap_chip(array, step):
    return lax.ppermute(array, "occi", [(d, d ^ step) for d in range(lax.axis_size("occi"))])


def slot(kind, step):
    first = lax.axis_index("occj") if kind == 0 else 1 - lax.axis_index("occj")
    return first, lax.axis_index("occi") ^ step


def keep_rows(mask_ref, first, second, half):
    lane = lax.broadcasted_iota(jnp.int32, (1, SLAB_TILES * TILE), 1) // TILE
    keep = jnp.zeros(lane.shape, F32)
    for tile in range(SLAB_TILES):
        keep = jnp.where(lane == tile, mask_ref[first, half, tile, second].astype(F32), keep)
    return jnp.broadcast_to(keep, (TILE, SLAB_TILES * TILE)).astype(BF16)


def mask_split_kernel(mask_hbm, pair_hbm, amp_hbm, *refs):
    kept_refs, (cross_ref, gate_ref, mask_ref, pair_ref, amp_ref, sems) = refs[:CHIPS], refs[CHIPS:]
    copies = [
        pltpu.make_async_copy(mask_hbm, mask_ref, sems.at[0]),
        pltpu.make_async_copy(pair_hbm, pair_ref, sems.at[1]),
    ]
    firsts, seconds = amp_ref.shape[:2]
    for first in range(firsts):
        for low in range(0, seconds, 2):
            part = first, pl.ds(low, 2)
            copies.append(pltpu.make_async_copy(amp_hbm.at[part], amp_ref.at[part], sems.at[len(copies)]))
    for copy in copies:
        copy.start()
    for copy in copies:
        copy.wait()
    for step in STEPS + (0,):
        for kind in range(2):
            first, second = slot(kind, step)
            gate_ref[kind * CHIPS + step] = jnp.full(gate_ref.shape[1:], pair_ref[first, second].astype(F32))
            for half in range(SLAB_TILES):
                part = slice(half * TILE, (half + 1) * TILE)
                kept = amp_ref[first, second, part] * keep_rows(mask_ref, first, second, half)
                kept_refs[step][kind, part] = kept
                if kind:
                    cross_ref[step, part] = kept


def mask_whole_kernel(mask_ref, pair_ref, amp_ref, kept_ref, gate_ref):
    seconds = amp_ref.shape[1]

    def one(block, carry):
        first, second = block // seconds, block % seconds
        for half in range(SLAB_TILES):
            part = slice(half * TILE, (half + 1) * TILE)
            kept_ref[block, part] = amp_ref[first, second, part] * keep_rows(mask_ref, first, second, half)
        gate_ref[block] = jnp.full(gate_ref.shape[1:], pair_ref[first, second].astype(F32))
        return carry

    lax.fori_loop(0, kept_ref.shape[0], one, 0)


def turn_kernel(chunks, *refs):
    vec_refs, turned_ref, left_ref = refs[:-2], refs[-2], refs[-1]
    slab = turned_ref.shape[1]
    rows = slab * left_ref.shape[0] // (turned_ref.shape[0] * chunks)
    me = lax.axis_index("virt")
    at, low = 0, 0
    for vec_ref in vec_refs:
        for q in range(vec_ref.shape[0]):
            turned_ref[at : at + slab] = vec_ref[q].astype(F32).T.astype(BF16)
            at += slab
            for chunk in range(chunks):
                start = pl.multiple_of((me ^ (2 * chunk)) * rows, rows)
                left_ref[low : low + rows] = vec_ref[q, pl.ds(start, rows), :]
                low += rows


def products(ready, inner_ref, sources, outs):
    turned_ref, left_ref = ready
    slab = turned_ref.shape[1]
    vectors = turned_ref.shape[0] // slab
    height = left_ref.shape[0] // vectors
    rows = height // len(outs[0])
    for base in range(0, len(sources), 2):
        both = [
            (kept.astype(F32) + partner.astype(F32).T).astype(BF16)
            for kept, partner in sources[base : base + 2]
        ]
        inner = jnp.dot(left_ref[...], jnp.concatenate(both, axis=1), preferred_element_type=F32).astype(BF16)
        for n in range(len(both)):
            for q in range(vectors):
                inner_ref[(base + n) * height : (base + n + 1) * height, q * slab : (q + 1) * slab] = inner[
                    q * height : (q + 1) * height, n * slab : (n + 1) * slab
                ]
    half = jnp.dot(inner_ref[...], turned_ref[...], preferred_element_type=F32)
    for n, targets in enumerate(outs):
        for chunk, (ref, index) in enumerate(targets):
            start = n * height + chunk * rows
            ref[index] = half[start : start + rows].astype(ref.dtype)


def first_kernel(*refs):
    ready, (kept_ref, far_ref, got_ref, beside_ref), outs = refs[:2], refs[2:6], refs[6:]
    own_ref, lent_ref, send_ref, inner_ref = outs
    sources = [
        (kept_ref[0], kept_ref[0]),
        (far_ref[0], got_ref[0]),
        (beside_ref[0], kept_ref[1]),
        (beside_ref[ORDER[1]], got_ref[1]),
    ]
    targets = [[(ref, n), (send_ref, at + n)] for at, ref in ((0, own_ref), (2, lent_ref)) for n in range(2)]
    products(ready, inner_ref, sources, targets)


def second_kernel(*refs):
    ready, kept_refs, got_refs, (beside_ref, lent_in, send_in) = refs[:2], refs[2:4], refs[4:6], refs[6:9]
    own_ref, lent_ref, same_ref, cross_ref, inner_ref = refs[9:]
    sources = [(kept[0], got[0]) for kept, got in zip(kept_refs, got_refs)]
    sources += [(beside_ref[step], got[1]) for step, got in zip(ORDER[2:], got_refs)]
    targets = [[(own_ref, n), (same_ref, 2 + n)] for n in range(2)]
    targets += [[(lent_ref, 2 + n), (cross_ref, 2 + n)] for n in range(2)]
    lent_ref[:2] = lent_in[...]
    same_ref[:2] = send_in[:2]
    cross_ref[:2] = send_in[2:]
    products(ready, inner_ref, sources, targets)


def whole_kernel(*refs):
    ready, (kept_ref, partner_ref), part_refs, inner_ref = refs[:2], refs[2:4], refs[4:-1], refs[-1]

    def two(g, carry):
        pairs = [2 * g, 2 * g + 1]
        sources = [(kept_ref[k], partner_ref[k]) for k in pairs]
        products(ready, inner_ref, sources, [[(ref, k) for ref in part_refs] for k in pairs])
        return carry

    lax.fori_loop(0, kept_ref.shape[0] // 2, two, 0)


def finish_kernel(first_ref, second_ref, cross_ref, same_ref, lent_ref, gate_ref, out_ref):
    for n, step in enumerate(ORDER):
        own = first_ref[n] if n < 2 else second_ref[n - 2]
        totals = own + same_ref[n].astype(F32), lent_ref[n].astype(F32) + cross_ref[n].astype(F32)
        for kind, total in enumerate(totals):
            first, second = slot(kind, step)
            gate = gate_ref[kind * CHIPS + step, :1]
            out_ref[first, second] = (total * gate).astype(BF16)


def vmem_specs(count):
    return [pl.BlockSpec(memory_space=pltpu.VMEM)] * count


def shaped(dtype, *shape):
    return jax.ShapeDtypeStruct(shape, dtype)


def kernel(body, outs, operands, spaces=(), scratch=(), flops=0):
    spaces = list(spaces) + [pltpu.VMEM] * (len(operands) - len(spaces))
    return pl.pallas_call(
        body,
        out_shape=outs,
        in_specs=[pl.BlockSpec(memory_space=space) for space in spaces],
        out_specs=vmem_specs(len(outs)),
        scratch_shapes=list(scratch),
        compiler_params=pltpu.CompilerParams(vmem_limit_bytes=24 * 1024 * 1024),
        cost_estimate=pl.CostEstimate(flops=flops, bytes_accessed=1 << 20, transcendentals=0),
    )(*operands)


def shards(amplitudes, vectors, tile_mask, pair_mask):
    firsts, seconds, slab, _ = amplitudes.shape
    pairs = firsts * seconds
    virt, chips, cores = lax.axis_size("virt"), lax.axis_size("occi"), lax.axis_size("occj")
    rows = slab // virt
    chunks = virt // 2
    depth = 2 * vectors.shape[0] * slab
    turned_mask = jnp.transpose(tile_mask, (0, 2, 3, 1))
    gate = shaped(F32, pairs, 8, slab)
    arranged = [shaped(BF16, depth, slab), shaped(BF16, depth // slab * chunks * rows, slab)]
    turn = functools.partial(turn_kernel, chunks)

    def parts(count):
        return [shaped(F32 if chunk == 0 else BF16, count, rows, slab) for chunk in range(chunks)]

    def inner(count):
        return pltpu.VMEM((count * chunks * rows, depth), BF16)

    def sent(part):
        return [part[0]] + [swap_virt(part[chunk], 2 * chunk) for chunk in range(1, chunks)]

    def work(count):
        return 2 * count * depth * slab * slab

    near = swap_virt(vectors, 1)
    if (firsts, seconds, chips, cores, virt) == (2, CHIPS, CHIPS, 2, 4):
        *kept, cross, gates = kernel(
            mask_split_kernel,
            [shaped(BF16, 2, slab, slab)] * CHIPS + [shaped(BF16, CHIPS, slab, slab), gate],
            [
                pltpu.with_memory_space_constraint(array, pltpu.HBM)
                for array in (turned_mask, pair_mask, amplitudes)
            ],
            spaces=[pltpu.HBM] * 3,
            scratch=[
                pltpu.SMEM(turned_mask.shape, jnp.int32),
                pltpu.SMEM(pair_mask.shape, jnp.int32),
                pltpu.VMEM(amplitudes.shape, BF16),
                pltpu.SemaphoreType.DMA((pairs // 2 + 2,)),
            ],
        )
        got = {step: swap_chip(kept[step], step) for step in STEPS}
        beside = swap_core(cross)
        ready = kernel(turn, arranged, (vectors, near))
        _, far, *rest = ORDER
        own_first, lent, sending = kernel(
            first_kernel,
            [shaped(F32, 2, rows, slab), shaped(BF16, 2, rows, slab), shaped(BF16, 4, rows, slab)],
            (*ready, kept[0], kept[far], got[far], beside),
            scratch=[inner(4)],
            flops=work(4),
        )
        own_second, lent, same, crossing = kernel(
            second_kernel,
            [shaped(F32, 2, rows, slab)] + [shaped(BF16, 4, rows, slab)] * 3,
            (*ready, *[kept[step] for step in rest], *[got[step] for step in rest], beside, lent, sending),
            scratch=[inner(4)],
            flops=work(4),
        )
        operands = (own_first, own_second, swap_both(crossing, 2), swap_virt(same, 2), swap_core(lent), gates)
        (out,) = kernel(finish_kernel, [shaped(BF16, firsts, seconds, rows, slab)], operands)
        return out
    kept, gates = kernel(
        mask_whole_kernel,
        [shaped(BF16, pairs, slab, slab), gate],
        (turned_mask, pair_mask, amplitudes),
        spaces=[pltpu.SMEM] * 2,
    )
    partner = lax.all_to_all(kept, ("occj", "occi"), split_axis=0, concat_axis=0, tiled=True)
    ready = kernel(turn, arranged, (vectors, near))
    part = sent(
        kernel(whole_kernel, parts(pairs), (*ready, kept, partner), scratch=[inner(2)], flops=work(pairs))
    )
    summed = part[0]
    for term in part[1:]:
        summed = summed + term.astype(F32)
    return (summed * gates[:, :1]).reshape(firsts, seconds, rows, slab).astype(BF16)


def solution(mesh):
    placed = (
        P("occi", "occj", None, None),
        P("virt", None, None),
        P("occi", "occj", None, None),
        P("occi", "occj"),
    )
    return jax.shard_map(
        shards,
        mesh=mesh,
        in_specs=placed,
        out_specs=P("occi", "occj", "virt", None),
        check_vma=False,
    )
```

```python
import functools

import jax
import jax.numpy as jnp
from jax import lax
from jax.experimental import pallas as pl
from jax.experimental.pallas import tpu as pltpu
from jax.sharding import PartitionSpec as P

TILE = 64
SLAB_TILES = 2
CHIPS = 4
STEPS = (3, 2, 1)
ORDER = (0, 3, 2, 1)
BF16 = jnp.bfloat16
F32 = jnp.float32


def swap_virt(array, step):
    return lax.ppermute(array, "virt", [(d, d ^ step) for d in range(lax.axis_size("virt"))])


def swap_both(array, step):
    size = lax.axis_size("virt")
    moves = [(c * size + d, (1 - c) * size + (d ^ step)) for c in range(2) for d in range(size)]
    return lax.ppermute(array, ("occj", "virt"), moves)


def swap_core(array):
    return lax.ppermute(array, "occj", [(0, 1), (1, 0)])


def swap_chip(array, step):
    return lax.ppermute(array, "occi", [(d, d ^ step) for d in range(lax.axis_size("occi"))])


def slot(kind, step):
    first = lax.axis_index("occj") if kind == 0 else 1 - lax.axis_index("occj")
    return first, lax.axis_index("occi") ^ step


def keep_rows(mask_ref, first, second, half):
    lane = lax.broadcasted_iota(jnp.int32, (1, SLAB_TILES * TILE), 1) // TILE
    keep = jnp.zeros(lane.shape, F32)
    for tile in range(SLAB_TILES):
        keep = jnp.where(lane == tile, mask_ref[first, half, tile, second].astype(F32), keep)
    return jnp.broadcast_to(keep, (TILE, SLAB_TILES * TILE)).astype(BF16)


def mask_split_kernel(mask_hbm, pair_hbm, amp_hbm, *refs):
    kept_refs, (cross_ref, gate_ref, mask_ref, pair_ref, sems) = refs[:CHIPS], refs[CHIPS:]
    copies = [
        pltpu.make_async_copy(mask_hbm, mask_ref, sems.at[0]),
        pltpu.make_async_copy(pair_hbm, pair_ref, sems.at[1]),
    ]
    blocks = []
    for step in STEPS + (0,):
        for kind in range(2):
            first, second = slot(kind, step)
            target = kept_refs[step].at[kind]
            copies.append(pltpu.make_async_copy(amp_hbm.at[first, second], target, sems.at[len(copies)]))
            blocks.append((first, second, target, kind, step, copies[-1]))
    for copy in copies:
        copy.start()
    copies[0].wait()
    copies[1].wait()
    for first, second, target, kind, step, copy in blocks:
        gate_ref[kind * CHIPS + step] = jnp.full(gate_ref.shape[1:], pair_ref[first, second].astype(F32))
        keeps = [keep_rows(mask_ref, first, second, half) for half in range(SLAB_TILES)]
        copy.wait()
        for half, keep in enumerate(keeps):
            part = slice(half * TILE, (half + 1) * TILE)
            kept = target[part] * keep
            target[part] = kept
            if kind:
                cross_ref[step, part] = kept
            elif step == 0:
                cross_ref[CHIPS, part] = kept


def mask_whole_kernel(mask_ref, pair_ref, amp_ref, kept_ref, gate_ref):
    seconds = amp_ref.shape[1]

    def one(block, carry):
        first, second = block // seconds, block % seconds
        for half in range(SLAB_TILES):
            part = slice(half * TILE, (half + 1) * TILE)
            kept_ref[block, part] = amp_ref[first, second, part] * keep_rows(mask_ref, first, second, half)
        gate_ref[block] = jnp.full(gate_ref.shape[1:], pair_ref[first, second].astype(F32))
        return carry

    lax.fori_loop(0, kept_ref.shape[0], one, 0)


def turn_kernel(chunks, *refs):
    vec_refs, turned_ref, left_ref = refs[:-2], refs[-2], refs[-1]
    slab = turned_ref.shape[1]
    rows = slab * left_ref.shape[0] // (turned_ref.shape[0] * chunks)
    me = lax.axis_index("virt")
    at, low = 0, 0
    for vec_ref in vec_refs:
        for q in range(vec_ref.shape[0]):
            turned_ref[at : at + slab] = vec_ref[q].astype(F32).T.astype(BF16)
            at += slab
            for chunk in range(chunks):
                start = pl.multiple_of((me ^ (2 * chunk)) * rows, rows)
                left_ref[low : low + rows] = vec_ref[q, pl.ds(start, rows), :]
                low += rows


def products(ready, inner_ref, sources, outs):
    turned_ref, left_ref = ready
    slab = turned_ref.shape[1]
    vectors = turned_ref.shape[0] // slab
    height = left_ref.shape[0] // vectors
    rows = height // len(outs[0])
    for base in range(0, len(sources), 2):
        both = [
            (kept.astype(F32) + partner.astype(F32).T).astype(BF16)
            for kept, partner in sources[base : base + 2]
        ]
        inner = jnp.dot(left_ref[...], jnp.concatenate(both, axis=1), preferred_element_type=F32).astype(BF16)
        for n in range(len(both)):
            for q in range(vectors):
                inner_ref[(base + n) * height : (base + n + 1) * height, q * slab : (q + 1) * slab] = inner[
                    q * height : (q + 1) * height, n * slab : (n + 1) * slab
                ]
    half = jnp.dot(inner_ref[...], turned_ref[...], preferred_element_type=F32)
    for n, targets in enumerate(outs):
        for chunk, (ref, index) in enumerate(targets):
            start = n * height + chunk * rows
            ref[index] = half[start : start + rows].astype(ref.dtype)


def first_kernel(*refs):
    ready, (kept_ref, far_ref, got_ref, beside_ref), outs = refs[:2], refs[2:6], refs[6:]
    own_ref, lent_ref, send_ref, inner_ref = outs
    sources = [
        (far_ref[0], got_ref[0]),
        (beside_ref[CHIPS], beside_ref[CHIPS]),
        (beside_ref[0], kept_ref[1]),
        (beside_ref[ORDER[1]], got_ref[1]),
    ]
    targets = [[(own_ref, 0), (send_ref, 0)]] + [[(lent_ref, n), (send_ref, 1 + n)] for n in range(3)]
    products(ready, inner_ref, sources, targets)


def second_kernel(*refs):
    ready, kept_refs, got_refs, (beside_ref, lent_in, send_in) = refs[:2], refs[2:4], refs[4:6], refs[6:9]
    own_ref, lent_ref, more_ref, same_ref, cross_ref, inner_ref = refs[9:]
    sources = [(kept[0], got[0]) for kept, got in zip(kept_refs, got_refs)]
    sources += [(beside_ref[step], got[1]) for step, got in zip(ORDER[2:], got_refs)]
    targets = [[(own_ref, n), (same_ref, 1 + n)] for n in range(2)]
    targets += [[(more_ref, n), (cross_ref, 3 + n)] for n in range(2)]
    lent_ref[...] = lent_in[...]
    same_ref[:1] = send_in[:1]
    cross_ref[:3] = send_in[1:]
    products(ready, inner_ref, sources, targets)


def whole_kernel(*refs):
    ready, (kept_ref, partner_ref), part_refs, inner_ref = refs[:2], refs[2:4], refs[4:-1], refs[-1]

    def two(g, carry):
        pairs = [2 * g, 2 * g + 1]
        sources = [(kept_ref[k], partner_ref[k]) for k in pairs]
        products(ready, inner_ref, sources, [[(ref, k) for ref in part_refs] for k in pairs])
        return carry

    lax.fori_loop(0, kept_ref.shape[0] // 2, two, 0)


def finish_kernel(first_ref, second_ref, cross_ref, same_ref, lent_ref, more_ref, gate_ref, out_ref):
    def put(kind, step, total):
        first, second = slot(kind, step)
        out_ref[first, second] = (total * gate_ref[kind * CHIPS + step, :1]).astype(BF16)

    for n, (kind, step) in enumerate([(0, 0)] + [(1, step) for step in ORDER]):
        lent = lent_ref[n] if n < 3 else more_ref[n - 3]
        put(kind, step, lent.astype(F32) + cross_ref[n].astype(F32))
    for n, step in enumerate(ORDER[1:]):
        own = first_ref[0] if n == 0 else second_ref[n - 1]
        put(0, step, own + same_ref[n].astype(F32))


def vmem_specs(count):
    return [pl.BlockSpec(memory_space=pltpu.VMEM)] * count


def shaped(dtype, *shape):
    return jax.ShapeDtypeStruct(shape, dtype)


def kernel(body, outs, operands, spaces=(), scratch=(), flops=0):
    spaces = list(spaces) + [pltpu.VMEM] * (len(operands) - len(spaces))
    return pl.pallas_call(
        body,
        out_shape=outs,
        in_specs=[pl.BlockSpec(memory_space=space) for space in spaces],
        out_specs=vmem_specs(len(outs)),
        scratch_shapes=list(scratch),
        compiler_params=pltpu.CompilerParams(vmem_limit_bytes=24 * 1024 * 1024),
        cost_estimate=pl.CostEstimate(flops=flops, bytes_accessed=1 << 20, transcendentals=0),
    )(*operands)


def shards(amplitudes, vectors, tile_mask, pair_mask):
    firsts, seconds, slab, _ = amplitudes.shape
    pairs = firsts * seconds
    virt, chips, cores = lax.axis_size("virt"), lax.axis_size("occi"), lax.axis_size("occj")
    rows = slab // virt
    chunks = virt // 2
    depth = 2 * vectors.shape[0] * slab
    turned_mask = jnp.transpose(tile_mask, (0, 2, 3, 1))
    gate = shaped(F32, pairs, 8, slab)
    arranged = [shaped(BF16, depth, slab), shaped(BF16, depth // slab * chunks * rows, slab)]
    turn = functools.partial(turn_kernel, chunks)

    def parts(count):
        return [shaped(F32 if chunk == 0 else BF16, count, rows, slab) for chunk in range(chunks)]

    def inner(count):
        return pltpu.VMEM((count * chunks * rows, depth), BF16)

    def sent(part):
        return [part[0]] + [swap_virt(part[chunk], 2 * chunk) for chunk in range(1, chunks)]

    def work(count):
        return 2 * count * depth * slab * slab

    near = swap_virt(vectors, 1)
    if (firsts, seconds, chips, cores, virt) == (2, CHIPS, CHIPS, 2, 4):
        *kept, cross, gates = kernel(
            mask_split_kernel,
            [shaped(BF16, 2, slab, slab)] * CHIPS + [shaped(BF16, CHIPS + 1, slab, slab), gate],
            [
                pltpu.with_memory_space_constraint(array, pltpu.HBM)
                for array in (turned_mask, pair_mask, amplitudes)
            ],
            spaces=[pltpu.HBM] * 3,
            scratch=[
                pltpu.SMEM(turned_mask.shape, jnp.int32),
                pltpu.SMEM(pair_mask.shape, jnp.int32),
                pltpu.SemaphoreType.DMA((pairs + 2,)),
            ],
        )
        got = {step: swap_chip(kept[step], step) for step in STEPS}
        beside = swap_core(cross)
        ready = kernel(turn, arranged, (vectors, near))
        _, far, *rest = ORDER
        own_first, lent, sending = kernel(
            first_kernel,
            [shaped(F32, 1, rows, slab), shaped(BF16, 3, rows, slab), shaped(BF16, 4, rows, slab)],
            (*ready, kept[0], kept[far], got[far], beside),
            scratch=[inner(4)],
            flops=work(4),
        )
        own_second, lent, more, same, crossing = kernel(
            second_kernel,
            [shaped(F32, 2, rows, slab)] + [shaped(BF16, count, rows, slab) for count in (3, 2, 3, 5)],
            (*ready, *[kept[step] for step in rest], *[got[step] for step in rest], beside, lent, sending),
            scratch=[inner(4)],
            flops=work(4),
        )
        operands = (own_first, own_second, swap_both(crossing, 2), swap_virt(same, 2), swap_core(lent), swap_core(more), gates)
        (out,) = kernel(finish_kernel, [shaped(BF16, firsts, seconds, rows, slab)], operands)
        return out
    kept, gates = kernel(
        mask_whole_kernel,
        [shaped(BF16, pairs, slab, slab), gate],
        (turned_mask, pair_mask, amplitudes),
        spaces=[pltpu.SMEM] * 2,
    )
    partner = lax.all_to_all(kept, ("occj", "occi"), split_axis=0, concat_axis=0, tiled=True)
    ready = kernel(turn, arranged, (vectors, near))
    part = sent(
        kernel(whole_kernel, parts(pairs), (*ready, kept, partner), scratch=[inner(2)], flops=work(pairs))
    )
    summed = part[0]
    for term in part[1:]:
        summed = summed + term.astype(F32)
    return (summed * gates[:, :1]).reshape(firsts, seconds, rows, slab).astype(BF16)


def solution(mesh):
    placed = (
        P("occi", "occj", None, None),
        P("virt", None, None),
        P("occi", "occj", None, None),
        P("occi", "occj"),
    )
    return jax.shard_map(
        shards,
        mesh=mesh,
        in_specs=placed,
        out_specs=P("occi", "occj", "virt", None),
        check_vma=False,
    )
```

```python
import functools

import jax
import jax.numpy as jnp
from jax import lax
from jax.experimental import pallas as pl
from jax.experimental.pallas import tpu as pltpu
from jax.sharding import PartitionSpec as P

TILE = 64
SLAB_TILES = 2
CHIPS = 4
STEPS = (3, 2, 1)
ORDER = (0, 3, 2, 1)
BF16 = jnp.bfloat16
F32 = jnp.float32


def swap_virt(array, step):
    return lax.ppermute(array, "virt", [(d, d ^ step) for d in range(lax.axis_size("virt"))])


def swap_both(array, step):
    size = lax.axis_size("virt")
    moves = [(c * size + d, (1 - c) * size + (d ^ step)) for c in range(2) for d in range(size)]
    return lax.ppermute(array, ("occj", "virt"), moves)


def swap_core(array):
    return lax.ppermute(array, "occj", [(0, 1), (1, 0)])


def swap_chip(array, step):
    return lax.ppermute(array, "occi", [(d, d ^ step) for d in range(lax.axis_size("occi"))])


def slot(kind, step):
    first = lax.axis_index("occj") if kind == 0 else 1 - lax.axis_index("occj")
    return first, lax.axis_index("occi") ^ step


def keep_rows(mask_ref, first, second, half):
    lane = lax.broadcasted_iota(jnp.int32, (1, SLAB_TILES * TILE), 1) // TILE
    keep = jnp.zeros(lane.shape, F32)
    for tile in range(SLAB_TILES):
        keep = jnp.where(lane == tile, mask_ref[first, half, tile, second].astype(F32), keep)
    return jnp.broadcast_to(keep, (TILE, SLAB_TILES * TILE)).astype(BF16)


def mask_split_kernel(mask_hbm, pair_hbm, amp_hbm, *refs):
    kept_refs, (cross_ref, gate_ref, mask_ref, pair_ref, sems) = refs[:CHIPS], refs[CHIPS:]
    copies = [
        pltpu.make_async_copy(mask_hbm, mask_ref, sems.at[0]),
        pltpu.make_async_copy(pair_hbm, pair_ref, sems.at[1]),
    ]
    blocks = []
    for step in STEPS + (0,):
        for kind in range(2):
            first, second = slot(kind, step)
            for half in range(SLAB_TILES):
                part = pl.ds(half * TILE, TILE)
                source, target = amp_hbm.at[first, second, part], kept_refs[step].at[kind, part]
                copies.append(pltpu.make_async_copy(source, target, sems.at[len(copies)]))
                blocks.append((first, second, target, kind, step, half, copies[-1]))
    for copy in copies:
        copy.start()
    copies[0].wait()
    copies[1].wait()
    for first, second, target, kind, step, half, copy in blocks:
        if half == 0:
            gate_ref[kind * CHIPS + step] = jnp.full(gate_ref.shape[1:], pair_ref[first, second].astype(F32))
        keep = keep_rows(mask_ref, first, second, half)
        copy.wait()
        kept = target[...] * keep
        target[...] = kept
        part = slice(half * TILE, (half + 1) * TILE)
        if kind:
            cross_ref[step, part] = kept
        elif step == 0:
            cross_ref[CHIPS, part] = kept


def mask_whole_kernel(mask_ref, pair_ref, amp_ref, kept_ref, gate_ref):
    seconds = amp_ref.shape[1]

    def one(block, carry):
        first, second = block // seconds, block % seconds
        for half in range(SLAB_TILES):
            part = slice(half * TILE, (half + 1) * TILE)
            kept_ref[block, part] = amp_ref[first, second, part] * keep_rows(mask_ref, first, second, half)
        gate_ref[block] = jnp.full(gate_ref.shape[1:], pair_ref[first, second].astype(F32))
        return carry

    lax.fori_loop(0, kept_ref.shape[0], one, 0)


def turn_kernel(chunks, *refs):
    vec_refs, turned_ref, left_ref = refs[:-2], refs[-2], refs[-1]
    slab = turned_ref.shape[1]
    rows = slab * left_ref.shape[0] // (turned_ref.shape[0] * chunks)
    me = lax.axis_index("virt")
    at, low = 0, 0
    for vec_ref in vec_refs:
        for q in range(vec_ref.shape[0]):
            turned_ref[at : at + slab] = vec_ref[q].astype(F32).T.astype(BF16)
            at += slab
            for chunk in range(chunks):
                start = pl.multiple_of((me ^ (2 * chunk)) * rows, rows)
                left_ref[low : low + rows] = vec_ref[q, pl.ds(start, rows), :]
                low += rows


def products(ready, inner_ref, sources, outs):
    turned_ref, left_ref = ready
    slab = turned_ref.shape[1]
    vectors = turned_ref.shape[0] // slab
    height = left_ref.shape[0] // vectors
    rows = height // len(outs[0])
    for base in range(0, len(sources), 2):
        both = [
            (kept.astype(F32) + partner.astype(F32).T).astype(BF16)
            for kept, partner in sources[base : base + 2]
        ]
        inner = jnp.dot(left_ref[...], jnp.concatenate(both, axis=1), preferred_element_type=F32).astype(BF16)
        for n in range(len(both)):
            for q in range(vectors):
                inner_ref[(base + n) * height : (base + n + 1) * height, q * slab : (q + 1) * slab] = inner[
                    q * height : (q + 1) * height, n * slab : (n + 1) * slab
                ]
    half = jnp.dot(inner_ref[...], turned_ref[...], preferred_element_type=F32)
    for n, targets in enumerate(outs):
        for chunk, (ref, index) in enumerate(targets):
            start = n * height + chunk * rows
            ref[index] = half[start : start + rows].astype(ref.dtype)


def first_kernel(*refs):
    ready, (kept_ref, far_ref, got_ref, beside_ref), outs = refs[:2], refs[2:6], refs[6:]
    own_ref, lent_ref, send_ref, inner_ref = outs
    sources = [
        (far_ref[0], got_ref[0]),
        (beside_ref[CHIPS], beside_ref[CHIPS]),
        (beside_ref[0], kept_ref[1]),
        (beside_ref[ORDER[1]], got_ref[1]),
    ]
    targets = [[(own_ref, 0), (send_ref, 0)]] + [[(lent_ref, n), (send_ref, 1 + n)] for n in range(3)]
    products(ready, inner_ref, sources, targets)


def second_kernel(*refs):
    ready, kept_refs, got_refs, (beside_ref, lent_in, send_in) = refs[:2], refs[2:4], refs[4:6], refs[6:9]
    own_ref, lent_ref, more_ref, same_ref, cross_ref, inner_ref = refs[9:]
    sources = [(kept[0], got[0]) for kept, got in zip(kept_refs, got_refs)]
    sources += [(beside_ref[step], got[1]) for step, got in zip(ORDER[2:], got_refs)]
    targets = [[(own_ref, n), (same_ref, 1 + n)] for n in range(2)]
    targets += [[(more_ref, n), (cross_ref, 3 + n)] for n in range(2)]
    lent_ref[...] = lent_in[...]
    same_ref[:1] = send_in[:1]
    cross_ref[:3] = send_in[1:]
    products(ready, inner_ref, sources, targets)


def whole_kernel(*refs):
    ready, (kept_ref, partner_ref), part_refs, inner_ref = refs[:2], refs[2:4], refs[4:-1], refs[-1]

    def two(g, carry):
        pairs = [2 * g, 2 * g + 1]
        sources = [(kept_ref[k], partner_ref[k]) for k in pairs]
        products(ready, inner_ref, sources, [[(ref, k) for ref in part_refs] for k in pairs])
        return carry

    lax.fori_loop(0, kept_ref.shape[0] // 2, two, 0)


def finish_kernel(first_ref, second_ref, cross_ref, same_ref, lent_ref, more_ref, gate_ref, out_ref):
    def put(kind, step, total):
        first, second = slot(kind, step)
        out_ref[first, second] = (total * gate_ref[kind * CHIPS + step, :1]).astype(BF16)

    for n, (kind, step) in enumerate([(0, 0)] + [(1, step) for step in ORDER]):
        lent = lent_ref[n] if n < 3 else more_ref[n - 3]
        put(kind, step, lent.astype(F32) + cross_ref[n].astype(F32))
    for n, step in enumerate(ORDER[1:]):
        own = first_ref[0] if n == 0 else second_ref[n - 1]
        put(0, step, own + same_ref[n].astype(F32))


def vmem_specs(count):
    return [pl.BlockSpec(memory_space=pltpu.VMEM)] * count


def shaped(dtype, *shape):
    return jax.ShapeDtypeStruct(shape, dtype)


def kernel(body, outs, operands, spaces=(), scratch=(), flops=0):
    spaces = list(spaces) + [pltpu.VMEM] * (len(operands) - len(spaces))
    return pl.pallas_call(
        body,
        out_shape=outs,
        in_specs=[pl.BlockSpec(memory_space=space) for space in spaces],
        out_specs=vmem_specs(len(outs)),
        scratch_shapes=list(scratch),
        compiler_params=pltpu.CompilerParams(vmem_limit_bytes=24 * 1024 * 1024),
        cost_estimate=pl.CostEstimate(flops=flops, bytes_accessed=1 << 20, transcendentals=0),
    )(*operands)


def shards(amplitudes, vectors, tile_mask, pair_mask):
    firsts, seconds, slab, _ = amplitudes.shape
    pairs = firsts * seconds
    virt, chips, cores = lax.axis_size("virt"), lax.axis_size("occi"), lax.axis_size("occj")
    rows = slab // virt
    chunks = virt // 2
    depth = 2 * vectors.shape[0] * slab
    turned_mask = jnp.transpose(tile_mask, (0, 2, 3, 1))
    gate = shaped(F32, pairs, 8, slab)
    arranged = [shaped(BF16, depth, slab), shaped(BF16, depth // slab * chunks * rows, slab)]
    turn = functools.partial(turn_kernel, chunks)

    def parts(count):
        return [shaped(F32 if chunk == 0 else BF16, count, rows, slab) for chunk in range(chunks)]

    def inner(count):
        return pltpu.VMEM((count * chunks * rows, depth), BF16)

    def sent(part):
        return [part[0]] + [swap_virt(part[chunk], 2 * chunk) for chunk in range(1, chunks)]

    def work(count):
        return 2 * count * depth * slab * slab

    near = swap_virt(vectors, 1)
    if (firsts, seconds, chips, cores, virt) == (2, CHIPS, CHIPS, 2, 4):
        *kept, cross, gates = kernel(
            mask_split_kernel,
            [shaped(BF16, 2, slab, slab)] * CHIPS + [shaped(BF16, CHIPS + 1, slab, slab), gate],
            [
                pltpu.with_memory_space_constraint(array, pltpu.HBM)
                for array in (turned_mask, pair_mask, amplitudes)
            ],
            spaces=[pltpu.HBM] * 3,
            scratch=[
                pltpu.SMEM(turned_mask.shape, jnp.int32),
                pltpu.SMEM(pair_mask.shape, jnp.int32),
                pltpu.SemaphoreType.DMA((SLAB_TILES * pairs + 2,)),
            ],
        )
        got = {step: swap_chip(kept[step], step) for step in STEPS}
        beside = swap_core(cross)
        ready = kernel(turn, arranged, (vectors, near))
        _, far, *rest = ORDER
        own_first, lent, sending = kernel(
            first_kernel,
            [shaped(F32, 1, rows, slab), shaped(BF16, 3, rows, slab), shaped(BF16, 4, rows, slab)],
            (*ready, kept[0], kept[far], got[far], beside),
            scratch=[inner(4)],
            flops=work(4),
        )
        own_second, lent, more, same, crossing = kernel(
            second_kernel,
            [shaped(F32, 2, rows, slab)] + [shaped(BF16, count, rows, slab) for count in (3, 2, 3, 5)],
            (*ready, *[kept[step] for step in rest], *[got[step] for step in rest], beside, lent, sending),
            scratch=[inner(4)],
            flops=work(4),
        )
        operands = (own_first, own_second, swap_both(crossing, 2), swap_virt(same, 2), swap_core(lent), swap_core(more), gates)
        (out,) = kernel(finish_kernel, [shaped(BF16, firsts, seconds, rows, slab)], operands)
        return out
    kept, gates = kernel(
        mask_whole_kernel,
        [shaped(BF16, pairs, slab, slab), gate],
        (turned_mask, pair_mask, amplitudes),
        spaces=[pltpu.SMEM] * 2,
    )
    partner = lax.all_to_all(kept, ("occj", "occi"), split_axis=0, concat_axis=0, tiled=True)
    ready = kernel(turn, arranged, (vectors, near))
    part = sent(
        kernel(whole_kernel, parts(pairs), (*ready, kept, partner), scratch=[inner(2)], flops=work(pairs))
    )
    summed = part[0]
    for term in part[1:]:
        summed = summed + term.astype(F32)
    return (summed * gates[:, :1]).reshape(firsts, seconds, rows, slab).astype(BF16)


def solution(mesh):
    placed = (
        P("occi", "occj", None, None),
        P("virt", None, None),
        P("occi", "occj", None, None),
        P("occi", "occj"),
    )
    return jax.shard_map(
        shards,
        mesh=mesh,
        in_specs=placed,
        out_specs=P("occi", "occj", "virt", None),
        check_vma=False,
    )
```

```python
import functools

import jax
import jax.numpy as jnp
from jax import lax
from jax.experimental import pallas as pl
from jax.experimental.pallas import tpu as pltpu
from jax.sharding import PartitionSpec as P

TILE = 64
SLAB_TILES = 2
CHIPS = 4
STEPS = (3, 2, 1)
ORDER = (0, 3, 2, 1)
BF16 = jnp.bfloat16
F32 = jnp.float32


def swap_virt(array, step):
    return lax.ppermute(array, "virt", [(d, d ^ step) for d in range(lax.axis_size("virt"))])


def swap_both(array, step):
    size = lax.axis_size("virt")
    moves = [(c * size + d, (1 - c) * size + (d ^ step)) for c in range(2) for d in range(size)]
    return lax.ppermute(array, ("occj", "virt"), moves)


def swap_core(array):
    return lax.ppermute(array, "occj", [(0, 1), (1, 0)])


def swap_chip(array, step):
    return lax.ppermute(array, "occi", [(d, d ^ step) for d in range(lax.axis_size("occi"))])


def slot(kind, step):
    first = lax.axis_index("occj") if kind == 0 else 1 - lax.axis_index("occj")
    return first, lax.axis_index("occi") ^ step


def keep_rows(mask_ref, first, second, half):
    lane = lax.broadcasted_iota(jnp.int32, (1, SLAB_TILES * TILE), 1) // TILE
    keep = jnp.zeros(lane.shape, F32)
    for tile in range(SLAB_TILES):
        keep = jnp.where(lane == tile, mask_ref[first, half, tile, second].astype(F32), keep)
    return jnp.broadcast_to(keep, (16, SLAB_TILES * TILE)).astype(BF16)


def masked_rows(block, keep):
    return (block.reshape(TILE // 16, 16, block.shape[1]) * keep[None]).reshape(block.shape)


def mask_split_kernel(mask_hbm, pair_hbm, amp_hbm, *refs):
    kept_refs, (cross_ref, gate_ref, mask_ref, pair_ref, sems) = refs[:CHIPS], refs[CHIPS:]
    copies = [
        pltpu.make_async_copy(mask_hbm, mask_ref, sems.at[0]),
        pltpu.make_async_copy(pair_hbm, pair_ref, sems.at[1]),
    ]
    blocks = []
    for step in STEPS + (0,):
        for kind in range(2):
            first, second = slot(kind, step)
            target = kept_refs[step].at[kind]
            copies.append(pltpu.make_async_copy(amp_hbm.at[first, second], target, sems.at[len(copies)]))
            blocks.append((first, second, target, kind, step, copies[-1]))
    for copy in copies:
        copy.start()
    copies[0].wait()
    copies[1].wait()
    for first, second, target, kind, step, copy in blocks:
        gate_ref[kind * CHIPS + step] = jnp.full(gate_ref.shape[1:], pair_ref[first, second].astype(F32))
        keeps = [keep_rows(mask_ref, first, second, half) for half in range(SLAB_TILES)]
        copy.wait()
        for half, keep in enumerate(keeps):
            part = slice(half * TILE, (half + 1) * TILE)
            kept = masked_rows(target[part], keep)
            target[part] = kept
            if kind:
                cross_ref[step, part] = kept
            elif step == 0:
                cross_ref[CHIPS, part] = kept


def mask_whole_kernel(mask_ref, pair_ref, amp_ref, kept_ref, gate_ref):
    seconds = amp_ref.shape[1]

    def one(block, carry):
        first, second = block // seconds, block % seconds
        for half in range(SLAB_TILES):
            part = slice(half * TILE, (half + 1) * TILE)
            kept_ref[block, part] = masked_rows(amp_ref[first, second, part], keep_rows(mask_ref, first, second, half))
        gate_ref[block] = jnp.full(gate_ref.shape[1:], pair_ref[first, second].astype(F32))
        return carry

    lax.fori_loop(0, kept_ref.shape[0], one, 0)


def turn_kernel(chunks, *refs):
    vec_refs, turned_ref, left_ref = refs[:-2], refs[-2], refs[-1]
    slab = turned_ref.shape[1]
    rows = slab * left_ref.shape[0] // (turned_ref.shape[0] * chunks)
    me = lax.axis_index("virt")
    at, low = 0, 0
    for vec_ref in vec_refs:
        for q in range(vec_ref.shape[0]):
            turned_ref[at : at + slab] = vec_ref[q].astype(F32).T.astype(BF16)
            at += slab
            for chunk in range(chunks):
                start = pl.multiple_of((me ^ (2 * chunk)) * rows, rows)
                left_ref[low : low + rows] = vec_ref[q, pl.ds(start, rows), :]
                low += rows


def products(ready, inner_ref, sources, outs):
    turned_ref, left_ref = ready
    slab = turned_ref.shape[1]
    vectors = turned_ref.shape[0] // slab
    height = left_ref.shape[0] // vectors
    rows = height // len(outs[0])
    for base in range(0, len(sources), 2):
        both = [
            (kept.astype(F32) + partner.astype(F32).T).astype(BF16)
            for kept, partner in sources[base : base + 2]
        ]
        inner = jnp.dot(left_ref[...], jnp.concatenate(both, axis=1), preferred_element_type=F32).astype(BF16)
        for n in range(len(both)):
            for q in range(vectors):
                inner_ref[(base + n) * height : (base + n + 1) * height, q * slab : (q + 1) * slab] = inner[
                    q * height : (q + 1) * height, n * slab : (n + 1) * slab
                ]
    half = jnp.dot(inner_ref[...], turned_ref[...], preferred_element_type=F32)
    for n, targets in enumerate(outs):
        for chunk, (ref, index) in enumerate(targets):
            start = n * height + chunk * rows
            ref[index] = half[start : start + rows].astype(ref.dtype)


def first_kernel(*refs):
    ready, (kept_ref, far_ref, got_ref, beside_ref), outs = refs[:2], refs[2:6], refs[6:]
    own_ref, lent_ref, send_ref, inner_ref = outs
    sources = [
        (far_ref[0], got_ref[0]),
        (beside_ref[CHIPS], beside_ref[CHIPS]),
        (beside_ref[0], kept_ref[1]),
        (beside_ref[ORDER[1]], got_ref[1]),
    ]
    targets = [[(own_ref, 0), (send_ref, 0)]] + [[(lent_ref, n), (send_ref, 1 + n)] for n in range(3)]
    products(ready, inner_ref, sources, targets)


def second_kernel(*refs):
    ready, kept_refs, got_refs, (beside_ref, lent_in, send_in) = refs[:2], refs[2:4], refs[4:6], refs[6:9]
    own_ref, lent_ref, more_ref, same_ref, cross_ref, inner_ref = refs[9:]
    sources = [(kept[0], got[0]) for kept, got in zip(kept_refs, got_refs)]
    sources += [(beside_ref[step], got[1]) for step, got in zip(ORDER[2:], got_refs)]
    targets = [[(own_ref, n), (same_ref, 1 + n)] for n in range(2)]
    targets += [[(more_ref, n), (cross_ref, 3 + n)] for n in range(2)]
    lent_ref[...] = lent_in[...]
    same_ref[:1] = send_in[:1]
    cross_ref[:3] = send_in[1:]
    products(ready, inner_ref, sources, targets)


def whole_kernel(*refs):
    ready, (kept_ref, partner_ref), part_refs, inner_ref = refs[:2], refs[2:4], refs[4:-1], refs[-1]

    def two(g, carry):
        pairs = [2 * g, 2 * g + 1]
        sources = [(kept_ref[k], partner_ref[k]) for k in pairs]
        products(ready, inner_ref, sources, [[(ref, k) for ref in part_refs] for k in pairs])
        return carry

    lax.fori_loop(0, kept_ref.shape[0] // 2, two, 0)


def finish_kernel(first_ref, second_ref, cross_ref, same_ref, lent_ref, more_ref, gate_ref, out_ref):
    def put(kind, step, total):
        first, second = slot(kind, step)
        out_ref[first, second] = (total * gate_ref[kind * CHIPS + step, :1]).astype(BF16)

    for n, (kind, step) in enumerate([(0, 0)] + [(1, step) for step in ORDER]):
        lent = lent_ref[n] if n < 3 else more_ref[n - 3]
        put(kind, step, lent.astype(F32) + cross_ref[n].astype(F32))
    for n, step in enumerate(ORDER[1:]):
        own = first_ref[0] if n == 0 else second_ref[n - 1]
        put(0, step, own + same_ref[n].astype(F32))


def vmem_specs(count):
    return [pl.BlockSpec(memory_space=pltpu.VMEM)] * count


def shaped(dtype, *shape):
    return jax.ShapeDtypeStruct(shape, dtype)


def kernel(body, outs, operands, spaces=(), scratch=(), flops=0):
    spaces = list(spaces) + [pltpu.VMEM] * (len(operands) - len(spaces))
    return pl.pallas_call(
        body,
        out_shape=outs,
        in_specs=[pl.BlockSpec(memory_space=space) for space in spaces],
        out_specs=vmem_specs(len(outs)),
        scratch_shapes=list(scratch),
        compiler_params=pltpu.CompilerParams(vmem_limit_bytes=24 * 1024 * 1024),
        cost_estimate=pl.CostEstimate(flops=flops, bytes_accessed=1 << 20, transcendentals=0),
    )(*operands)


def shards(amplitudes, vectors, tile_mask, pair_mask):
    firsts, seconds, slab, _ = amplitudes.shape
    pairs = firsts * seconds
    virt, chips, cores = lax.axis_size("virt"), lax.axis_size("occi"), lax.axis_size("occj")
    rows = slab // virt
    chunks = virt // 2
    depth = 2 * vectors.shape[0] * slab
    turned_mask = jnp.transpose(tile_mask, (0, 2, 3, 1))
    gate = shaped(F32, pairs, 8, slab)
    arranged = [shaped(BF16, depth, slab), shaped(BF16, depth // slab * chunks * rows, slab)]
    turn = functools.partial(turn_kernel, chunks)

    def parts(count):
        return [shaped(F32 if chunk == 0 else BF16, count, rows, slab) for chunk in range(chunks)]

    def inner(count):
        return pltpu.VMEM((count * chunks * rows, depth), BF16)

    def sent(part):
        return [part[0]] + [swap_virt(part[chunk], 2 * chunk) for chunk in range(1, chunks)]

    def work(count):
        return 2 * count * depth * slab * slab

    near = swap_virt(vectors, 1)
    if (firsts, seconds, chips, cores, virt) == (2, CHIPS, CHIPS, 2, 4):
        *kept, cross, gates = kernel(
            mask_split_kernel,
            [shaped(BF16, 2, slab, slab)] * CHIPS + [shaped(BF16, CHIPS + 1, slab, slab), gate],
            [
                pltpu.with_memory_space_constraint(array, pltpu.HBM)
                for array in (turned_mask, pair_mask, amplitudes)
            ],
            spaces=[pltpu.HBM] * 3,
            scratch=[
                pltpu.SMEM(turned_mask.shape, jnp.int32),
                pltpu.SMEM(pair_mask.shape, jnp.int32),
                pltpu.SemaphoreType.DMA((pairs + 2,)),
            ],
        )
        got = {step: swap_chip(kept[step], step) for step in STEPS}
        beside = swap_core(cross)
        ready = kernel(turn, arranged, (vectors, near))
        _, far, *rest = ORDER
        own_first, lent, sending = kernel(
            first_kernel,
            [shaped(F32, 1, rows, slab), shaped(BF16, 3, rows, slab), shaped(BF16, 4, rows, slab)],
            (*ready, kept[0], kept[far], got[far], beside),
            scratch=[inner(4)],
            flops=work(4),
        )
        own_second, lent, more, same, crossing = kernel(
            second_kernel,
            [shaped(F32, 2, rows, slab)] + [shaped(BF16, count, rows, slab) for count in (3, 2, 3, 5)],
            (*ready, *[kept[step] for step in rest], *[got[step] for step in rest], beside, lent, sending),
            scratch=[inner(4)],
            flops=work(4),
        )
        operands = (own_first, own_second, swap_both(crossing, 2), swap_virt(same, 2), swap_core(lent), swap_core(more), gates)
        (out,) = kernel(finish_kernel, [shaped(BF16, firsts, seconds, rows, slab)], operands)
        return out
    kept, gates = kernel(
        mask_whole_kernel,
        [shaped(BF16, pairs, slab, slab), gate],
        (turned_mask, pair_mask, amplitudes),
        spaces=[pltpu.SMEM] * 2,
    )
    partner = lax.all_to_all(kept, ("occj", "occi"), split_axis=0, concat_axis=0, tiled=True)
    ready = kernel(turn, arranged, (vectors, near))
    part = sent(
        kernel(whole_kernel, parts(pairs), (*ready, kept, partner), scratch=[inner(2)], flops=work(pairs))
    )
    summed = part[0]
    for term in part[1:]:
        summed = summed + term.astype(F32)
    return (summed * gates[:, :1]).reshape(firsts, seconds, rows, slab).astype(BF16)


def solution(mesh):
    placed = (
        P("occi", "occj", None, None),
        P("virt", None, None),
        P("occi", "occj", None, None),
        P("occi", "occj"),
    )
    return jax.shard_map(
        shards,
        mesh=mesh,
        in_specs=placed,
        out_specs=P("occi", "occj", "virt", None),
        check_vma=False,
    )
```

```python
import functools

import jax
import jax.numpy as jnp
from jax import lax
from jax.experimental import pallas as pl
from jax.experimental.pallas import tpu as pltpu
from jax.sharding import PartitionSpec as P

TILE = 64
SLAB_TILES = 2
CHIPS = 4
STEPS = (3, 1, 2)
ORDER = (0, 3, 1, 2)
BF16 = jnp.bfloat16
F32 = jnp.float32


def swap_virt(array, step):
    return lax.ppermute(array, "virt", [(d, d ^ step) for d in range(lax.axis_size("virt"))])


def swap_both(array, step):
    size = lax.axis_size("virt")
    moves = [(c * size + d, (1 - c) * size + (d ^ step)) for c in range(2) for d in range(size)]
    return lax.ppermute(array, ("occj", "virt"), moves)


def swap_core(array):
    return lax.ppermute(array, "occj", [(0, 1), (1, 0)])


def swap_chip(array, step):
    return lax.ppermute(array, "occi", [(d, d ^ step) for d in range(lax.axis_size("occi"))])


def slot(kind, step):
    first = lax.axis_index("occj") if kind == 0 else 1 - lax.axis_index("occj")
    return first, lax.axis_index("occi") ^ step


def keep_rows(mask_ref, first, second, half):
    lane = lax.broadcasted_iota(jnp.int32, (1, SLAB_TILES * TILE), 1) // TILE
    keep = jnp.zeros(lane.shape, F32)
    for tile in range(SLAB_TILES):
        keep = jnp.where(lane == tile, mask_ref[first, half, tile, second].astype(F32), keep)
    return jnp.broadcast_to(keep, (16, SLAB_TILES * TILE)).astype(BF16)


def masked_rows(block, keep):
    return (block.reshape(TILE // 16, 16, block.shape[1]) * keep[None]).reshape(block.shape)


def mask_split_kernel(mask_hbm, pair_hbm, amp_hbm, *refs):
    kept_refs, (cross_ref, gate_ref, mask_ref, pair_ref, sems) = refs[:CHIPS], refs[CHIPS:]
    copies = [
        pltpu.make_async_copy(mask_hbm, mask_ref, sems.at[0]),
        pltpu.make_async_copy(pair_hbm, pair_ref, sems.at[1]),
    ]
    blocks = []
    for step in STEPS + (0,):
        for kind in range(2):
            first, second = slot(kind, step)
            target = kept_refs[step].at[kind]
            copies.append(pltpu.make_async_copy(amp_hbm.at[first, second], target, sems.at[len(copies)]))
            blocks.append((first, second, target, kind, step, copies[-1]))
    for copy in copies:
        copy.start()
    copies[0].wait()
    copies[1].wait()
    for first, second, target, kind, step, copy in blocks:
        gate_ref[kind * CHIPS + step] = jnp.full(gate_ref.shape[1:], pair_ref[first, second].astype(F32))
        keeps = [keep_rows(mask_ref, first, second, half) for half in range(SLAB_TILES)]
        copy.wait()
        for half, keep in enumerate(keeps):
            part = slice(half * TILE, (half + 1) * TILE)
            kept = masked_rows(target[part], keep)
            target[part] = kept
            if kind:
                cross_ref[step, part] = kept
            elif step == 0:
                cross_ref[CHIPS, part] = kept


def mask_whole_kernel(mask_ref, pair_ref, amp_ref, kept_ref, gate_ref):
    seconds = amp_ref.shape[1]

    def one(block, carry):
        first, second = block // seconds, block % seconds
        for half in range(SLAB_TILES):
            part = slice(half * TILE, (half + 1) * TILE)
            kept_ref[block, part] = masked_rows(amp_ref[first, second, part], keep_rows(mask_ref, first, second, half))
        gate_ref[block] = jnp.full(gate_ref.shape[1:], pair_ref[first, second].astype(F32))
        return carry

    lax.fori_loop(0, kept_ref.shape[0], one, 0)


def turn_kernel(chunks, *refs):
    vec_refs, turned_ref, left_ref = refs[:-2], refs[-2], refs[-1]
    slab = turned_ref.shape[1]
    rows = slab * left_ref.shape[0] // (turned_ref.shape[0] * chunks)
    me = lax.axis_index("virt")
    at, low = 0, 0
    for vec_ref in vec_refs:
        for q in range(vec_ref.shape[0]):
            turned_ref[at : at + slab] = vec_ref[q].astype(F32).T.astype(BF16)
            at += slab
            for chunk in range(chunks):
                start = pl.multiple_of((me ^ (2 * chunk)) * rows, rows)
                left_ref[low : low + rows] = vec_ref[q, pl.ds(start, rows), :]
                low += rows


def products(ready, inner_ref, sources, outs):
    turned_ref, left_ref = ready
    slab = turned_ref.shape[1]
    vectors = turned_ref.shape[0] // slab
    height = left_ref.shape[0] // vectors
    rows = height // len(outs[0])
    for base in range(0, len(sources), 2):
        both = [
            (kept.astype(F32) + partner.astype(F32).T).astype(BF16)
            for kept, partner in sources[base : base + 2]
        ]
        inner = jnp.dot(left_ref[...], jnp.concatenate(both, axis=1), preferred_element_type=F32).astype(BF16)
        for n in range(len(both)):
            for q in range(vectors):
                inner_ref[(base + n) * height : (base + n + 1) * height, q * slab : (q + 1) * slab] = inner[
                    q * height : (q + 1) * height, n * slab : (n + 1) * slab
                ]
    half = jnp.dot(inner_ref[...], turned_ref[...], preferred_element_type=F32)
    for n, targets in enumerate(outs):
        for chunk, (ref, index) in enumerate(targets):
            start = n * height + chunk * rows
            ref[index] = half[start : start + rows].astype(ref.dtype)


def first_kernel(*refs):
    ready, (kept_ref, far_ref, got_ref, beside_ref), outs = refs[:2], refs[2:6], refs[6:]
    own_ref, lent_ref, send_ref, inner_ref = outs
    sources = [
        (far_ref[0], got_ref[0]),
        (beside_ref[CHIPS], beside_ref[CHIPS]),
        (beside_ref[0], kept_ref[1]),
        (beside_ref[ORDER[1]], got_ref[1]),
    ]
    targets = [[(own_ref, 0), (send_ref, 0)]] + [[(lent_ref, n), (send_ref, 1 + n)] for n in range(3)]
    products(ready, inner_ref, sources, targets)


def second_kernel(*refs):
    ready, kept_refs, got_refs, (beside_ref, lent_in, send_in) = refs[:2], refs[2:4], refs[4:6], refs[6:9]
    own_ref, lent_ref, more_ref, same_ref, cross_ref, inner_ref = refs[9:]
    sources = [(kept[0], got[0]) for kept, got in zip(kept_refs, got_refs)]
    sources += [(beside_ref[step], got[1]) for step, got in zip(ORDER[2:], got_refs)]
    targets = [[(own_ref, n), (same_ref, 1 + n)] for n in range(2)]
    targets += [[(more_ref, n), (cross_ref, 3 + n)] for n in range(2)]
    lent_ref[...] = lent_in[...]
    same_ref[:1] = send_in[:1]
    cross_ref[:3] = send_in[1:]
    products(ready, inner_ref, sources, targets)


def whole_kernel(*refs):
    ready, (kept_ref, partner_ref), part_refs, inner_ref = refs[:2], refs[2:4], refs[4:-1], refs[-1]

    def two(g, carry):
        pairs = [2 * g, 2 * g + 1]
        sources = [(kept_ref[k], partner_ref[k]) for k in pairs]
        products(ready, inner_ref, sources, [[(ref, k) for ref in part_refs] for k in pairs])
        return carry

    lax.fori_loop(0, kept_ref.shape[0] // 2, two, 0)


def finish_kernel(first_ref, second_ref, cross_ref, same_ref, lent_ref, more_ref, gate_ref, out_ref):
    def put(kind, step, total):
        first, second = slot(kind, step)
        out_ref[first, second] = (total * gate_ref[kind * CHIPS + step, :1]).astype(BF16)

    for n, (kind, step) in enumerate([(0, 0)] + [(1, step) for step in ORDER]):
        lent = lent_ref[n] if n < 3 else more_ref[n - 3]
        put(kind, step, lent.astype(F32) + cross_ref[n].astype(F32))
    for n, step in enumerate(ORDER[1:]):
        own = first_ref[0] if n == 0 else second_ref[n - 1]
        put(0, step, own + same_ref[n].astype(F32))


def vmem_specs(count):
    return [pl.BlockSpec(memory_space=pltpu.VMEM)] * count


def shaped(dtype, *shape):
    return jax.ShapeDtypeStruct(shape, dtype)


def kernel(body, outs, operands, spaces=(), scratch=(), flops=0):
    spaces = list(spaces) + [pltpu.VMEM] * (len(operands) - len(spaces))
    return pl.pallas_call(
        body,
        out_shape=outs,
        in_specs=[pl.BlockSpec(memory_space=space) for space in spaces],
        out_specs=vmem_specs(len(outs)),
        scratch_shapes=list(scratch),
        compiler_params=pltpu.CompilerParams(vmem_limit_bytes=24 * 1024 * 1024),
        cost_estimate=pl.CostEstimate(flops=flops, bytes_accessed=1 << 20, transcendentals=0),
    )(*operands)


def shards(amplitudes, vectors, tile_mask, pair_mask):
    firsts, seconds, slab, _ = amplitudes.shape
    pairs = firsts * seconds
    virt, chips, cores = lax.axis_size("virt"), lax.axis_size("occi"), lax.axis_size("occj")
    rows = slab // virt
    chunks = virt // 2
    depth = 2 * vectors.shape[0] * slab
    turned_mask = jnp.transpose(tile_mask, (0, 2, 3, 1))
    gate = shaped(F32, pairs, 8, slab)
    arranged = [shaped(BF16, depth, slab), shaped(BF16, depth // slab * chunks * rows, slab)]
    turn = functools.partial(turn_kernel, chunks)

    def parts(count):
        return [shaped(F32 if chunk == 0 else BF16, count, rows, slab) for chunk in range(chunks)]

    def inner(count):
        return pltpu.VMEM((count * chunks * rows, depth), BF16)

    def sent(part):
        return [part[0]] + [swap_virt(part[chunk], 2 * chunk) for chunk in range(1, chunks)]

    def work(count):
        return 2 * count * depth * slab * slab

    near = swap_virt(vectors, 1)
    if (firsts, seconds, chips, cores, virt) == (2, CHIPS, CHIPS, 2, 4):
        *kept, cross, gates = kernel(
            mask_split_kernel,
            [shaped(BF16, 2, slab, slab)] * CHIPS + [shaped(BF16, CHIPS + 1, slab, slab), gate],
            [
                pltpu.with_memory_space_constraint(array, pltpu.HBM)
                for array in (turned_mask, pair_mask, amplitudes)
            ],
            spaces=[pltpu.HBM] * 3,
            scratch=[
                pltpu.SMEM(turned_mask.shape, jnp.int32),
                pltpu.SMEM(pair_mask.shape, jnp.int32),
                pltpu.SemaphoreType.DMA((pairs + 2,)),
            ],
        )
        got = {step: swap_chip(kept[step], step) for step in STEPS}
        beside = swap_core(cross)
        ready = kernel(turn, arranged, (vectors, near))
        _, far, *rest = ORDER
        own_first, lent, sending = kernel(
            first_kernel,
            [shaped(F32, 1, rows, slab), shaped(BF16, 3, rows, slab), shaped(BF16, 4, rows, slab)],
            (*ready, kept[0], kept[far], got[far], beside),
            scratch=[inner(4)],
            flops=work(4),
        )
        own_second, lent, more, same, crossing = kernel(
            second_kernel,
            [shaped(F32, 2, rows, slab)] + [shaped(BF16, count, rows, slab) for count in (3, 2, 3, 5)],
            (*ready, *[kept[step] for step in rest], *[got[step] for step in rest], beside, lent, sending),
            scratch=[inner(4)],
            flops=work(4),
        )
        operands = (own_first, own_second, swap_both(crossing, 2), swap_virt(same, 2), swap_core(lent), swap_core(more), gates)
        (out,) = kernel(finish_kernel, [shaped(BF16, firsts, seconds, rows, slab)], operands)
        return out
    kept, gates = kernel(
        mask_whole_kernel,
        [shaped(BF16, pairs, slab, slab), gate],
        (turned_mask, pair_mask, amplitudes),
        spaces=[pltpu.SMEM] * 2,
    )
    partner = lax.all_to_all(kept, ("occj", "occi"), split_axis=0, concat_axis=0, tiled=True)
    ready = kernel(turn, arranged, (vectors, near))
    part = sent(
        kernel(whole_kernel, parts(pairs), (*ready, kept, partner), scratch=[inner(2)], flops=work(pairs))
    )
    summed = part[0]
    for term in part[1:]:
        summed = summed + term.astype(F32)
    return (summed * gates[:, :1]).reshape(firsts, seconds, rows, slab).astype(BF16)


def solution(mesh):
    placed = (
        P("occi", "occj", None, None),
        P("virt", None, None),
        P("occi", "occj", None, None),
        P("occi", "occj"),
    )
    return jax.shard_map(
        shards,
        mesh=mesh,
        in_specs=placed,
        out_specs=P("occi", "occj", "virt", None),
        check_vma=False,
    )
```
